32 devices in a mesh: section: 2 (over y), dp: 4 (over z), expert: 4 (over x, core).
Axes of the slice: x: 2, y: 2, z: 4, core: 2. Of those that a mesh axis runs over, the one named last changes fastest.
Arguments:
- inputs: bfloat16 [2, 2, 4, 1024, 512], P('section', None, 'dp', 'expert'), may hold values from -6 to 6
- cotangents: bfloat16 [2, 2, 4, 1024, 512], P('section', None, 'dp', 'expert'), may hold values from -6 to 6
- pair_ids: int32 [2, 2, 4, 1024], P(None, None, 'dp'), may hold values from 0 to 15, never falling along the last dimension, each value on 1 to 512 neighbouring positions
- self_routes: int32 [2, 2, 4, 1024, 2], P('section', None, 'dp'), may hold values from 0 to 3, all different within a row; in each aligned block of 1024 rows (0 to 1023, 1024 to 2047, ..., all dimensions but the last counted through in order) at most 640 rows name the same one
- cross_routes: int32 [2, 4, 1024, 2], P(None, 'dp'), may hold values from 0 to 3, all different within a row; in each aligned block of 1024 rows (0 to 1023, 1024 to 2047, ..., all dimensions but the last counted through in order) at most 640 rows name the same one
- norm_gain: float32 [2, 2, 512], P('section'), may hold values from 0.5 to 1.5
- norm_bias: float32 [2, 2, 512], P('section'), may hold values from -2 to 2
- w_kv: bfloat16 [2, 512, 128], P('section'), may hold values from -0.25 to 0.25
- w_router: bfloat16 [2, 512, 4], P('section'), may hold values from -0.1875 to 0.1875
- w_query: bfloat16 [2, 4, 512, 64], P('section', 'expert'), may hold values from -0.25 to 0.25
- w_out: bfloat16 [2, 4, 64, 512], P('section', 'expert'), may hold values from -3 to 3
- w_in: bfloat16 [2, 512, 2048], P('section', None, 'expert'), may hold values from -0.25 to 0.25
- w_back: bfloat16 [2, 2048, 512], P('section', 'expert'), may hold values from -0.125 to 0.125
- cross_gain: float32 [512], replicated, may hold values from 0.5 to 1.5
- cross_bias: float32 [512], replicated, may hold values from -2 to 2
- cross_kv: bfloat16 [512, 128], replicated, may hold values from -0.25 to 0.25
- cross_router: bfloat16 [512, 4], replicated, may hold values from -0.1875 to 0.1875
- cross_query: bfloat16 [4, 512, 64], P('expert'), may hold values from -0.25 to 0.25
- cross_out: bfloat16 [4, 64, 512], P('expert'), may hold values from -3 to 3
Outputs:
- layer_outputs: bfloat16 [2, 2, 4, 1024, 512], P('section', None, 'dp', 'expert')
- input_grads: float32 [2, 2, 4, 1024, 512], P('section', None, 'dp', 'expert')
- grad_norm_gain: float32 [2, 2, 512], P('section', None, ('dp', 'expert'))
- grad_norm_bias: float32 [2, 2, 512], P('section', None, ('dp', 'expert'))
- grad_w_kv: float32 [2, 512, 128], P('section', ('dp', 'expert'))
- grad_w_router: float32 [2, 512, 4], P('section', ('dp', 'expert'))
- grad_w_query: float32 [2, 4, 512, 64], P('section', 'expert', 'dp')
- grad_w_out: float32 [2, 4, 64, 512], P('section', 'expert', None, 'dp')
- grad_w_in: float32 [2, 512, 2048], P('section', 'dp', 'expert')
- grad_w_back: float32 [2, 2048, 512], P('section', 'expert', 'dp')
- grad_cross_gain: float32 [512], P(('dp', 'expert'))
- grad_cross_bias: float32 [512], P(('dp', 'expert'))
- grad_cross_kv: float32 [512, 128], P(('dp', 'expert'))
- grad_cross_router: float32 [512, 4], P(('dp', 'expert'))
- grad_cross_query: float32 [4, 512, 64], P('expert', 'dp')
- grad_cross_out: float32 [4, 64, 512], P('expert', None, 'dp')
The draws below stay inside these ranges and needn't reach their ends.
Inputs may be any that keep to these rules, and one draw needn't show every extreme that they name: `pair_ids`: in each packed row the ids run from 0 to 15 in order, each as one run of positions, every id present; source and target rows with the same indices hold the same pairs. `self_routes`: each token names 2 different experts; in each packed row no expert is named by more than 640 tokens. `cross_routes`: each token names 2 different experts; in each packed row no expert is named by more than 640 tokens.
All inputs are finite; a program needn't handle non-finite values.
Results may differ from the reference program's by a relative error of at most 0.025.
Values may be sent and summed in bfloat16 or wider, within the bound.
A program may use at most 192 MiB of HBM per device.

```python
import math
import jax
import jax.numpy as jnp
import numpy as np
from jax import lax

D = 512
HEAD = 64
FF = 2048
EXPERTS = 4
TOPK = 2
SEQ = 1024
PAIRS = 16
MB = 2
ROWS = 4
CAP = 640


def block_scale(own_key, dims, cuts, least, largest):
    loudness = 1.0
    for axis_at, parts in cuts:
        draws = jax.random.uniform(jax.random.fold_in(jax.random.fold_in(own_key, 6), axis_at), (parts,), jnp.float32, least / len(cuts), largest / len(cuts))
        loudness = loudness * jnp.repeat(jnp.exp(draws), dims[axis_at] // parts).reshape((-1,) + (1,) * (len(dims) - 1 - axis_at))
    return loudness


def split_up(amount, total, most, skew):
    loads = [(1 << 20) // math.isqrt(rank ** skew) + 1 for rank in range(2, amount + 1)]
    surplus, holding = total - most - (amount - 1), [1] * (amount - 1)
    while surplus > 0:
        movable = [i for i in range(amount - 1) if holding[i] < most]
        whole, remaining = sum([loads[i] for i in movable]), surplus
        for i in movable:
            extra = min(most - holding[i], max(1, remaining * loads[i] // whole), surplus)
            holding[i] = holding[i] + extra
            surplus = surplus - extra
    return np.array([most] + holding)


def ragged(stream_key, amount, total, most, slope):
    if amount == 2:
        one = jax.random.randint(stream_key, (), max(1, total - most), min(most, total - 1) + 1)
        return jnp.stack([one, total - one])
    tallies = jnp.asarray(split_up(amount, total, most, slope), jnp.int32)
    pairs = (amount - 1) // 2
    donor, sink = tallies[1:1 + 2 * pairs:2], tallies[2:2 + 2 * pairs:2]
    margin = jnp.minimum(donor - 1, most - sink)
    moved = jax.random.randint(jax.random.fold_in(stream_key, 1), (pairs,), 0, 1 << 20) % (margin + 1)
    tallies = tallies.at[1:1 + 2 * pairs:2].set(donor - moved).at[2:2 + 2 * pairs:2].set(sink + moved)
    return tallies[jax.random.permutation(jax.random.fold_in(stream_key, 2), amount)]


def deal_out(stream_key, own, number, rows, amount, top, most, lean):
    ranking = jax.random.permutation(stream_key, amount)
    heavy_load, common = shares(amount, rows * top, most, lean, True), shares(amount, rows * top, most, lean, False)
    places = jnp.arange(amount)

    def named(tallies, offset_by):
        used = int((tallies > 0).sum())
        fixed = max(1, used // 4)
        passed = fixed + (places - fixed + offset_by * (used - fixed)) % max(1, amount - fixed)
        return jnp.zeros((amount,), jnp.int32).at[ranking[jnp.where(places < fixed, places, passed)]].set(jnp.asarray(tallies, jnp.int32))

    tallies = jnp.where(number % 4 == 0, named(heavy_load, number // 4), named(common, number - number // 4 - 1))
    mixed = jax.random.permutation(jax.random.fold_in(own, 3), amount)
    source_of, sink = mixed[0:amount // 2 * 2:2], mixed[1:amount // 2 * 2:2]
    slack = jnp.minimum(tallies[source_of] - 1, most - tallies[sink]) // 2
    slack = jnp.where((source_of == ranking[0]) | (sink == ranking[0]) | (tallies[sink] == 0), 0, jnp.maximum(slack, 0))
    passed = jax.random.randint(jax.random.fold_in(own, 4), (amount // 2,), 0, 1 << 20) % (slack + 1)
    tallies = tallies.at[source_of].add(-passed).at[sink].add(passed)
    items = jnp.searchsorted(jnp.cumsum(tallies), jnp.arange(rows * top), side="right").astype(jnp.int32)
    table = items.reshape(top, rows).T
    table = table[jax.random.permutation(jax.random.fold_in(own, 1), rows)]
    offset_by = jax.random.randint(jax.random.fold_in(own, 2), (rows, 1), 0, top)
    return jnp.take_along_axis(table, (jnp.arange(top)[None, :] + offset_by) % top, axis=1)


def shares(count, total, limit, slope, full):
    loads = [(1 << 20) // math.isqrt(grade ** slope) + 1 for grade in range(1, count + 1)]
    largest = limit if full else min(limit, max(-(-total // count), total * loads[0] // sum(loads)))
    least = 1 if total - largest >= count - 1 else 0
    given, spare = [largest] + [least] * (count - 1), total - largest - least * (count - 1)
    while spare > 0:
        candidates = [i for i in range(1, count) if given[i] < largest] or [i for i in range(1, count) if given[i] < limit]
        pool, left = sum([loads[i] for i in candidates]), spare
        for i in candidates:
            extra = min(limit - given[i], max(1, left * loads[i] // pool), spare)
            given[i] = given[i] + extra
            spare = spare - extra
    return np.array(given)


def scatter_about(stream_key, dims, width, limit, pieces=(), kind=jnp.bfloat16):
    drawn = jax.random.normal(stream_key, dims, jnp.float32) * width
    if len(pieces) > 0:
        drawn = block_scale(stream_key, dims, pieces, -0.22, 0.18) * drawn
    return jnp.clip(drawn, min=-limit, max=limit).astype(kind)


def setup_inputs(seed: int = 0) -> dict:
    splits = jax.random.split(jax.random.key(seed), 20)
    inputs = scatter_about(splits[0], (2, MB, ROWS, SEQ, D), 1.0, 6.0, ((0, 2), (2, 4), (3, 4)))
    cotangents = scatter_about(splits[1], (2, MB, ROWS, SEQ, D), 1.0, 6.0, ((0, 2), (2, 4), (3, 4)))
    pair_ids = jax.vmap(lambda own: jnp.searchsorted(jnp.cumsum(ragged(own, PAIRS, SEQ, SEQ // 2, 1)), jnp.arange(SEQ), side="right"))(jax.random.split(splits[2], 2 * MB * ROWS)).reshape((2, MB, ROWS, SEQ)).astype(jnp.int32)
    self_routes_keys = jax.random.split(jax.random.fold_in(splits[3], 1), 2 * MB * ROWS * SEQ // SEQ)
    self_routes_turns = jax.random.permutation(jax.random.fold_in(splits[3], 3), 2 * MB * ROWS * SEQ // SEQ)
    self_routes = jax.vmap(lambda own, number: deal_out(jax.random.fold_in(splits[3], 2), own, number, SEQ, EXPERTS, TOPK, CAP, 1))(self_routes_keys, self_routes_turns).reshape((2, MB, ROWS, SEQ, TOPK))
    cross_routes_keys = jax.random.split(jax.random.fold_in(splits[4], 1), MB * ROWS * SEQ // SEQ)
    cross_routes_turns = jax.random.permutation(jax.random.fold_in(splits[4], 3), MB * ROWS * SEQ // SEQ)
    cross_routes = jax.vmap(lambda own, number: deal_out(jax.random.fold_in(splits[4], 2), own, number, SEQ, EXPERTS, TOPK, CAP, 1))(cross_routes_keys, cross_routes_turns).reshape((MB, ROWS, SEQ, TOPK))
    norm_gain = jnp.clip(1.0 + 0.1 * jax.random.normal(splits[5], (2, 2, D), jnp.float32), 0.5, 1.5)
    norm_bias = scatter_about(splits[6], (2, 2, D), 0.3, 2.0, ((0, 2),), jnp.float32)
    w_kv = scatter_about(splits[7], (2, D, 2 * HEAD), D ** -0.5, 0.25, ((0, 2),))
    w_router = scatter_about(splits[8], (2, D, EXPERTS), (2 * D) ** -0.5, 0.1875, ((0, 2),))
    w_query = scatter_about(splits[9], (2, EXPERTS, D, HEAD), D ** -0.5, 0.25, ((0, 2), (1, 4)))
    w_out = scatter_about(splits[10], (2, EXPERTS, HEAD, D), (HEAD // 16) ** -0.5, 3.0, ((0, 2), (1, 4)))
    w_in = scatter_about(splits[11], (2, D, FF), D ** -0.5, 0.25, ((0, 2), (2, 4)))
    w_back = scatter_about(splits[12], (2, FF, D), FF ** -0.5, 0.125, ((0, 2), (1, 4)))
    cross_gain = jnp.clip(1.0 + 0.1 * jax.random.normal(splits[13], (D,), jnp.float32), 0.5, 1.5)
    cross_bias = scatter_about(splits[14], (D,), 0.3, 2.0, (), jnp.float32)
    cross_kv = scatter_about(splits[15], (D, 2 * HEAD), D ** -0.5, 0.25)
    cross_router = scatter_about(splits[16], (D, EXPERTS), (2 * D) ** -0.5, 0.1875)
    cross_query = scatter_about(splits[17], (EXPERTS, D, HEAD), D ** -0.5, 0.25, ((0, 4),))
    cross_out = scatter_about(splits[18], (EXPERTS, HEAD, D), (HEAD // 16) ** -0.5, 3.0, ((0, 4),))
    return dict(inputs=inputs, cotangents=cotangents, pair_ids=pair_ids, self_routes=self_routes, cross_routes=cross_routes, norm_gain=norm_gain, norm_bias=norm_bias, w_kv=w_kv, w_router=w_router, w_query=w_query, w_out=w_out, w_in=w_in, w_back=w_back, cross_gain=cross_gain, cross_bias=cross_bias, cross_kv=cross_kv, cross_router=cross_router, cross_query=cross_query, cross_out=cross_out)


@jax.custom_vjp
def low(v):
    return lax.optimization_barrier(v.astype(jnp.bfloat16)).astype(jnp.float32)

@jax.custom_vjp
def low_back(v):
    return v

def low_keep(v):
    return (low(v), None)

def low_pass(kept, grad):
    return (grad,)

def back_keep(v):
    return (v, None)

def back_low(kept, grad):
    return (low(grad),)
low.defvjp(low_keep, low_pass)
low_back.defvjp(back_keep, back_low)

def norm_rows(stream, gain_vec, shift_vec):
    middle = lax.optimization_barrier(jnp.mean(stream, -1, keepdims=True))
    centred = stream - middle
    spread = lax.optimization_barrier(jnp.mean(centred * centred, -1, keepdims=True))
    return centred * lax.rsqrt(spread + 1e-05) * gain_vec + shift_vec

def slot_table(routes):
    expert_ids = jnp.arange(EXPERTS, dtype=jnp.int32)
    member = jnp.any(routes[:, :, None] == expert_ids[None, None, :], axis=1)
    rank_pos = (jnp.cumsum(member.astype(jnp.int32), axis=0) - 1).astype(jnp.int32)
    target = jnp.where(member, rank_pos, CAP).astype(jnp.int32).T
    positions = jnp.broadcast_to(jnp.arange(SEQ, dtype=jnp.int32)[None, :], (EXPERTS, SEQ))
    slot_tok = jnp.zeros((EXPERTS, CAP), jnp.int32).at[expert_ids[:, None], target].set(positions, mode='drop')
    counts = lax.optimization_barrier(jnp.sum(member.astype(jnp.int32), axis=0))
    in_use = (jnp.arange(CAP, dtype=jnp.int32)[None, :] < counts[:, None]).astype(jnp.float32)
    return (slot_tok, in_use)

def mixture(normed, source, routes, query_pairs, key_pairs, causal, w_kv, w_router, w_query, w_out):
    highest = lax.Precision.HIGHEST
    kv_rows = low_back(low(jnp.dot(source, w_kv, precision=highest)))
    key_rows = kv_rows[:, :HEAD]
    value_rows = kv_rows[:, HEAD:]
    logits = low_back(jnp.dot(normed, w_router, precision=highest))
    picked = (routes[:, :, None] == jnp.arange(EXPERTS, dtype=jnp.int32)[None, None, :]).astype(jnp.float32)
    chosen = lax.optimization_barrier(jnp.sum(picked * logits[:, None, :], -1))
    gate_vals = jax.nn.softmax(chosen, -1)
    gate_grid = lax.optimization_barrier(jnp.sum(picked * gate_vals[:, :, None], 1))
    slot_tok, in_use = slot_table(routes)
    gathered = normed[slot_tok]
    queries = low_back(low(jnp.einsum('ecd,edh->ech', gathered, w_query, precision=highest)))
    raw_scores = jnp.einsum('ech,lh->ecl', queries, key_rows, precision=highest) * HEAD ** (-0.5)
    same_pair = query_pairs[slot_tok][:, :, None] == key_pairs[None, None, :]
    key_pos = jnp.arange(SEQ, dtype=jnp.int32)[None, None, :]
    allowed = same_pair & (jnp.logical_not(causal) | (key_pos <= slot_tok[:, :, None]))
    scores = low_back(jnp.where(allowed, raw_scores, -1e+30))
    attn_probs = jax.nn.softmax(scores, -1)
    head_out = low_back(low(jnp.einsum('ecl,lh->ech', low(attn_probs), value_rows, precision=highest)))
    result = low_back(jnp.einsum('ech,ehd->ecd', head_out, w_out, precision=highest))
    weight = gate_grid[slot_tok, jnp.arange(EXPERTS, dtype=jnp.int32)[:, None]] * in_use
    return jnp.zeros((SEQ, D), jnp.float32).at[slot_tok].add(result * weight[:, :, None])

def feed_forward(normed, w_in, w_back):
    highest = lax.Precision.HIGHEST
    hidden = low_back(jnp.dot(normed, w_in, precision=highest))
    active = low(jax.nn.gelu(hidden, approximate=True))
    return low_back(jnp.dot(active, w_back, precision=highest))

def reference(inputs, cotangents, pair_ids, self_routes, cross_routes, norm_gain, norm_bias, w_kv, w_router, w_query, w_out, w_in, w_back, cross_gain, cross_bias, cross_kv, cross_router, cross_query, cross_out):
    row_total = MB * ROWS
    floats = tuple((item.astype(jnp.float32) for item in (inputs, norm_gain, norm_bias, w_kv, w_router, w_query, w_out, w_in, w_back, cross_gain, cross_bias, cross_kv, cross_router, cross_query, cross_out)))
    enc_routes = self_routes[0].reshape(row_total, SEQ, TOPK)
    dec_routes = self_routes[1].reshape(row_total, SEQ, TOPK)
    crs_routes = cross_routes.reshape(row_total, SEQ, TOPK)
    src_pairs = pair_ids[0].reshape(row_total, SEQ)
    tgt_pairs = pair_ids[1].reshape(row_total, SEQ)

    def forward(activations, gain_all, shift_all, kv_all, router_all, query_all, out_all, in_all, back_all, cgain, cshift, ckv, crouter, cquery, cout):

        def encode(row_item):
            stream, routes, pairs = row_item
            normed = low(norm_rows(stream, gain_all[0, 0], shift_all[0, 0]))
            stream = stream + mixture(normed, normed, routes, pairs, pairs, False, kv_all[0], router_all[0], query_all[0], out_all[0])
            normed = low(norm_rows(stream, gain_all[0, 1], shift_all[0, 1]))
            return stream + feed_forward(normed, in_all[0], back_all[0])
        encoded = lax.map(jax.checkpoint(encode), (activations[0].reshape(row_total, SEQ, D), enc_routes, src_pairs))
        memory = low_back(low(encoded))

        def decode(row_item):
            stream, memory_row, routes, routes_cross, pairs, source_pairs = row_item
            normed = low(norm_rows(stream, gain_all[1, 0], shift_all[1, 0]))
            stream = stream + mixture(normed, normed, routes, pairs, pairs, True, kv_all[1], router_all[1], query_all[1], out_all[1])
            normed = low(norm_rows(stream, cgain, cshift))
            stream = stream + mixture(normed, memory_row, routes_cross, pairs, source_pairs, False, ckv, crouter, cquery, cout)
            normed = low(norm_rows(stream, gain_all[1, 1], shift_all[1, 1]))
            return stream + feed_forward(normed, in_all[1], back_all[1])
        decoded = lax.map(jax.checkpoint(decode), (activations[1].reshape(row_total, SEQ, D), memory, dec_routes, crs_routes, tgt_pairs, src_pairs))
        return jnp.stack([encoded, decoded]).reshape(2, MB, ROWS, SEQ, D)
    result, pullback = jax.vjp(forward, *floats)
    grads = pullback(cotangents.astype(jnp.float32))
    return (result.astype(jnp.bfloat16), grads[0], grads[1], grads[2], grads[3], grads[4], grads[5], grads[6], grads[7], grads[8], grads[9], grads[10], grads[11], grads[12], grads[13], grads[14])
```

```python
from types import SimpleNamespace

import jax
import jax.numpy as jnp
from jax import lax
from jax.experimental import pallas as pl
from jax.experimental.pallas import tpu as pltpu
from jax.sharding import PartitionSpec as P

F32 = jnp.float32
BF16 = jnp.bfloat16
MESH = pl.DeviceIdType.MESH
RT = 16


def nn(a, b):
    return lax.dot_general(a, b, (((1,), (0,)), ((), ())), preferred_element_type=F32)


def nt(a, b):
    return lax.dot_general(a, b, (((1,), (1,)), ((), ())), preferred_element_type=F32)


def tn(a, b):
    return lax.dot_general(a, b, (((0,), (0,)), ((), ())), preferred_element_type=F32)


def gelu_parts(h):
    c = 0.7978845608028654
    h2 = h * h
    t = jnp.tanh(c * h * (1.0 + 0.044715 * h2))
    half = 0.5 * (1.0 + t)
    slope = half + 0.5 * h * (1.0 - t * t) * (c * (1.0 + 3 * 0.044715 * h2))
    return h * half, slope


def norm_stats(x):
    centred = x - jnp.mean(x, -1, keepdims=True)
    r = lax.rsqrt(jnp.mean(centred * centred, -1, keepdims=True) + 1e-05)
    return centred * r, r


def norm_back(x, gain, grad):
    xhat, r = norm_stats(x)
    gg = grad * gain
    m1 = jnp.mean(gg, -1, keepdims=True)
    m2 = jnp.mean(gg * xhat, -1, keepdims=True)
    return (
        r * (gg - m1 - xhat * m2),
        jnp.sum(grad * xhat, 0, keepdims=True),
        jnp.sum(grad, 0, keepdims=True),
    )


def make_plan(dims):
    (NI, L, D, SEQ, T, NE, HD, HB, E, DP) = dims
    npd = NE // E
    QB = npd * HD
    NQ = NE * HD
    X = E // 2
    DB = D // DP
    ins = [
        "x", "cot", "pairs", "routes_s", "routes_c", "ng", "nb", "wkv", "wr", "wq", "wo", "win",
        "wback", "cg", "cb", "ckv", "cr", "cq", "co",
    ]
    outs = [
        ("o_layer", (NI, L, D), BF16),
        ("o_ig", (NI, L, D), F32),
        ("o_in", (DB, HB), F32),
        ("o_back", (DB, HB), F32),
        ("o_qos", (DB, 2 * QB), F32),
        ("o_qoc", (DB, 2 * QB), F32),
        ("o_kv", (2, DB, 2 * HD), F32),
        ("o_small", (24, D), F32),
    ]
    bufs = [
        ("win_all", (E, D, HB), BF16),
        ("wback_all", (E, HB, D), BF16),
        ("wqr", (2, NQ + RT, D), BF16),
        ("wo_all", (2, NQ, D), BF16),
        ("x1", (NI, L, D), F32),
        ("x2", (NI, L, D), F32),
        ("n", (NI, 3, L, D), BF16),
        ("dz", (NI, L, D), BF16),
        ("acc", (L, D), F32),
        ("h", (NI, E, L, HB), F32),
        ("dh", (max(NI * E * L, E * D), HB), BF16),
        ("kv_s", (NI, SEQ, 2 * HD), BF16),
        ("kv_c", (NI, SEQ, 2 * HD), BF16),
        ("kvt", (2, NI, 2 * HD, SEQ), BF16),
        ("bias", (SEQ, L), F32),
        ("qt", (2, NI, T, HD, L), BF16),
        ("gate", (2, NI, T, 8, L), F32),
        ("p", (2, NI, T, SEQ, L), BF16),
        ("heads", (2, NI, T, HD, L), F32),
        ("ht", (2, NI, NQ, L), BF16),
        ("dq", (T, HD, L), BF16),
        ("dkv_acc", (SEQ, 2 * HD), F32),
        ("dkv_send", (NI, SEQ, 2 * HD), BF16),
        ("dkv_recv", (NI, E, L, 2 * HD), BF16),
        ("dckv_send", (NI, SEQ, 2 * HD), BF16),
        ("dckv_recv", (NI, E, L, 2 * HD), BF16),
        ("ckv_own", (NI, L, 2 * HD), BF16),
        ("g_big", (E, 2, D, HB), F32),
        ("g_qr", (2, NQ + RT, D), F32),
        ("g_o", (2, NQ, D), F32),
        ("g_kv", (2, D, 2 * HD), F32),
        ("small", (24, D), F32),
        ("a_big_r", (2, X * D, HB), BF16),
        ("a_qo", (X, 4 * QB, D), BF16),
        ("a_qo_r", (X, 4 * QB, D), BF16),
        ("b_big", (X - 1, 2, D, HB), BF16),
        ("b_big_r", (X - 1, 2, D, HB), BF16),
        ("b_qo", (X - 1, 4 * QB, D), BF16),
        ("b_qo_r", (X - 1, 4 * QB, D), BF16),
        ("c_big", (DP, 2, DB, HB), BF16),
        ("c_big_r", (DP, 2, DB, HB), BF16),
        ("c_qo", (DP, DB, 4 * QB), F32),
        ("c_qo_r", (DP, DB, 4 * QB), F32),
        ("own_qo", (D, 4 * QB), F32),
        ("kv_r", (DP, 2, DB, 2 * HD), F32),
        ("kv_sum", (2, DB, 2 * HD), F32),
        ("kv_x", (E, 2, DB, 2 * HD), F32),
        ("sm_x", (E, 24, D), F32),
        ("sm_sum", (24, D), F32),
        ("sm_d", (DP, 24, D), F32),
        ("sec_qo", (DB, 2 * QB), F32),
        ("sec_qo_r", (DB, 2 * QB), F32),
        ("sec_kv_r", (DB, 2 * HD), F32),
        ("sec_sm_r", (24, D), F32),
    ]
    sems = [
        ("q_s", (4, E)), ("q_r", (4, E)),
        ("sib_s", (2,)), ("sib_r", (2,)),
        ("wx_s", (2, X)), ("wx_r", (2, X)),
        ("wf_s", (2, X)), ("wf_r", (2, X)),
        ("kv_ss", (NI, E)), ("kv_rs", (NI, E)),
        ("ckv_s", (NI, E)), ("ckv_r", (NI, E)),
        ("dckv_s", (NI, E)), ("dckv_r", (NI, E)),
        ("dkv_s", (NI, E)), ("dkv_r", (NI, E)),
        ("a_s", (3,)), ("a_r", (3,)),
        ("b_s", (3, X - 1)), ("b_r", (3, X - 1)),
        ("c_s", (2, DP)), ("c_r", (2, DP)),
        ("kd_s", (DP,)), ("kd_r", (DP,)),
        ("ke_s", (E,)), ("ke_r", (E,)),
        ("se_s", (E,)), ("se_r", (E,)),
        ("sd_s", (DP,)), ("sd_r", (DP,)),
        ("sec_s", (3,)), ("sec_r", (3,)),
    ]
    return ins, outs, bufs, sems


def make_kernel(dims):
    (NI, L, D, SEQ, T, NE, HD, HB, E, DP) = dims
    npd = NE // E
    QB = npd * HD
    NQ = NE * HD
    X = E // 2
    DB = D // DP
    scale = HD ** -0.5
    ins, outs, bufs, sems = make_plan(dims)
    names = ins + [o[0] for o in outs] + [b[0] for b in bufs] + [s[0] for s in sems]

    def kernel(*refs):
        r = SimpleNamespace(**dict(zip(names, refs)))
        sec = lax.axis_index("section")
        dpi = lax.axis_index("dp")
        me = lax.axis_index("expert")
        core = lax.rem(me, 2)
        xi = me // 2
        sib = xi * 2 + (1 - core)
        dec = sec == 1
        enc = sec == 0
        other = 1 - sec
        row0 = pl.multiple_of(me * L, L)

        def to_expert(j):
            return (sec, dpi, j)

        def to_dp(j):
            return (sec, j, me)

        def to_section(j):
            return (other, dpi, j)

        def rcopy(src, dst, ssem, rsem, dev):
            return pltpu.make_async_remote_copy(
                src_ref=src, dst_ref=dst, send_sem=ssem, recv_sem=rsem, device_id=dev,
                device_id_type=MESH,
            )

        def qblock(a, j):
            return r.wqr.at[a, pl.ds(pl.multiple_of(j * QB, QB), QB)]

        def oblock(a, j):
            return r.wo_all.at[a, pl.ds(pl.multiple_of(j * QB, QB), QB)]

        def q_copy(kind, block, to, frm):
            ref = qblock(kind // 2, block) if kind % 2 == 0 else oblock(kind // 2, block)
            return rcopy(ref, ref, r.q_s.at[kind, to], r.q_r.at[kind, frm], to_expert(to))

        def w_ref(kind, c):
            return (r.win_all if kind == 0 else r.wback_all).at[c]

        def sib_copy(kind, c):
            ref = w_ref(kind, c)
            return rcopy(ref, ref, r.sib_s.at[kind], r.sib_r.at[kind], to_expert(sib))

        def wx_copy(kind, c, to_x, frm_x):
            ref = w_ref(kind, c)
            return rcopy(
                ref, ref, r.wx_s.at[kind, to_x], r.wx_r.at[kind, frm_x], to_expert(to_x * 2 + core)
            )

        def wf_copy(kind, c, x):
            ref = w_ref(kind, c)
            return rcopy(ref, ref, r.wf_s.at[kind, x], r.wf_r.at[kind, x], to_expert(sib))

        def rows_of(ref, i, j):
            return ref.at[i, pl.ds(pl.multiple_of(j * L, L), L)]

        def kv_copy(i, block, to, frm):
            ref = rows_of(r.kv_s, i, block)
            return rcopy(ref, ref, r.kv_ss.at[i, to], r.kv_rs.at[i, frm], to_expert(to))

        def ckv_copy(i, block, to, frm):
            return rcopy(
                r.ckv_own.at[i], rows_of(r.kv_c, i, block), r.ckv_s.at[i, to], r.ckv_r.at[i, frm],
                to_section(to),
            )

        def dckv_copy(i, to, frm):
            return rcopy(
                rows_of(r.dckv_send, i, to), r.dckv_recv.at[i, frm], r.dckv_s.at[i, to],
                r.dckv_r.at[i, frm], to_section(to),
            )

        def dkv_copy(i, to, frm):
            return rcopy(
                rows_of(r.dkv_send, i, to), r.dkv_recv.at[i, frm], r.dkv_s.at[i, to],
                r.dkv_r.at[i, frm], to_expert(to),
            )

        def a_copy(kind):
            if kind < 2:
                src, dst = r.dh.at[pl.ds(kind * X * D, X * D)], r.a_big_r.at[kind]
            else:
                src, dst = r.a_qo, r.a_qo_r
            return rcopy(src, dst, r.a_s.at[kind], r.a_r.at[kind], to_expert(sib))

        def b_copy(kind, o):
            if kind < 2:
                src, dst = r.b_big.at[o, kind], r.b_big_r.at[o, kind]
            else:
                src, dst = r.b_qo.at[o], r.b_qo_r.at[o]
            to = lax.rem(xi + o + 1, X) * 2 + core
            return rcopy(src, dst, r.b_s.at[kind, o], r.b_r.at[kind, o], to_expert(to))

        def c_copy(kind, to, frm):
            src, dst = (r.c_big, r.c_big_r) if kind == 0 else (r.c_qo, r.c_qo_r)
            return rcopy(src.at[to], dst.at[frm], r.c_s.at[kind, to], r.c_r.at[kind, frm], to_dp(to))

        def kd_copy(to, frm):
            return rcopy(
                r.g_kv.at[:, pl.ds(pl.multiple_of(to * DB, DB), DB)], r.kv_r.at[frm], r.kd_s.at[to],
                r.kd_r.at[frm], to_dp(to),
            )

        def ke_copy(to, frm):
            return rcopy(r.kv_sum, r.kv_x.at[frm], r.ke_s.at[to], r.ke_r.at[frm], to_expert(to))

        def se_copy(to, frm):
            return rcopy(r.small, r.sm_x.at[frm], r.se_s.at[to], r.se_r.at[frm], to_expert(to))

        def sd_copy(to, frm):
            return rcopy(r.sm_sum, r.sm_d.at[frm], r.sd_s.at[to], r.sd_r.at[frm], to_dp(to))

        def sec_copy(kind):
            src, dst = (
                (r.sec_qo, r.sec_qo_r), (r.o_kv.at[1], r.sec_kv_r), (r.o_small, r.sec_sm_r)
            )[kind]
            return rcopy(src, dst, r.sec_s.at[kind], r.sec_r.at[kind], to_section(me))

        def peers():
            return [lax.rem(me + o, E) for o in range(1, E)]

        def xpeers():
            return [lax.rem(xi + o, X) for o in range(1, X)]

        def dpeers():
            return [lax.rem(dpi + o, DP) for o in range(1, DP)]

        barrier = pltpu.get_barrier_semaphore()
        for j in peers():
            pl.semaphore_signal(barrier, inc=1, device_id=to_expert(j), device_id_type=MESH)
        for j in dpeers():
            pl.semaphore_signal(barrier, inc=1, device_id=to_dp(j), device_id_type=MESH)
        for j in range(E):
            pl.semaphore_signal(barrier, inc=1, device_id=to_section(j), device_id_type=MESH)

        for a, (q_ref, o_ref, wr_ref) in enumerate(
            ((r.wq, r.wo, r.wr), (r.cq, r.co, r.cr))
        ):
            for j in range(npd):
                at = pl.multiple_of(me * QB + j * HD, HD)
                r.wqr[a, pl.ds(at, HD)] = q_ref[j].astype(F32).T.astype(BF16)
                r.wo_all[a, pl.ds(at, HD)] = o_ref[j]
            r.wqr[a, pl.ds(NQ, RT)] = wr_ref[...]
        r.win_all[me] = r.win[...]
        r.wback_all[me] = r.wback[...]

        pl.semaphore_wait(barrier, (E - 1) + (DP - 1) + E)

        for kind in (0, 1):
            for j in peers():
                q_copy(kind, me, j, me).start()

        def norm_rows(x, gain, shift):
            return norm_stats(x)[0] * gain + shift

        def gain_of(which):
            if which == 1:
                return r.cg[...], r.cb[...]
            return r.ng[which // 2 : which // 2 + 1], r.nb[which // 2 : which // 2 + 1]

        def first_norm(i, _):
            g, b = gain_of(0)
            n = norm_rows(r.x[i].astype(F32), g, b).astype(BF16)
            r.n[i, 0] = n
            r.kv_s[i, pl.ds(row0, L)] = nn(n, r.wkv[...]).astype(BF16)
            for j in peers():
                kv_copy(i, me, j, me).start()
            return 0

        lax.fori_loop(0, NI, first_norm, 0)

        for kind in (0, 1):
            sib_copy(kind, me).start()
            for x in xpeers():
                wx_copy(kind, me, x, xi).start()

        @pl.when(dec)
        def _():
            for kind in (2, 3):
                for j in peers():
                    q_copy(kind, me, j, me).start()

        zeros_h = jnp.zeros((HD, L), BF16)

        def set_bias(i, a):
            own = r.pairs[sec, i, :, pl.ds(row0, L)].astype(F32)
            if a == 0:
                keys = r.pairs[sec, i].astype(F32)
            else:
                keys = r.pairs[0, i].astype(F32)
            kc = jnp.broadcast_to(keys, (128, SEQ)).T
            if L > 128:
                kc = jnp.concatenate([kc] * (L // 128), 1)
            same = kc == own
            if a == 0:
                qpos = row0 + lax.broadcasted_iota(jnp.int32, (1, L), 1)
                limit = jnp.where(dec, qpos, SEQ)
                same = same & (lax.broadcasted_iota(jnp.int32, (SEQ, L), 0) <= limit)
            r.bias[...] = jnp.where(same, 0.0, -1e30)

        def route_rows(i, a):
            ref = r.routes_s if a == 0 else r.routes_c
            return [ref[i, k, :, pl.ds(row0, L)] for k in range(T)]

        def pick(rows, route, size):
            total = jnp.zeros((size, L), F32)
            for e in range(NE):
                total = jnp.where(route == e, rows[e * size : (e + 1) * size], total)
            return total

        def project_queries(i, a):
            n = r.n[i, a]
            ql = nt(r.wqr[a], n)
            routes = route_rows(i, a)
            chosen = []
            for k in range(T):
                r.qt[a, i, k] = (pick(ql[:NQ], routes[k], HD).astype(BF16).astype(F32) * scale).astype(BF16)
                chosen.append(pick(ql[NQ : NQ + NE], routes[k], 1))
            top = chosen[0]
            for k in range(1, T):
                top = jnp.maximum(top, chosen[k])
            ex = [jnp.exp(c - top) for c in chosen]
            total = ex[0]
            for k in range(1, T):
                total = total + ex[k]
            for k in range(T):
                r.gate[a, i, k] = jnp.broadcast_to(ex[k] / total, (8, L))

        def attend(i, a, kv_ref, base):
            kv = kv_ref[i]
            r.kvt[a, i] = kv.astype(F32).T.astype(BF16)

            def one(k, _):
                q = jnp.concatenate([r.qt[a, i, k], zeros_h], 0)
                s = nn(kv, q) + r.bias[...]
                m = jnp.max(s, 0, keepdims=True)
                ex = jnp.exp(s - m)
                p = (ex * (1.0 / jnp.sum(ex, 0, keepdims=True))).astype(BF16)
                r.p[a, i, k] = p
                r.heads[a, i, k] = nn(r.kvt[a, i, HD:], p)
                return 0

            lax.fori_loop(0, T, one, 0)
            routes = route_rows(i, a)
            gated = [
                r.heads[a, i, k].astype(BF16).astype(F32) * r.gate[a, i, k, 0:1] for k in range(T)
            ]
            for e in range(NE):
                block = jnp.zeros((HD, L), F32)
                for k in range(T):
                    block = jnp.where(routes[k] == e, gated[k], block)
                r.ht[a, i, e * HD : (e + 1) * HD] = block.astype(BF16)
            return base + tn(r.ht[a, i], r.wo_all[a])

        def attend_back(i, a, kv_ref, dx, send_ref):
            dxb = dx.astype(BF16)
            routes = route_rows(i, a)
            r.g_o[a] += nn(r.ht[a, i], dxb)
            gt = nt(r.wo_all[a], dxb)
            dgates = []
            for k in range(T):
                g = pick(gt, routes[k], HD)
                dgates.append(
                    jnp.sum(r.heads[a, i, k].astype(BF16).astype(F32) * g, 0, keepdims=True)
                )
                r.dq[k] = (g * r.gate[a, i, k, 0:1]).astype(BF16)
            gates = [r.gate[a, i, k, 0:1] for k in range(T)]
            mid = gates[0] * dgates[0]
            for k in range(1, T):
                mid = mid + gates[k] * dgates[k]
            dchosen = [gates[k] * (dgates[k] - mid) for k in range(T)]
            kv = kv_ref[i]
            r.dkv_acc[...] = jnp.zeros_like(r.dkv_acc)

            def one(k, _):
                dheads = r.dq[k]
                p = r.p[a, i, k]
                dv = jnp.concatenate([zeros_h, dheads], 0)
                dp = nn(kv, dv)
                pf = p.astype(F32)
                delta = jnp.sum(dp * pf, 0, keepdims=True)
                ds = (pf * (dp - delta)).astype(BF16)
                qk = jnp.concatenate([r.qt[a, i, k], zeros_h], 0)
                r.dkv_acc[...] += nt(ds, qk) + nt(p, dv)
                r.dq[k] = (nn(r.kvt[a, i, :HD], ds) * scale).astype(BF16)
                return 0

            lax.fori_loop(0, T, one, 0)
            send_ref[i] = r.dkv_acc[...].astype(BF16)
            blocks = []
            for e in range(NE):
                block = jnp.zeros((HD, L), F32)
                for k in range(T):
                    block = jnp.where(routes[k] == e, r.dq[k].astype(F32), block)
                blocks.append(block)
            logit_rows = jnp.zeros((RT, L), F32)
            rows = lax.broadcasted_iota(jnp.int32, (RT, L), 0)
            for k in range(T):
                logit_rows = jnp.where(rows == routes[k], dchosen[k], logit_rows)
            dql = jnp.concatenate(blocks + [logit_rows], 0).astype(BF16)
            r.g_qr[a] += nn(dql, r.n[i, a])
            return tn(dql, r.wqr[a])

        def chunk_at(s):
            x = lax.rem(xi + s // 2, X)
            return x * 2 + jnp.where(lax.rem(s, 2) == 0, core, 1 - core)

        def weights_in(s):
            for kind in (0, 1):
                c = chunk_at(s)

                @pl.when(s == 1)
                def _():
                    sib_copy(kind, c).wait_recv()

                for o in range(1, X):
                    x = lax.rem(xi + o, X)

                    @pl.when(s == 2 * o)
                    def _():
                        wx_copy(kind, c, x, x).wait_recv()
                        wf_copy(kind, c, x).start()

                    @pl.when(s == 2 * o + 1)
                    def _():
                        wf_copy(kind, c, x).wait_recv()

        def dh_rows(i, c):
            return pl.ds(pl.multiple_of((i * E + c) * L, L), L)

        def ffn_hidden(i, wait, finish):
            n = r.n[i, 2]
            if finish:
                r.acc[...] = jnp.zeros_like(r.acc)

            def one(s, _):
                if wait:
                    weights_in(s)
                c = chunk_at(s)
                h = nn(n, r.win_all[c])
                r.h[i, c] = h
                if finish:
                    r.acc[...] += nn(gelu_parts(h)[0].astype(BF16), r.wback_all[c])
                return 0

            lax.fori_loop(0, E, one, 0)

        def ffn_back(i):
            dz = r.dz[i]
            r.acc[...] = jnp.zeros_like(r.acc)

            def one(c, _):
                da = nt(dz, r.wback_all[c])
                dh = (da * gelu_parts(r.h[i, c])[1]).astype(BF16)
                r.dh[dh_rows(i, c)] = dh
                r.acc[...] += nt(dh, r.win_all[c])
                return 0

            lax.fori_loop(0, E, one, 0)
            return r.acc[...]

        def ffn_weights(i):
            nt_ = r.n[i, 2].astype(F32).T.astype(BF16)
            dzt = r.dz[i].astype(F32).T.astype(BF16)
            r.acc[...] = jnp.zeros_like(r.acc)

            def one(c, _):
                act = gelu_parts(r.h[i, c])[0].astype(BF16)
                r.g_big[c, 0] += nn(nt_, r.dh[dh_rows(i, c)])
                r.g_big[c, 1] += nn(dzt, act)

                @pl.when(dec)
                def _():
                    r.acc[...] += nn(act, r.wback_all[c])

                return 0

            lax.fori_loop(0, E, one, 0)

            @pl.when(dec)
            def _():
                r.o_layer[i] = (r.x2[i] + r.acc[...]).astype(BF16)

        def add_small(which, dgain, dshift):
            r.small[2 * which : 2 * which + 1] += dgain
            r.small[2 * which + 1 : 2 * which + 2] += dshift

        def zero(ref):
            ref[...] = jnp.zeros_like(ref)

        r.small[...] = jnp.zeros_like(r.small)
        r.g_qr[...] = jnp.zeros_like(r.g_qr)
        r.g_o[...] = jnp.zeros_like(r.g_o)
        r.g_kv[...] = jnp.zeros_like(r.g_kv)

        def zero_big(c, _):
            r.g_big[c] = jnp.zeros((2, D, HB), F32)
            return 0

        lax.fori_loop(0, E, zero_big, 0)

        for kind in (0, 1):
            for j in peers():
                q_copy(kind, j, j, j).wait_recv()

        def forward(i, _):
            project_queries(i, 0)
            set_bias(i, 0)
            for j in peers():
                kv_copy(i, j, j, j).wait_recv()
            x1 = attend(i, 0, r.kv_s, r.x[i].astype(F32))
            r.x1[i] = x1

            @pl.when(enc)
            def _():
                g, b = gain_of(2)
                r.n[i, 2] = norm_rows(r.x1[i], g, b).astype(BF16)

                @pl.when(i == 0)
                def _():
                    ffn_hidden(0, True, True)

                @pl.when(i > 0)
                def _():
                    ffn_hidden(i, False, True)

                mem = (r.x1[i] + r.acc[...]).astype(BF16)
                r.o_layer[i] = mem
                r.ckv_own[i] = nn(mem, r.ckv[...]).astype(BF16)
                for j in range(E):
                    ckv_copy(i, me, j, me).start()

            @pl.when(dec)
            def _():
                g, b = gain_of(1)
                r.n[i, 1] = norm_rows(r.x1[i], g, b).astype(BF16)
                r.dz[i] = r.cot[i]

            return 0

        lax.fori_loop(0, NI, forward, 0)

        @pl.when(dec)
        def _():
            for s in range(E):
                weights_in(jnp.int32(s))
            for kind in (2, 3):
                for j in peers():
                    q_copy(kind, j, j, j).wait_recv()

            def middle(i, _):
                project_queries(i, 1)
                set_bias(i, 1)
                for j in range(E):
                    ckv_copy(i, j, j, j).wait_recv()
                x2 = attend(i, 1, r.kv_c, r.x1[i])
                r.x2[i] = x2
                g, b = gain_of(2)
                r.n[i, 2] = norm_rows(x2, g, b).astype(BF16)
                ffn_hidden(i, False, False)
                dn = ffn_back(i)
                dx, dg, db = norm_back(r.x2[i], g, dn)
                add_small(2, dg, db)
                r.o_ig[i] = r.cot[i].astype(F32) + dx
                dn = attend_back(i, 1, r.kv_c, r.o_ig[i], r.dckv_send)
                for j in range(E):
                    dckv_copy(i, j, me).start()
                g, b = gain_of(1)
                dx, dg, db = norm_back(r.x1[i], g, dn)
                add_small(1, dg, db)
                r.o_ig[i] += dx
                return 0

            lax.fori_loop(0, NI, middle, 0)

        def send_big(kind):
            for x in range(X):
                r.dh[(kind * X + x) * D : (kind * X + x + 1) * D] = r.g_big[
                    x * 2 + (1 - core), kind
                ].astype(BF16)
            a_copy(kind).start()

        def backward(i, _):
            @pl.when(enc)
            def _():
                total = jnp.zeros((L, 2 * HD), F32)
                for j in range(E):
                    dckv_copy(i, j, j).wait_recv()
                    total = total + r.dckv_recv[i, j].astype(F32)
                dkv = total.astype(BF16)
                r.g_kv[1] += tn(r.o_layer[i], dkv)
                dmem = nt(dkv, r.ckv[...]).astype(BF16).astype(F32)
                dx = r.cot[i].astype(F32) + dmem
                r.o_ig[i] = dx
                r.dz[i] = dx.astype(BF16)
                dn = ffn_back(i)
                g, b = gain_of(2)
                dx, dg, db = norm_back(r.x1[i], g, dn)
                add_small(2, dg, db)
                r.o_ig[i] += dx

            ffn_weights(i)

            @pl.when(i == NI - 1)
            def _():
                send_big(0)
                send_big(1)

            dn = attend_back(i, 0, r.kv_s, r.o_ig[i], r.dkv_send)
            r.acc[...] = dn
            for j in peers():
                dkv_copy(i, j, me).start()
            total = r.dkv_send[i, pl.ds(row0, L)].astype(F32)
            for j in peers():
                dkv_copy(i, j, j).wait_recv()
                total = total + r.dkv_recv[i, j].astype(F32)
            dkv = total.astype(BF16)
            r.g_kv[0] += tn(r.n[i, 0], dkv)
            dn = r.acc[...] + nt(dkv, r.wkv[...])
            g, b = gain_of(0)
            dx, dg, db = norm_back(r.x[i].astype(F32), g, dn)
            add_small(0, dg, db)
            r.o_ig[i] += dx
            return 0

        lax.fori_loop(0, NI, backward, 0)

        for a in range(2):
            r.small[6 + a * NE : 6 + (a + 1) * NE] = r.g_qr[a, NQ : NQ + NE]
        for j in peers():
            se_copy(j, me).start()
        for j in dpeers():
            kd_copy(j, dpi).start()

        def qo_rows(c):
            at = pl.ds(pl.multiple_of(c * QB, QB), QB)
            return jnp.concatenate([r.g_qr[0, at], r.g_o[0, at], r.g_qr[1, at], r.g_o[1, at]], 0)

        for x in range(X):
            r.a_qo[x] = qo_rows(x * 2 + (1 - core)).astype(BF16)
        a_copy(2).start()

        for kind in range(2):
            a_copy(kind).wait_recv()
            for o, x in enumerate(xpeers()):
                r.b_big[o, kind] = (
                    r.g_big[x * 2 + core, kind] + r.a_big_r[kind, pl.ds(pl.multiple_of(x * D, D), D)].astype(F32)
                ).astype(BF16)
                b_copy(kind, o).start()
            r.g_big[me, kind] += r.a_big_r[kind, pl.ds(pl.multiple_of(xi * D, D), D)].astype(F32)
        a_copy(2).wait_recv()
        for o, x in enumerate(xpeers()):
            r.b_qo[o] = (qo_rows(x * 2 + core) + r.a_qo_r[x].astype(F32)).astype(BF16)
            b_copy(2, o).start()
        own_qo = qo_rows(me) + r.a_qo_r[xi].astype(F32)

        total = r.g_kv[:, pl.ds(pl.multiple_of(dpi * DB, DB), DB)]
        for j in dpeers():
            kd_copy(j, j).wait_recv()
            total = total + r.kv_r[j]
        r.kv_sum[...] = total
        for j in peers():
            ke_copy(j, me).start()
        total = r.small[...]
        for j in peers():
            se_copy(j, j).wait_recv()
            total = total + r.sm_x[j]
        r.sm_sum[...] = total
        for j in dpeers():
            sd_copy(j, dpi).start()

        for kind in range(2):
            total = r.g_big[me, kind]
            for o in range(X - 1):
                b_copy(kind, o).wait_recv()
                total = total + r.b_big_r[o, kind].astype(F32)
            r.g_big[me, kind] = total
            for d in range(DP):
                r.c_big[d, kind] = total[d * DB : (d + 1) * DB].astype(BF16)
        for j in dpeers():
            c_copy(0, j, dpi).start()
        for o in range(X - 1):
            b_copy(2, o).wait_recv()
            own_qo = own_qo + r.b_qo_r[o].astype(F32)
        r.own_qo[...] = own_qo.T
        for d in range(DP):
            r.c_qo[d] = r.own_qo[d * DB : (d + 1) * DB]
        for j in dpeers():
            c_copy(1, j, dpi).start()

        total = r.kv_sum[...]
        for j in peers():
            ke_copy(j, j).wait_recv()
            total = total + r.kv_x[j]
        r.o_kv[...] = total
        total = r.sm_sum[...]
        for j in dpeers():
            sd_copy(j, j).wait_recv()
            total = total + r.sm_d[j]
        r.o_small[...] = total
        sec_copy(1).start()
        sec_copy(2).start()

        mine = pl.ds(pl.multiple_of(dpi * DB, DB), DB)
        for j in dpeers():
            c_copy(0, j, j).wait_recv()
        for kind, out in ((0, r.o_in), (1, r.o_back)):
            total = r.g_big[me, kind, mine]
            for j in dpeers():
                total = total + r.c_big_r[j, kind].astype(F32)
            out[...] = total
        total = r.own_qo[mine]
        for j in dpeers():
            c_copy(1, j, j).wait_recv()
            total = total + r.c_qo_r[j]
        r.o_qos[...] = total[:, : 2 * QB]
        r.sec_qo[...] = total[:, 2 * QB :]
        sec_copy(0).start()
        for kind in range(3):
            sec_copy(kind).wait_send()
            sec_copy(kind).wait_recv()
        r.o_qoc[...] = r.sec_qo[...] + r.sec_qo_r[...]
        r.o_kv[1] += r.sec_kv_r[...]
        r.o_small[2:4] += r.sec_sm_r[2:4]
        r.o_small[6 + NE : 6 + 2 * NE] += r.sec_sm_r[6 + NE : 6 + 2 * NE]

        for kind in (0, 1):
            for j in peers():
                q_copy(kind, me, j, me).wait_send()
            sib_copy(kind, me).wait_send()
            for x in xpeers():
                wx_copy(kind, me, x, xi).wait_send()
                wf_copy(kind, x * 2 + core, x).wait_send()

        @pl.when(dec)
        def _():
            for kind in (2, 3):
                for j in peers():
                    q_copy(kind, me, j, me).wait_send()

        def sent(i, _):
            for j in peers():
                kv_copy(i, me, j, me).wait_send()
                dkv_copy(i, j, me).wait_send()

            @pl.when(enc)
            def _():
                for j in range(E):
                    ckv_copy(i, me, j, me).wait_send()

            @pl.when(dec)
            def _():
                for j in range(E):
                    dckv_copy(i, j, me).wait_send()

            return 0

        lax.fori_loop(0, NI, sent, 0)
        for kind in range(3):
            a_copy(kind).wait_send()
            for o in range(X - 1):
                b_copy(kind, o).wait_send()
        for j in dpeers():
            kd_copy(j, dpi).wait_send()
            sd_copy(j, dpi).wait_send()
            for kind in range(2):
                c_copy(kind, j, dpi).wait_send()
        for j in peers():
            ke_copy(j, me).wait_send()
            se_copy(j, me).wait_send()

    return kernel


def body(
    inputs, cotangents, pair_ids, self_routes, cross_routes, norm_gain, norm_bias, w_kv, w_router,
    w_query, w_out, w_in, w_back, cross_gain, cross_bias, cross_kv, cross_router, cross_query,
    cross_out,
):
    E = lax.axis_size("expert")
    DP = lax.axis_size("dp")
    _, MB, R, L, D = inputs.shape
    NI = MB * R
    SEQ = pair_ids.shape[-1]
    T = self_routes.shape[-1]
    NE = w_router.shape[-1]
    HD = w_query.shape[-1]
    HB = w_in.shape[-1]
    npd = NE // E
    QB = npd * HD
    dims = (NI, L, D, SEQ, T, NE, HD, HB, E, DP)
    ins, outs, bufs, sems = make_plan(dims)

    def router_rows(w):
        return jnp.pad(w.T, ((0, RT - NE), (0, 0)))

    operands = [
        inputs.reshape(NI, L, D),
        cotangents.reshape(NI, L, D),
        pair_ids.reshape(2, NI, 1, SEQ),
        jnp.swapaxes(self_routes.reshape(NI, SEQ, T), 1, 2)[:, :, None],
        jnp.swapaxes(cross_routes.reshape(NI, SEQ, T), 1, 2)[:, :, None],
        norm_gain[0],
        norm_bias[0],
        w_kv[0],
        router_rows(w_router[0]),
        w_query[0],
        w_out[0],
        w_in[0],
        w_back[0],
        cross_gain[None],
        cross_bias[None],
        cross_kv,
        router_rows(cross_router),
        cross_query,
        cross_out,
    ]
    vmem = pl.BlockSpec(memory_space=pltpu.VMEM)
    res = pl.pallas_call(
        make_kernel(dims),
        out_shape=[jax.ShapeDtypeStruct(s, t) for _, s, t in outs],
        in_specs=[vmem] * len(operands),
        out_specs=[vmem] * len(outs),
        scratch_shapes=[pltpu.VMEM(s, t) for _, s, t in bufs]
        + [pltpu.SemaphoreType.DMA(s) for _, s in sems],
        compiler_params=pltpu.CompilerParams(
            collective_id=0, has_side_effects=True, vmem_limit_bytes=62 * 1024 * 1024
        ),
        name="layers",
    )(*operands)
    o_layer, o_ig, o_in, o_back, o_qos, o_qoc, o_kv, o_small = res
    me = lax.axis_index("expert")
    dpi = lax.axis_index("dp")
    DB = D // DP
    EB = DB // E
    kv = lax.dynamic_slice_in_dim(o_kv, me * EB, EB, 1)
    small = lax.dynamic_slice_in_dim(o_small, (dpi * E + me) * EB, EB, 1)
    qos = o_qos.reshape(DB, 2, npd, HD)
    qoc = o_qoc.reshape(DB, 2, npd, HD)
    return (
        o_layer.reshape(inputs.shape),
        o_ig.reshape(inputs.shape),
        jnp.stack([small[0], small[4]])[None],
        jnp.stack([small[1], small[5]])[None],
        kv[0][None],
        small[6 : 6 + NE].T[None],
        qos[:, 0].transpose(1, 0, 2)[None],
        qos[:, 1].transpose(1, 2, 0)[None],
        o_in[None],
        o_back.T[None],
        small[2],
        small[3],
        kv[1],
        small[6 + NE : 6 + 2 * NE].T,
        qoc[:, 0].transpose(1, 0, 2),
        qoc[:, 1].transpose(1, 2, 0),
    )


def solution(mesh):
    placed = (
        P("section", None, "dp", "expert", None),
        P("section", None, "dp", "expert", None),
        P(None, None, "dp", None),
        P("section", None, "dp", None, None),
        P(None, "dp", None, None),
        P("section", None, None),
        P("section", None, None),
        P("section", None, None),
        P("section", None, None),
        P("section", "expert", None, None),
        P("section", "expert", None, None),
        P("section", None, "expert"),
        P("section", "expert", None),
        P(),
        P(),
        P(),
        P(),
        P("expert", None, None),
        P("expert", None, None),
    )
    return jax.shard_map(
        body,
        mesh=mesh,
        in_specs=placed,
        out_specs=(
            P("section", None, "dp", "expert", None),
            P("section", None, "dp", "expert", None),
            P("section", None, ("dp", "expert")),
            P("section", None, ("dp", "expert")),
            P("section", ("dp", "expert"), None),
            P("section", ("dp", "expert"), None),
            P("section", "expert", "dp", None),
            P("section", "expert", None, "dp"),
            P("section", "dp", "expert"),
            P("section", "expert", "dp"),
            P(("dp", "expert")),
            P(("dp", "expert")),
            P(("dp", "expert"), None),
            P(("dp", "expert"), None),
            P("expert", "dp", None),
            P("expert", None, "dp"),
        ),
        check_vma=False,
    )
```

```python
from types import SimpleNamespace

import jax
import jax.numpy as jnp
from jax import lax
from jax.experimental import pallas as pl
from jax.experimental.pallas import tpu as pltpu
from jax.sharding import PartitionSpec as P

F32 = jnp.float32
BF16 = jnp.bfloat16
MESH = pl.DeviceIdType.MESH
RT = 16
SR = 32
NP = 4


def nn(a, b):
    return lax.dot_general(a, b, (((1,), (0,)), ((), ())), preferred_element_type=F32)


def nt(a, b):
    return lax.dot_general(a, b, (((1,), (1,)), ((), ())), preferred_element_type=F32)


def tn(a, b):
    return lax.dot_general(a, b, (((0,), (0,)), ((), ())), preferred_element_type=F32)


def gelu_parts(h):
    c = 0.7978845608028654
    h2 = h * h
    t = jnp.tanh(c * h * (1.0 + 0.044715 * h2))
    half = 0.5 * (1.0 + t)
    slope = half + 0.5 * h * (1.0 - t * t) * (c * (1.0 + 3 * 0.044715 * h2))
    return h * half, slope


def norm_stats(x):
    centred = x - jnp.mean(x, -1, keepdims=True)
    r = lax.rsqrt(jnp.mean(centred * centred, -1, keepdims=True) + 1e-05)
    return centred * r, r


def norm_back(x, gain, grad):
    xhat, r = norm_stats(x)
    gg = grad * gain
    m1 = jnp.mean(gg, -1, keepdims=True)
    m2 = jnp.mean(gg * xhat, -1, keepdims=True)
    return (
        r * (gg - m1 - xhat * m2),
        jnp.sum(grad * xhat, 0, keepdims=True),
        jnp.sum(grad, 0, keepdims=True),
    )


def make_plan(dims):
    (NI, L, D, SEQ, T, NE, HD, HB, E, DP) = dims
    npd = NE // E
    QB = npd * HD
    NQ = NE * HD
    X = E // 2
    DB = D // DP
    ins = [
        "x", "cot", "pairs", "routes_s", "routes_c", "ng", "nb", "wkv", "wr", "wq", "wo", "win",
        "wback", "cg", "cb", "ckv", "cr", "cq", "co",
    ]
    outs = [
        ("o_layer", (NI, L, D), BF16),
        ("o_ig", (NI, L, D), F32),
        ("o_in", (DB, HB), F32),
        ("o_back", (DB, HB), F32),
        ("o_qo", (2, DB, 2 * QB), F32),
        ("o_kv", (2, DB, 2 * HD), F32),
        ("o_small", (SR, D), F32),
    ]
    bufs = [
        ("win_all", (E, D, HB), BF16),
        ("wback_all", (E, HB, D), BF16),
        ("wqr", (2, NQ + RT, D), BF16),
        ("wo_all", (2, NQ, D), BF16),
        ("wr_pad", (RT, D), F32),
        ("x1", (NI, L, D), F32),
        ("x2", (NI, L, D), F32),
        ("n", (NI, 3, L, D), BF16),
        ("dz", (NI, L, D), BF16),
        ("acc", (L, D), F32),
        ("act", (NI, E, L, HB), BF16),
        ("dh", (NI, E, L, HB), BF16),
        ("kv_s", (NI, SEQ, 2 * HD), BF16),
        ("kv_c", (NI, SEQ, 2 * HD), BF16),
        ("kvt", (2, NI, 2 * HD, SEQ), BF16),
        ("bias", (SEQ, L), F32),
        ("qt", (2, NI, T, HD, L), BF16),
        ("gate", (2, NI, T, 8, L), F32),
        ("p", (2, NI, T, SEQ, L), BF16),
        ("heads", (2, NI, T, HD, L), F32),
        ("ht", (2, NI, NQ, L), BF16),
        ("dq", (T, HD, L), BF16),
        ("dkv_acc", (SEQ, 2 * HD), F32),
        ("dkv_send", (NI, SEQ, 2 * HD), BF16),
        ("dkv_recv", (NI, E, L, 2 * HD), BF16),
        ("dckv_send", (NI, SEQ, 2 * HD), BF16),
        ("dckv_recv", (NI, E, L, 2 * HD), BF16),
        ("ckv_own", (NI, L, 2 * HD), BF16),
        ("g_big", (E, 2, D, HB), F32),
        ("g_qr", (2, NQ + RT, D), F32),
        ("g_o", (2, NQ, D), F32),
        ("g_kv", (2, D, 2 * HD), F32),
        ("small", (SR, D), F32),
        ("a_big", (2, X, D, HB), BF16),
        ("a_big_r", (2, X, D, HB), BF16),
        ("a_qo", (2, X, 2 * QB, D), BF16),
        ("a_qo_r", (2, X, 2 * QB, D), BF16),
        ("b_big", (X - 1, 2, D, HB), BF16),
        ("b_big_r", (X - 1, 2, D, HB), BF16),
        ("b_qo", (2, X - 1, 2 * QB, D), BF16),
        ("b_qo_r", (2, X - 1, 2 * QB, D), BF16),
        ("c_big", (DP - 1, 2, DB, HB), BF16),
        ("c_big_r", (DP - 1, 2, DB, HB), BF16),
        ("own_qo", (D, 2 * QB), F32),
        ("c_qo", (2, DP - 1, DB, 2 * QB), BF16),
        ("c_qo_r", (2, DP - 1, DB, 2 * QB), BF16),
        ("kv_ar", (D, 2 * HD), F32),
        ("kv_sum", (D, 2 * HD), F32),
        ("kv_b", (D, 2 * HD), BF16),
        ("kv_br", (X - 1, D, 2 * HD), BF16),
        ("kv_c2", (DP - 1, DB, 2 * HD), BF16),
        ("kv_cr", (DP - 1, DB, 2 * HD), BF16),
        ("kv_fin", (DB, 2 * HD), F32),
        ("kv_sib", (DB, 2 * HD), F32),
        ("kv_sec", (DB, 2 * HD), F32),
        ("sm_ar", (SR, D), F32),
        ("sm_b", (SR, D), BF16),
        ("sm_br", (X - 1, SR, D), BF16),
        ("sm_c", (SR, D), BF16),
        ("sm_cr", (DP - 1, SR, D), BF16),
        ("sm_fin", (SR, D), F32),
        ("sm_sec", (SR, D), F32),
        ("qo_fin", (DB, 2 * QB), F32),
        ("qo_sec", (DB, 2 * QB), F32),
    ]
    sems = [
        ("q_s", (2, 2, E)), ("q_r", (2, 2, E)),
        ("sib_s", (2,)), ("sib_r", (2,)),
        ("wx_s", (2, X, NP // 2)), ("wx_r", (2, X, NP // 2)),
        ("wz_s", (2, X, NP // 2)), ("wz_r", (2, X, NP // 2)),
        ("wf_s", (2, X, NP)), ("wf_r", (2, X, NP)),
        ("kv_ss", (NI, E)), ("kv_rs", (NI, E)),
        ("ckv_s", (NI, E)), ("ckv_r", (NI, E)),
        ("dckv_s", (NI, E)), ("dckv_r", (NI, E)),
        ("dkv_s", (NI, E)), ("dkv_r", (NI, E)),
        ("a_s", (2, X)), ("a_r", (2, X)),
        ("b_s", (X - 1, 2, DP)), ("b_r", (X - 1, 2, DP)),
        ("c_s", (2, DP - 1)), ("c_r", (2, DP - 1)),
        ("aq_s", (2,)), ("aq_r", (2,)),
        ("bq_s", (2, X - 1)), ("bq_r", (2, X - 1)),
        ("cq_s", (2, DP - 1)), ("cq_r", (2, DP - 1)),
        ("ka_s", (1,)), ("ka_r", (1,)),
        ("kb_s", (X - 1,)), ("kb_r", (X - 1,)),
        ("kc_s", (DP - 1,)), ("kc_r", (DP - 1,)),
        ("kf_s", (3,)), ("kf_r", (2,)),
        ("sa_s", (1,)), ("sa_r", (1,)),
        ("sb_s", (X - 1,)), ("sb_r", (X - 1,)),
        ("sc_s", (DP - 1,)), ("sc_r", (DP - 1,)),
        ("sec_s", (2,)), ("sec_r", (2,)),
    ]
    return ins, outs, bufs, sems


def make_kernel(dims):
    (NI, L, D, SEQ, T, NE, HD, HB, E, DP) = dims
    npd = NE // E
    QB = npd * HD
    NQ = NE * HD
    X = E // 2
    DB = D // DP
    scale = HD ** -0.5
    ins, outs, bufs, sems = make_plan(dims)
    names = ins + [o[0] for o in outs] + [b[0] for b in bufs] + [s[0] for s in sems]

    def kernel(*refs):
        r = SimpleNamespace(**dict(zip(names, refs)))
        sec = lax.axis_index("section")
        dpi = lax.axis_index("dp")
        me = lax.axis_index("expert")
        core = lax.rem(me, 2)
        xi = me // 2
        sib = xi * 2 + (1 - core)
        dec = sec == 1
        enc = sec == 0
        other = 1 - sec
        half = lax.rem(dpi, 2)
        mate = dpi + 1 - 2 * half
        row0 = pl.multiple_of(me * L, L)

        def to_expert(j):
            return (sec, dpi, j)

        def to_dp(j):
            return (sec, j, me)

        def to_section(j):
            return (other, dpi, j)

        def rcopy(src, dst, ssem, rsem, dev):
            return pltpu.make_async_remote_copy(
                src_ref=src, dst_ref=dst, send_sem=ssem, recv_sem=rsem, device_id=dev,
                device_id_type=MESH,
            )

        def chip(x):
            return x * 2 + core

        def q_copy(a, kind, block, to, slot):
            ref = r.wqr if kind == 0 else r.wo_all
            ref = ref.at[a, pl.ds(pl.multiple_of(block * QB, QB), QB)]
            return rcopy(ref, ref, r.q_s.at[a, kind, slot], r.q_r.at[a, kind, block], to_expert(to))

        def w_ref(kind, c):
            return (r.win_all if kind == 0 else r.wback_all).at[c]

        def w_piece(kind, c, p):
            rows = (D if kind == 0 else HB) // NP
            return w_ref(kind, c).at[pl.ds(pl.multiple_of(p * rows, rows), rows)]

        def sib_copy(kind, c):
            ref = w_ref(kind, c)
            return rcopy(ref, ref, r.sib_s.at[kind], r.sib_r.at[kind], to_expert(sib))

        def wx_copy(kind, c, q, to_x, frm_x):
            ref = w_piece(kind, c, 2 * q + half)
            return rcopy(
                ref, ref, r.wx_s.at[kind, to_x, q], r.wx_r.at[kind, frm_x, q],
                to_expert(chip(to_x)),
            )

        def wz_copy(kind, x, q, parity):
            ref = w_piece(kind, chip(x), 2 * q + parity)
            return rcopy(ref, ref, r.wz_s.at[kind, x, q], r.wz_r.at[kind, x, q], to_dp(mate))

        def wf_copy(kind, c, x, p):
            ref = w_piece(kind, c, p)
            return rcopy(ref, ref, r.wf_s.at[kind, x, p], r.wf_r.at[kind, x, p], to_expert(sib))

        def rows_of(ref, i, j):
            return ref.at[i, pl.ds(pl.multiple_of(j * L, L), L)]

        def kv_copy(i, block, to, slot):
            ref = rows_of(r.kv_s, i, block)
            return rcopy(ref, ref, r.kv_ss.at[i, slot], r.kv_rs.at[i, block], to_expert(to))

        def ckv_copy(i, block, to, frm):
            return rcopy(
                r.ckv_own.at[i], rows_of(r.kv_c, i, block), r.ckv_s.at[i, to], r.ckv_r.at[i, frm],
                to_section(to),
            )

        def dckv_copy(i, to, frm):
            return rcopy(
                rows_of(r.dckv_send, i, to), r.dckv_recv.at[i, frm], r.dckv_s.at[i, to],
                r.dckv_r.at[i, frm], to_section(to),
            )

        def dkv_copy(i, to, frm):
            return rcopy(
                rows_of(r.dkv_send, i, to), r.dkv_recv.at[i, frm], r.dkv_s.at[i, to],
                r.dkv_r.at[i, frm], to_expert(to),
            )

        def over_x(src, dst, ssem, rsem, o):
            return rcopy(src, dst, ssem, rsem, to_expert(chip(lax.rem(xi + o + 1, X))))

        def over_dp(src, dst, ssem, rsem, o):
            return rcopy(src, dst, ssem, rsem, to_dp(lax.rem(dpi + o + 1, DP)))

        def over_sib(src, dst, ssem, rsem):
            return rcopy(src, dst, ssem, rsem, to_expert(sib))

        def a_copy(kind, x):
            return over_sib(
                r.a_big.at[kind, x], r.a_big_r.at[kind, x], r.a_s.at[kind, x], r.a_r.at[kind, x]
            )

        def block_rows(d):
            return pl.ds(pl.multiple_of(d * DB, DB), DB)

        def b_copy(kind, o, d):
            return over_x(
                r.b_big.at[o, kind, block_rows(d)], r.b_big_r.at[o, kind, block_rows(d)],
                r.b_s.at[o, kind, d], r.b_r.at[o, kind, d], o,
            )

        def c_copy(kind, o):
            return over_dp(
                r.c_big.at[o, kind], r.c_big_r.at[o, kind], r.c_s.at[kind, o], r.c_r.at[kind, o], o
            )

        def aq_copy(a):
            return over_sib(r.a_qo.at[a], r.a_qo_r.at[a], r.aq_s.at[a], r.aq_r.at[a])

        def bq_copy(a, o):
            return over_x(
                r.b_qo.at[a, o], r.b_qo_r.at[a, o], r.bq_s.at[a, o], r.bq_r.at[a, o], o
            )

        def cq_copy(a, o):
            return over_dp(
                r.c_qo.at[a, o], r.c_qo_r.at[a, o], r.cq_s.at[a, o], r.cq_r.at[a, o], o
            )

        def ka_copy():
            return over_sib(r.g_kv.at[1 - core], r.kv_ar, r.ka_s.at[0], r.ka_r.at[0])

        def kb_copy(o):
            return over_x(r.kv_b, r.kv_br.at[o], r.kb_s.at[o], r.kb_r.at[o], o)

        def kc_copy(o):
            return over_dp(r.kv_c2.at[o], r.kv_cr.at[o], r.kc_s.at[o], r.kc_r.at[o], o)

        def kf_copy():
            return over_sib(r.kv_fin, r.kv_sib, r.kf_s.at[0], r.kf_r.at[0])

        def ks_copy(to_core):
            return rcopy(
                r.kv_fin, r.kv_sec, r.kf_s.at[1 + to_core], r.kf_r.at[1],
                to_section(xi * 2 + to_core),
            )

        def sa_copy():
            return over_sib(r.small, r.sm_ar, r.sa_s.at[0], r.sa_r.at[0])

        def sb_copy(o):
            return over_x(r.sm_b, r.sm_br.at[o], r.sb_s.at[o], r.sb_r.at[o], o)

        def sc_copy(o):
            return over_dp(r.sm_c, r.sm_cr.at[o], r.sc_s.at[o], r.sc_r.at[o], o)

        def sec_copy(kind):
            src, dst = ((r.qo_fin, r.qo_sec), (r.sm_fin, r.sm_sec))[kind]
            return rcopy(src, dst, r.sec_s.at[kind], r.sec_r.at[kind], to_section(me))

        def peers():
            return [lax.rem(me + o, E) for o in range(1, E)]

        def xpeers():
            return [lax.rem(xi + o, X) for o in range(1, X)]

        def dpeers():
            return [lax.rem(dpi + o, DP) for o in range(1, DP)]

        barrier = pltpu.get_barrier_semaphore()
        for j in peers():
            pl.semaphore_signal(barrier, inc=1, device_id=to_expert(j), device_id_type=MESH)
        for j in dpeers():
            pl.semaphore_signal(barrier, inc=1, device_id=to_dp(j), device_id_type=MESH)
        for j in range(E):
            pl.semaphore_signal(barrier, inc=1, device_id=to_section(j), device_id_type=MESH)

        for a, (q_ref, o_ref, wr_ref) in enumerate(((r.wq, r.wo, r.wr), (r.cq, r.co, r.cr))):
            for j in range(npd):
                at = pl.multiple_of(me * QB + j * HD, HD)
                r.wqr[a, pl.ds(at, HD)] = q_ref[j]
                r.wo_all[a, pl.ds(at, HD)] = o_ref[j]
            r.wr_pad[...] = jnp.zeros_like(r.wr_pad)
            r.wr_pad[:NE] = wr_ref[...].astype(F32)
            r.wqr[a, pl.ds(NQ, RT)] = r.wr_pad[...].astype(BF16)

        pl.semaphore_wait(barrier, (E - 1) + (DP - 1) + E)

        def gather_send(copy):
            copy(me, sib, sib).start()
            for x in xpeers():
                copy(me, chip(x), chip(x)).start()

        def gather_relay(copy):
            for x in xpeers():
                copy(chip(x), sib, x * 2 + 1 - core).wait_recv()
                copy(chip(x), sib, x * 2 + 1 - core).start()

        def gather_take(copy):
            copy(sib, sib, sib).wait_recv()
            for x in xpeers():
                c = x * 2 + 1 - core
                copy(c, sib, c).wait_recv()

        def gather_sent(copy):
            copy(me, sib, sib).wait_send()
            for x in xpeers():
                copy(me, chip(x), chip(x)).wait_send()
                copy(chip(x), sib, x * 2 + 1 - core).wait_send()

        def q_of(a, kind):
            return lambda block, to, slot: q_copy(a, kind, block, to, slot)

        def kv_of(i):
            return lambda block, to, slot: kv_copy(i, block, to, slot)

        for kind in (0, 1):
            gather_send(q_of(0, kind))

        def norm_rows(x, gain, shift):
            return norm_stats(x)[0] * gain + shift

        def gain_of(which):
            if which == 1:
                return r.cg[...], r.cb[...]
            return r.ng[which // 2 : which // 2 + 1], r.nb[which // 2 : which // 2 + 1]

        def first_norm(i, _):
            g, b = gain_of(0)
            n = norm_rows(r.x[i].astype(F32), g, b).astype(BF16)
            r.n[i, 0] = n
            r.kv_s[i, pl.ds(row0, L)] = nn(n, r.wkv[...]).astype(BF16)
            gather_send(kv_of(i))
            return 0

        lax.fori_loop(0, NI, first_norm, 0)

        r.win_all[me] = r.win[...]
        r.wback_all[me] = r.wback[...]
        for kind in (0, 1):
            sib_copy(kind, me).start()
        for kind in (0, 1):
            for q in range(NP // 2):
                for x in xpeers():
                    wx_copy(kind, me, q, x, xi).start()

        @pl.when(dec)
        def _():
            for kind in (0, 1):
                gather_send(q_of(1, kind))

        def weights_over_x(kind, q):
            for x in xpeers():
                wx_copy(kind, chip(x), q, x, x).wait_recv()
                wz_copy(kind, x, q, half).start()
                wf_copy(kind, chip(x), x, 2 * q + half).start()

        def weights_over_z(kind, q):
            for x in xpeers():
                wz_copy(kind, x, q, 1 - half).wait_recv()
                wf_copy(kind, chip(x), x, 2 * q + 1 - half).start()

        def weights_over_sib(kind):
            for x in xpeers():
                for p in range(NP):
                    wf_copy(kind, x * 2 + 1 - core, x, p).wait_recv()

        def weights_sent():
            for kind in (0, 1):
                sib_copy(kind, me).wait_send()
                for x in xpeers():
                    for q in range(NP // 2):
                        wx_copy(kind, me, q, x, xi).wait_send()
                        wz_copy(kind, x, q, half).wait_send()
                    for p in range(NP):
                        wf_copy(kind, chip(x), x, p).wait_send()

        zeros_h = jnp.zeros((HD, L), BF16)

        def set_bias(i, a):
            own = r.pairs[sec, i, :, pl.ds(row0, L)].astype(F32)
            if a == 0:
                keys = r.pairs[sec, i].astype(F32)
            else:
                keys = r.pairs[0, i].astype(F32)
            kc = jnp.broadcast_to(keys, (128, SEQ)).T
            if L > 128:
                kc = jnp.concatenate([kc] * (L // 128), 1)
            same = kc == own
            if a == 0:
                qpos = row0 + lax.broadcasted_iota(jnp.int32, (1, L), 1)
                limit = jnp.where(dec, qpos, SEQ)
                same = same & (lax.broadcasted_iota(jnp.int32, (SEQ, L), 0) <= limit)
            r.bias[...] = jnp.where(same, 0.0, -1e30)

        def route_rows(i, a):
            ref = r.routes_s if a == 0 else r.routes_c
            return [ref[i, k : k + 1, pl.ds(row0, L)] for k in range(T)]

        def pick(rows, route, size):
            total = jnp.zeros((size, L), F32)
            for e in range(NE):
                total = jnp.where(route == e, rows[e * size : (e + 1) * size], total)
            return total

        def project_queries(i, a):
            n = r.n[i, a]
            ql = nt(r.wqr[a], n)
            routes = route_rows(i, a)
            chosen = []
            for k in range(T):
                r.qt[a, i, k] = (pick(ql[:NQ], routes[k], HD).astype(BF16).astype(F32) * scale).astype(BF16)
                chosen.append(pick(ql[NQ : NQ + NE], routes[k], 1))
            top = chosen[0]
            for k in range(1, T):
                top = jnp.maximum(top, chosen[k])
            ex = [jnp.exp(c - top) for c in chosen]
            total = ex[0]
            for k in range(1, T):
                total = total + ex[k]
            for k in range(T):
                r.gate[a, i, k] = jnp.broadcast_to(ex[k] / total, (8, L))

        def attend(i, a, kv_ref, base):
            kv = kv_ref[i]
            r.kvt[a, i] = kv.astype(F32).T.astype(BF16)

            def one(k, _):
                q = jnp.concatenate([r.qt[a, i, k], zeros_h], 0)
                s = nn(kv, q) + r.bias[...]
                m = jnp.max(s, 0, keepdims=True)
                ex = jnp.exp(s - m)
                p = (ex * (1.0 / jnp.sum(ex, 0, keepdims=True))).astype(BF16)
                r.p[a, i, k] = p
                r.heads[a, i, k] = nn(r.kvt[a, i, HD:], p)
                return 0

            lax.fori_loop(0, T, one, 0)
            routes = route_rows(i, a)
            gated = [
                r.heads[a, i, k].astype(BF16).astype(F32) * r.gate[a, i, k, 0:1] for k in range(T)
            ]
            for e in range(NE):
                block = jnp.zeros((HD, L), F32)
                for k in range(T):
                    block = jnp.where(routes[k] == e, gated[k], block)
                r.ht[a, i, e * HD : (e + 1) * HD] = block.astype(BF16)
            return base + tn(r.ht[a, i], r.wo_all[a])

        def attend_back(i, a, kv_ref, dx, send_ref):
            dxb = dx.astype(BF16)
            routes = route_rows(i, a)
            r.g_o[a] += nn(r.ht[a, i], dxb)
            gt = nt(r.wo_all[a], dxb)
            dgates = []
            for k in range(T):
                g = pick(gt, routes[k], HD)
                dgates.append(
                    jnp.sum(r.heads[a, i, k].astype(BF16).astype(F32) * g, 0, keepdims=True)
                )
                r.dq[k] = (g * r.gate[a, i, k, 0:1]).astype(BF16)
            gates = [r.gate[a, i, k, 0:1] for k in range(T)]
            mid = gates[0] * dgates[0]
            for k in range(1, T):
                mid = mid + gates[k] * dgates[k]
            dchosen = [gates[k] * (dgates[k] - mid) for k in range(T)]
            kv = kv_ref[i]
            r.dkv_acc[...] = jnp.zeros_like(r.dkv_acc)

            def one(k, _):
                dheads = r.dq[k]
                p = r.p[a, i, k]
                dv = jnp.concatenate([zeros_h, dheads], 0)
                dp = nn(kv, dv)
                pf = p.astype(F32)
                delta = jnp.sum(dp * pf, 0, keepdims=True)
                ds = (pf * (dp - delta)).astype(BF16)
                qk = jnp.concatenate([r.qt[a, i, k], zeros_h], 0)
                r.dkv_acc[...] += nt(ds, qk) + nt(p, dv)
                r.dq[k] = (nn(r.kvt[a, i, :HD], ds) * scale).astype(BF16)
                return 0

            lax.fori_loop(0, T, one, 0)
            send_ref[i] = r.dkv_acc[...].astype(BF16)
            blocks = []
            for e in range(NE):
                block = jnp.zeros((HD, L), F32)
                for k in range(T):
                    block = jnp.where(routes[k] == e, r.dq[k].astype(F32), block)
                blocks.append(block)
            logit_rows = jnp.zeros((RT, L), F32)
            rows = lax.broadcasted_iota(jnp.int32, (RT, L), 0)
            for k in range(T):
                logit_rows = jnp.where(rows == routes[k], dchosen[k], logit_rows)
            dql = jnp.concatenate(blocks + [logit_rows], 0).astype(BF16)
            r.g_qr[a] += nn(dql, r.n[i, a])
            return tn(dql, r.wqr[a])

        def chunk_at(s):
            return lax.rem(xi + s // 2, X) * 2 + jnp.where(lax.rem(s, 2) == 0, core, 1 - core)

        def chunk_out(s):
            return lax.rem(xi + s // 2 + 1, X) * 2 + jnp.where(lax.rem(s, 2) == 0, 1 - core, core)

        def ffn_forward(i, low, high):
            n = r.n[i, 2]

            def one(s, _):
                c = chunk_at(s)
                act, slope = gelu_parts(nn(n, r.win_all[c]))
                act = act.astype(BF16)
                r.act[i, c] = act
                r.dh[i, c] = slope.astype(BF16)
                r.acc[...] += nn(act, r.wback_all[c])
                return 0

            lax.fori_loop(low, high, one, 0)

        def ffn_middle(i):
            n = r.n[i, 2]
            dz = r.cot[i]
            r.acc[...] = jnp.zeros_like(r.acc)

            def one(c, _):
                act, slope = gelu_parts(nn(n, r.win_all[c]))
                r.act[i, c] = act.astype(BF16)
                dh = (nt(dz, r.wback_all[c]) * slope).astype(BF16)
                r.dh[i, c] = dh
                r.acc[...] += nt(dh, r.win_all[c])
                return 0

            lax.fori_loop(0, E, one, 0)
            return r.acc[...]

        def hand_out(i, s, c, kind):
            @pl.when((i == NI - 1) & (lax.rem(s, 2) == 0))
            def _():
                x = c // 2
                r.a_big[kind, x] = r.g_big[c, kind].astype(BF16)
                a_copy(kind, x).start()

        def ffn_back(i):
            dz = r.dz[i]
            dzt = dz.astype(F32).T.astype(BF16)
            nt_ = r.n[i, 2].astype(F32).T.astype(BF16)
            r.acc[...] = jnp.zeros_like(r.acc)

            def back(s, _):
                c = chunk_out(s)
                r.g_big[c, 1] += nn(dzt, r.act[i, c])
                hand_out(i, s, c, 1)
                return 0

            lax.fori_loop(0, E, back, 0)

            def inward(s, _):
                c = chunk_out(s)
                dh = (nt(dz, r.wback_all[c]) * r.dh[i, c].astype(F32)).astype(BF16)
                r.acc[...] += nt(dh, r.win_all[c])
                r.g_big[c, 0] += nn(nt_, dh)
                hand_out(i, s, c, 0)
                return 0

            lax.fori_loop(0, E, inward, 0)
            return r.acc[...]

        def ffn_weights(i):
            dzt = r.cot[i].astype(F32).T.astype(BF16)
            nt_ = r.n[i, 2].astype(F32).T.astype(BF16)
            r.acc[...] = r.x2[i]

            def one(s, _):
                c = chunk_out(s)
                act = r.act[i, c]
                r.g_big[c, 1] += nn(dzt, act)
                hand_out(i, s, c, 1)
                r.g_big[c, 0] += nn(nt_, r.dh[i, c])
                hand_out(i, s, c, 0)
                r.acc[...] += nn(act, r.wback_all[c])
                return 0

            lax.fori_loop(0, E, one, 0)
            r.o_layer[i] = r.acc[...].astype(BF16)

        def add_small(which, dgain, dshift):
            r.small[2 * which : 2 * which + 1] += dgain
            r.small[2 * which + 1 : 2 * which + 2] += dshift

        r.small[...] = jnp.zeros_like(r.small)
        r.g_qr[...] = jnp.zeros_like(r.g_qr)
        r.g_o[...] = jnp.zeros_like(r.g_o)
        r.g_kv[...] = jnp.zeros_like(r.g_kv)

        def zero_big(c, _):
            r.g_big[c] = jnp.zeros((2, D, HB), F32)
            return 0

        lax.fori_loop(0, E, zero_big, 0)

        for kind in (0, 1):
            gather_relay(q_of(0, kind))
        for kind in (0, 1):
            gather_take(q_of(0, kind))

        def forward(i, _):
            project_queries(i, 0)
            set_bias(i, 0)
            gather_relay(kv_of(i))
            gather_take(kv_of(i))
            x1 = attend(i, 0, r.kv_s, r.x[i].astype(F32))
            r.x1[i] = x1

            @pl.when(enc)
            def _():
                g, b = gain_of(2)
                r.n[i, 2] = norm_rows(r.x1[i], g, b).astype(BF16)

            @pl.when(dec)
            def _():
                g, b = gain_of(1)
                r.n[i, 1] = norm_rows(r.x1[i], g, b).astype(BF16)

            return 0

        lax.fori_loop(0, NI, forward, 0)

        @pl.when(enc)
        def _():
            r.acc[...] = r.x1[0]
            for kind in (0, 1):
                sib_copy(kind, sib).wait_recv()
            ffn_forward(0, 0, 2)

        for kind in (0, 1):
            for q in range(NP // 2):
                weights_over_x(kind, q)
        for kind in (0, 1):
            for q in range(NP // 2):
                weights_over_z(kind, q)
        for kind in (0, 1):
            weights_over_sib(kind)

        @pl.when(enc)
        def _():
            def encode(i, _):
                @pl.when(i == 0)
                def _():
                    ffn_forward(0, 2, E)

                @pl.when(i > 0)
                def _():
                    r.acc[...] = r.x1[i]
                    ffn_forward(i, 0, E)

                mem = r.acc[...].astype(BF16)
                r.o_layer[i] = mem
                r.ckv_own[i] = nn(mem, r.ckv[...]).astype(BF16)
                for j in range(E):
                    ckv_copy(i, me, j, me).start()
                return 0

            lax.fori_loop(0, NI, encode, 0)

        @pl.when(dec)
        def _():
            for kind in (0, 1):
                sib_copy(kind, sib).wait_recv()
            for kind in (0, 1):
                gather_relay(q_of(1, kind))
            for kind in (0, 1):
                gather_take(q_of(1, kind))

            def middle(i, _):
                project_queries(i, 1)
                set_bias(i, 1)
                for j in range(E):
                    ckv_copy(i, j, j, j).wait_recv()
                x2 = attend(i, 1, r.kv_c, r.x1[i])
                r.x2[i] = x2
                g, b = gain_of(2)
                r.n[i, 2] = norm_rows(x2, g, b).astype(BF16)
                dn = ffn_middle(i)
                dx, dg, db = norm_back(r.x2[i], g, dn)
                add_small(2, dg, db)
                r.o_ig[i] = r.cot[i].astype(F32) + dx
                dn = attend_back(i, 1, r.kv_c, r.o_ig[i], r.dckv_send)
                for j in range(E):
                    dckv_copy(i, j, me).start()
                g, b = gain_of(1)
                dx, dg, db = norm_back(r.x1[i], g, dn)
                add_small(1, dg, db)
                r.o_ig[i] += dx
                return 0

            lax.fori_loop(0, NI, middle, 0)

            def weights(i, _):
                ffn_weights(i)
                return 0

            lax.fori_loop(0, NI, weights, 0)

        def big_sib(kind):
            for o, x in enumerate(xpeers()):
                a_copy(kind, x).wait_recv()
                r.b_big[o, kind] = (
                    r.g_big[chip(x), kind] + r.a_big_r[kind, x].astype(F32)
                ).astype(BF16)
            a_copy(kind, xi).wait_recv()
            r.g_big[me, kind] += r.a_big_r[kind, xi].astype(F32)

        def dp_at(s):
            return lax.rem(dpi + s + 1, DP)

        def big_send(kind, low, high):
            for s in range(low, high):
                for o in range(X - 1):
                    b_copy(kind, o, dp_at(s)).start()

        def big_over_x(kind, s):
            d = dp_at(s)
            total = r.g_big[me, kind, block_rows(d)]
            for o in range(X - 1):
                b_copy(kind, o, d).wait_recv()
                total = total + r.b_big_r[o, kind, block_rows(d)].astype(F32)
            if s < DP - 1:
                r.c_big[s, kind] = total.astype(BF16)
                c_copy(kind, s).start()
            else:
                r.g_big[me, kind, block_rows(d)] = total

        def big_end(kind, out):
            total = r.g_big[me, kind, block_rows(dpi)]
            for o in range(DP - 1):
                c_copy(kind, o).wait_recv()
                total = total + r.c_big_r[o, kind].astype(F32)
            out[...] = total

        def qo_rows(a, c):
            at = pl.ds(pl.multiple_of(c * QB, QB), QB)
            return jnp.concatenate([r.g_qr[a, at], r.g_o[a, at]], 0)

        def qo_send(a):
            for x in range(X):
                r.a_qo[a, x] = qo_rows(a, x * 2 + (1 - core)).astype(BF16)
            aq_copy(a).start()

        def qo_sib(a):
            aq_copy(a).wait_recv()
            for o, x in enumerate(xpeers()):
                r.b_qo[a, o] = (qo_rows(a, chip(x)) + r.a_qo_r[a, x].astype(F32)).astype(BF16)
                bq_copy(a, o).start()

        def qo_over_x(a):
            total = qo_rows(a, me) + r.a_qo_r[a, xi].astype(F32)
            for o in range(X - 1):
                bq_copy(a, o).wait_recv()
                total = total + r.b_qo_r[a, o].astype(F32)
            r.own_qo[...] = total.T
            for o in range(DP - 1):
                r.c_qo[a, o] = r.own_qo[block_rows(dp_at(o))].astype(BF16)
                cq_copy(a, o).start()
            return r.own_qo[block_rows(dpi)]

        def qo_end(a, total):
            for o in range(DP - 1):
                cq_copy(a, o).wait_recv()
                total = total + r.c_qo_r[a, o].astype(F32)
            return total

        kv_busy = enc | (core == 0)
        kv_sib_busy = enc | (core == 1)

        def kv_send():
            @pl.when(kv_sib_busy)
            def _():
                ka_copy().start()

        def kv_sib():
            @pl.when(kv_busy)
            def _():
                ka_copy().wait_recv()
                total = r.g_kv[core] + r.kv_ar[...]
                r.kv_sum[...] = total
                r.kv_b[...] = total.astype(BF16)
                for o in range(X - 1):
                    kb_copy(o).start()

        def kv_over_x():
            @pl.when(kv_busy)
            def _():
                total = r.kv_sum[...]
                for o in range(X - 1):
                    kb_copy(o).wait_recv()
                    total = total + r.kv_br[o].astype(F32)
                r.kv_sum[...] = total
                for o in range(DP - 1):
                    r.kv_c2[o] = r.kv_sum[block_rows(dp_at(o))].astype(BF16)
                    kc_copy(o).start()

        def kv_over_dp():
            @pl.when(kv_busy)
            def _():
                total = r.kv_sum[block_rows(dpi)]
                for o in range(DP - 1):
                    kc_copy(o).wait_recv()
                    total = total + r.kv_cr[o].astype(F32)
                r.kv_fin[...] = total
                kf_copy().start()

            @pl.when(enc & (core == 1))
            def _():
                ks_copy(0).start()
                ks_copy(1).start()

        def kv_end():
            @pl.when(kv_sib_busy)
            def _():
                kf_copy().wait_recv()

            @pl.when(dec)
            def _():
                ks_copy(core).wait_recv()
                r.o_kv[0] = jnp.where(core == 0, r.kv_fin[...], r.kv_sib[...])
                r.o_kv[1] = r.kv_sec[...]

            @pl.when(enc)
            def _():
                r.o_kv[0] = jnp.where(core == 0, r.kv_fin[...], r.kv_sib[...])
                r.o_kv[1] = jnp.where(core == 0, r.kv_sib[...], r.kv_fin[...])

        def small_sib():
            sa_copy().wait_recv()
            r.sm_fin[...] = r.small[...] + r.sm_ar[...]
            r.sm_b[...] = r.sm_fin[...].astype(BF16)
            for o in range(X - 1):
                sb_copy(o).start()

        def small_over_x():
            total = r.sm_fin[...]
            for o in range(X - 1):
                sb_copy(o).wait_recv()
                total = total + r.sm_br[o].astype(F32)
            r.sm_fin[...] = total
            r.sm_c[...] = total.astype(BF16)
            for o in range(DP - 1):
                sc_copy(o).start()

        def small_over_dp():
            total = r.sm_fin[...]
            for o in range(DP - 1):
                sc_copy(o).wait_recv()
                total = total + r.sm_cr[o].astype(F32)
            r.sm_fin[...] = total

        def backward(i, _):
            @pl.when(enc)
            def _():
                total = jnp.zeros((L, 2 * HD), F32)
                for j in range(E):
                    dckv_copy(i, j, j).wait_recv()
                    total = total + r.dckv_recv[i, j].astype(F32)
                dkv = total.astype(BF16)
                dmem = nt(dkv, r.ckv[...]).astype(BF16).astype(F32)
                dx = r.cot[i].astype(F32) + dmem
                r.o_ig[i] = dx
                r.dz[i] = dx.astype(BF16)
                dn = ffn_back(i)
                r.g_kv[1] += tn(r.o_layer[i], dkv)
                g, b = gain_of(2)
                dx, dg, db = norm_back(r.x1[i], g, dn)
                add_small(2, dg, db)
                r.o_ig[i] += dx

            @pl.when(i == NI - 1)
            def _():
                big_sib(1)
                big_send(1, 0, DP // 2)

            r.acc[...] = attend_back(i, 0, r.kv_s, r.o_ig[i], r.dkv_send)
            for j in peers():
                dkv_copy(i, j, me).start()

            @pl.when(i == NI - 1)
            def _():
                big_send(1, DP // 2, DP)
                qo_send(0)
                big_sib(0)
                big_send(0, 0, DP // 2)

            total = r.dkv_send[i, pl.ds(row0, L)].astype(F32)
            for j in peers():
                dkv_copy(i, j, j).wait_recv()
                total = total + r.dkv_recv[i, j].astype(F32)
            dkv = total.astype(BF16)
            r.g_kv[0] += tn(r.n[i, 0], dkv)
            dn = r.acc[...] + nt(dkv, r.wkv[...])
            g, b = gain_of(0)
            dx, dg, db = norm_back(r.x[i].astype(F32), g, dn)
            add_small(0, dg, db)
            r.o_ig[i] += dx
            return 0

        lax.fori_loop(0, NI, backward, 0)

        for a in range(2):
            r.small[6 + a * NE : 6 + (a + 1) * NE] = r.g_qr[a, NQ : NQ + NE]
        sa_copy().start()
        kv_send()

        @pl.when(dec)
        def _():
            qo_send(1)

        qo_sib(0)
        small_sib()
        kv_sib()

        @pl.when(dec)
        def _():
            qo_sib(1)

        big_send(0, DP // 2, DP)
        for s in range(DP):
            big_over_x(1, s)
        small_over_x()
        kv_over_x()
        own_qo = qo_over_x(0)
        r.o_qo[0] = own_qo

        @pl.when(dec)
        def _():
            r.qo_fin[...] = qo_over_x(1)

        for s in range(DP):
            big_over_x(0, s)
        small_over_dp()
        kv_over_dp()
        r.o_qo[0] = qo_end(0, r.o_qo[0])

        @pl.when(dec)
        def _():
            sec_copy(1).start()
            r.qo_fin[...] = qo_end(1, r.qo_fin[...])
            sec_copy(0).start()
            r.o_qo[1] = r.qo_fin[...]
            r.o_small[...] = r.sm_fin[...]

        big_end(1, r.o_back)
        big_end(0, r.o_in)
        kv_end()

        @pl.when(enc)
        def _():
            sec_copy(1).wait_recv()
            sec_copy(0).wait_recv()
            r.o_qo[1] = r.qo_sec[...]
            rows = lax.broadcasted_iota(jnp.int32, (SR, D), 0)
            theirs = ((rows >= 2) & (rows < 4)) | ((rows >= 6 + NE) & (rows < 6 + 2 * NE))
            r.o_small[...] = jnp.where(theirs, r.sm_sec[...], r.sm_fin[...])

        for kind in (0, 1):
            gather_sent(q_of(0, kind))
            for x in range(X):
                a_copy(kind, x).wait_send()
            for o in range(X - 1):
                for d in range(DP):
                    b_copy(kind, o, d).wait_send()
            for o in range(DP - 1):
                c_copy(kind, o).wait_send()
        weights_sent()
        sa_copy().wait_send()
        for o in range(X - 1):
            sb_copy(o).wait_send()
        for o in range(DP - 1):
            sc_copy(o).wait_send()

        def qo_sent(a):
            aq_copy(a).wait_send()
            for o in range(X - 1):
                bq_copy(a, o).wait_send()
            for o in range(DP - 1):
                cq_copy(a, o).wait_send()

        qo_sent(0)

        @pl.when(dec)
        def _():
            for kind in (0, 1):
                gather_sent(q_of(1, kind))
                sec_copy(kind).wait_send()
            qo_sent(1)

        @pl.when(kv_sib_busy)
        def _():
            ka_copy().wait_send()

        @pl.when(kv_busy)
        def _():
            for o in range(X - 1):
                kb_copy(o).wait_send()
            for o in range(DP - 1):
                kc_copy(o).wait_send()
            kf_copy().wait_send()

        @pl.when(enc & (core == 1))
        def _():
            ks_copy(0).wait_send()
            ks_copy(1).wait_send()

        def sent(i, _):
            gather_sent(kv_of(i))
            for j in peers():
                dkv_copy(i, j, me).wait_send()

            @pl.when(enc)
            def _():
                for j in range(E):
                    ckv_copy(i, me, j, me).wait_send()

            @pl.when(dec)
            def _():
                for j in range(E):
                    dckv_copy(i, j, me).wait_send()

            return 0

        lax.fori_loop(0, NI, sent, 0)

    return kernel


def make_finish(E, NE, EB, QB):
    def kernel(
        layer, grads, w_in, w_back, qo, kv, small, o_layer, o_grads, o_gain, o_bias, o_kv, o_router,
        o_query, o_out, o_w_in, o_w_back, o_cgain, o_cbias, o_ckv, o_crouter, o_cquery, o_cout,
    ):
        me = lax.axis_index("expert")
        o_layer[...] = layer[...]
        o_grads[...] = grads[...]
        o_w_in[...] = w_in[...]
        o_w_back[...] = w_back[...].T
        for a, (q, o) in enumerate(((o_query, o_out), (o_cquery, o_cout))):
            both = qo[a].T
            q[...] = both[:QB]
            o[...] = both[QB:]
        for a, out in enumerate((o_kv, o_ckv)):
            total = kv[a, :EB]
            for j in range(1, E):
                total = jnp.where(me == j, kv[a, j * EB : (j + 1) * EB], total)
            out[...] = total
        off = (lax.axis_index("dp") * E + me) * EB
        part = small[:, pl.ds(pl.multiple_of(off // 128 * 128, 128), 128)]
        part = pltpu.roll(part, lax.rem(128 - lax.rem(off, 128), 128), 1)[:, :EB]
        o_gain[0] = jnp.concatenate([part[0:1], part[4:5]], 0)
        o_bias[0] = jnp.concatenate([part[1:2], part[5:6]], 0)
        o_cgain[...] = part[2:3]
        o_cbias[...] = part[3:4]
        o_router[...] = part[6 : 6 + NE]
        o_crouter[...] = part[6 + NE : 6 + 2 * NE]

    return kernel


def body(
    inputs, cotangents, pair_ids, self_routes, cross_routes, norm_gain, norm_bias, w_kv, w_router,
    w_query, w_out, w_in, w_back, cross_gain, cross_bias, cross_kv, cross_router, cross_query,
    cross_out,
):
    E = lax.axis_size("expert")
    DP = lax.axis_size("dp")
    _, MB, R, L, D = inputs.shape
    NI = MB * R
    SEQ = pair_ids.shape[-1]
    T = self_routes.shape[-1]
    NE = w_router.shape[-1]
    HD = w_query.shape[-1]
    HB = w_in.shape[-1]
    npd = NE // E
    QB = npd * HD
    dims = (NI, L, D, SEQ, T, NE, HD, HB, E, DP)
    ins, outs, bufs, sems = make_plan(dims)

    operands = [
        inputs.reshape(NI, L, D),
        cotangents.reshape(NI, L, D),
        pair_ids.reshape(2, NI, 1, SEQ),
        jnp.swapaxes(self_routes.reshape(NI, SEQ, T), 1, 2),
        jnp.swapaxes(cross_routes.reshape(NI, SEQ, T), 1, 2),
        norm_gain[0],
        norm_bias[0],
        w_kv[0],
        w_router[0].T,
        jnp.swapaxes(w_query[0], 1, 2),
        w_out[0],
        w_in[0],
        w_back[0],
        cross_gain[None],
        cross_bias[None],
        cross_kv,
        cross_router.T,
        jnp.swapaxes(cross_query, 1, 2),
        cross_out,
    ]
    vmem = pl.BlockSpec(memory_space=pltpu.VMEM)
    res = pl.pallas_call(
        make_kernel(dims),
        out_shape=[jax.ShapeDtypeStruct(s, t) for _, s, t in outs],
        in_specs=[vmem] * len(operands),
        out_specs=[vmem] * len(outs),
        scratch_shapes=[pltpu.VMEM(s, t) for _, s, t in bufs]
        + [pltpu.SemaphoreType.DMA(s) for _, s in sems],
        compiler_params=pltpu.CompilerParams(
            collective_id=0, has_side_effects=True, vmem_limit_bytes=62 * 1024 * 1024
        ),
        name="layers",
    )(*operands)
    DB = D // DP
    EB = DB // E
    shapes = [
        ((NI, L, D), BF16),
        ((NI, L, D), F32),
        ((1, 2, EB), F32),
        ((1, 2, EB), F32),
        ((EB, 2 * HD), F32),
        ((NE, EB), F32),
        ((QB, DB), F32),
        ((QB, DB), F32),
        ((DB, HB), F32),
        ((HB, DB), F32),
        ((1, EB), F32),
        ((1, EB), F32),
        ((EB, 2 * HD), F32),
        ((NE, EB), F32),
        ((QB, DB), F32),
        ((QB, DB), F32),
    ]
    (
        layer, grads, gain, bias, kv, router, query, out, w_in_g, w_back_g, c_gain, c_bias, c_kv,
        c_router, c_query, c_out,
    ) = pl.pallas_call(
        make_finish(E, NE, EB, QB),
        out_shape=[jax.ShapeDtypeStruct(s, t) for s, t in shapes],
        in_specs=[vmem] * len(outs),
        out_specs=[vmem] * len(shapes),
        name="results",
    )(*res)

    def of_query(g):
        return jnp.swapaxes(g.reshape(npd, HD, DB), 1, 2)

    def of_out(g):
        return g.reshape(npd, HD, DB)

    return (
        layer.reshape(inputs.shape),
        grads.reshape(inputs.shape),
        gain,
        bias,
        kv[None],
        router.T[None],
        of_query(query)[None],
        of_out(out)[None],
        w_in_g[None],
        w_back_g[None],
        c_gain[0],
        c_bias[0],
        c_kv,
        c_router.T,
        of_query(c_query),
        of_out(c_out),
    )


def solution(mesh):
    placed = (
        P("section", None, "dp", "expert", None),
        P("section", None, "dp", "expert", None),
        P(None, None, "dp", None),
        P("section", None, "dp", None, None),
        P(None, "dp", None, None),
        P("section", None, None),
        P("section", None, None),
        P("section", None, None),
        P("section", None, None),
        P("section", "expert", None, None),
        P("section", "expert", None, None),
        P("section", None, "expert"),
        P("section", "expert", None),
        P(),
        P(),
        P(),
        P(),
        P("expert", None, None),
        P("expert", None, None),
    )
    return jax.shard_map(
        body,
        mesh=mesh,
        in_specs=placed,
        out_specs=(
            P("section", None, "dp", "expert", None),
            P("section", None, "dp", "expert", None),
            P("section", None, ("dp", "expert")),
            P("section", None, ("dp", "expert")),
            P("section", ("dp", "expert"), None),
            P("section", ("dp", "expert"), None),
            P("section", "expert", "dp", None),
            P("section", "expert", None, "dp"),
            P("section", "dp", "expert"),
            P("section", "expert", "dp"),
            P(("dp", "expert")),
            P(("dp", "expert")),
            P(("dp", "expert"), None),
            P(("dp", "expert"), None),
            P("expert", "dp", None),
            P("expert", None, "dp"),
        ),
        check_vma=False,
    )
```

```python
from types import SimpleNamespace

import jax
import jax.numpy as jnp
from jax import lax
from jax.experimental import pallas as pl
from jax.experimental.pallas import tpu as pltpu
from jax.sharding import PartitionSpec as P

F32 = jnp.float32
BF16 = jnp.bfloat16
MESH = pl.DeviceIdType.MESH
RT = 16
SR = 32
NP = 8
NS = 3
NX = NP - NS


def nn(a, b):
    return lax.dot_general(a, b, (((1,), (0,)), ((), ())), preferred_element_type=F32)


def nt(a, b):
    return lax.dot_general(a, b, (((1,), (1,)), ((), ())), preferred_element_type=F32)


def tn(a, b):
    return lax.dot_general(a, b, (((0,), (0,)), ((), ())), preferred_element_type=F32)


def gelu_parts(h):
    c = 0.7978845608028654
    h2 = h * h
    t = jnp.tanh(c * h * (1.0 + 0.044715 * h2))
    half = 0.5 * (1.0 + t)
    slope = half + 0.5 * h * (1.0 - t * t) * (c * (1.0 + 3 * 0.044715 * h2))
    return h * half, slope


def norm_stats(x):
    centred = x - jnp.mean(x, -1, keepdims=True)
    r = lax.rsqrt(jnp.mean(centred * centred, -1, keepdims=True) + 1e-05)
    return centred * r, r


def norm_back(x, gain, grad):
    xhat, r = norm_stats(x)
    gg = grad * gain
    m1 = jnp.mean(gg, -1, keepdims=True)
    m2 = jnp.mean(gg * xhat, -1, keepdims=True)
    return (
        r * (gg - m1 - xhat * m2),
        jnp.sum(grad * xhat, 0, keepdims=True),
        jnp.sum(grad, 0, keepdims=True),
    )


INS = [
    "x", "cot", "pairs", "routes_s", "routes_c", "ng", "nb", "wkv", "wr", "wq", "wo", "win",
    "wback", "cg", "cb", "ckv", "cr", "cq", "co",
]
STAY = ("wr", "cr")
PLACED = ("win", "wback")


def fetched(ins):
    return [n for n in ins if n not in STAY + PLACED]


def make_plan(dims):
    (NI, L, D, SEQ, T, NE, HD, HB, E, DP) = dims
    npd = NE // E
    QB = npd * HD
    NQ = NE * HD
    X = E // 2
    DB = D // DP
    HP = DP // 2
    ins = INS
    outs = dict(
        out_layer=((NI, L, D), BF16),
        out_ig=((NI, L, D), F32),
        o_in=((DB, HB), F32),
        o_back=((DB, HB), F32),
        o_qo=((2, DB, 2 * QB), F32),
        o_kv=((2, DB, 2 * HD), F32),
        o_small=((SR, D), F32),
    )
    bufs = dict(
        o_layer=((NI, L, D), BF16),
        o_ig=((NI, L, D), F32),
        win_all=((E, D, HB), BF16),
        wback_all=((E, HB, D), BF16),
        wqr=((2, NQ + RT, D), BF16),
        wo_all=((2, NQ, D), BF16),
        wr_pad=((RT, D), F32),
        x1=((NI, L, D), F32),
        x2=((NI, L, D), F32),
        n=((NI, 3, L, D), BF16),
        dz=((NI, L, D), BF16),
        acc=((L, D), F32),
        dn=((NI, L, D), F32),
        act=((NI, E, L, HB), BF16),
        turned=((NI, D, L), BF16),
        dh=((NI, E, L, HB), BF16),
        kv_s=((NI, SEQ, 2 * HD), BF16),
        kv_c=((NI, SEQ, 2 * HD), BF16),
        kvt=((2, NI, 2 * HD, SEQ), BF16),
        bias=((SEQ, L), F32),
        qt=((2, NI, T, HD, L), BF16),
        gate=((2, NI, T, 8, L), F32),
        p=((2, NI, T, SEQ, L), BF16),
        heads=((2, NI, T, HD, L), F32),
        ht=((2, NI, NQ, L), BF16),
        dq=((T, HD, L), BF16),
        dkv_acc=((SEQ, 2 * HD), F32),
        dkv_own=((NI, L, 2 * HD), F32),
        dkv_send=((NI, SEQ, 2 * HD), BF16),
        dkv_recv=((NI, X, L, 2 * HD), BF16),
        dksum_r=((NI, X, L, 2 * HD), BF16),
        dckv_send=((NI, SEQ, 2 * HD), BF16),
        dckv_recv=((NI, X, L, 2 * HD), BF16),
        dsum_r=((NI, X, L, 2 * HD), BF16),
        ckv_own=((NI, L, 2 * HD), BF16),
        g_big=((E, 2, D, HB), F32),
        g_qr=((2, NQ + RT, D), F32),
        g_o=((2, NQ, D), F32),
        g_kv=((2, D, 2 * HD), F32),
        small=((SR, D), F32),
        a_big=((2, X, D, HB), BF16),
        a_big_r=((2, X, D, HB), BF16),
        a_qo=((2, X, 2 * QB, D), BF16),
        a_qo_r=((2, X, 2 * QB, D), BF16),
        b_big=((X - 1, 2, D, HB), BF16),
        b_big_r=((X - 1, 2, D, HB), BF16),
        za_big=((2, HP, DB, HB), BF16),
        za_big_r=((2, HP, DB, HB), BF16),
        zb_big=((2, HP - 1, DB, HB), BF16),
        zb_big_r=((2, HP - 1, DB, HB), BF16),
        own_qo=((2, X, D, 2 * QB), F32),
        za_qo=((2, HP, X, DB, 2 * QB), BF16),
        za_qo_r=((2, HP, X, DB, 2 * QB), BF16),
        zb_qo=((2, HP - 1, X, DB, 2 * QB), BF16),
        zb_qo_r=((2, HP - 1, X, DB, 2 * QB), BF16),
        b_qo=((2, X - 1, DB, 2 * QB), BF16),
        b_qo_r=((2, X - 1, DB, 2 * QB), BF16),
        qo_own=((2, DB, 2 * QB), F32),
        kv_ar=((D, 2 * HD), F32),
        kv_sum=((D, 2 * HD), F32),
        za_kv=((HP, DB, 2 * HD), BF16),
        za_kv_r=((HP, DB, 2 * HD), BF16),
        zb_kv=((HP - 1, DB, 2 * HD), BF16),
        zb_kv_r=((HP - 1, DB, 2 * HD), BF16),
        kv_b=((DB, 2 * HD), BF16),
        kv_br=((X - 1, DB, 2 * HD), BF16),
        kv_fin=((DB, 2 * HD), F32),
        kv_sib=((DB, 2 * HD), F32),
        kv_sec=((DB, 2 * HD), F32),
        sm_ar=((SR, D), F32),
        sm_b=((SR, D), BF16),
        sm_br=((X - 1, SR, D), BF16),
        za_sm=((SR, D), BF16),
        za_sm_r=((DP - 1, SR, D), BF16),
        sm_fin=((SR, D), F32),
        sm_sec=((SR, D), F32),
        qo_fin=((DB, 2 * QB), F32),
        qo_sec=((DB, 2 * QB), F32),
    )
    sems = dict(
        q_s=(2, 2, E), q_r=(2, 2, E),
        sib_s=(2,), sib_r=(2,),
        wx_s=(2, X, NX), wx_r=(2, X, NX),
        wz_s=(2, X, NS), wz_r=(2, X, NS),
        wf_s=(2, X, NP), wf_r=(2, X, NP),
        kv_ss=(NI, E), kv_rs=(NI, E),
        ckv_s=(NI, E), ckv_r=(NI, E),
        dckv_s=(NI, X), dckv_r=(NI, X),
        dsum_ss=(NI, X), dsum_rs=(NI, X),
        dkv_s=(NI, X), dkv_r=(NI, X),
        dksum_ss=(NI, X), dksum_rs=(NI, X),
        a_s=(2, X), a_r=(2, X),
        b_s=(X - 1, 2, DP), b_r=(X - 1, 2, DP),
        zab_s=(2, HP), zab_r=(2, HP),
        zbb_s=(2, HP), zbb_r=(2, HP),
        aq_s=(2,), aq_r=(2,),
        zaq_s=(2,), zaq_r=(2,),
        zbq_s=(2, HP), zbq_r=(2, HP),
        bq_s=(2, X - 1), bq_r=(2, X - 1),
        ka_s=(1,), ka_r=(1,),
        kb_s=(X - 1,), kb_r=(X - 1,),
        zak_s=(1,), zak_r=(1,),
        zbk_s=(HP,), zbk_r=(HP,),
        kf_s=(3,), kf_r=(2,),
        sa_s=(1,), sa_r=(1,),
        sb_s=(X - 1,), sb_r=(X - 1,),
        zs_s=(DP - 1,), zs_r=(DP - 1,),
        sec_s=(2,), sec_r=(2,),
        ld=(len(ins) + 2,),
    )
    return ins, outs, bufs, sems


def make_kernel(dims):
    (NI, L, D, SEQ, T, NE, HD, HB, E, DP) = dims
    npd = NE // E
    QB = npd * HD
    NQ = NE * HD
    X = E // 2
    DB = D // DP
    HP = DP // 2
    scale = HD ** -0.5
    ins, outs, bufs, sems = make_plan(dims)
    names = [n if n in STAY else "in_" + n for n in ins]
    names += list(outs) + list(bufs) + list(sems) + fetched(ins)

    def kernel(*refs):
        r = SimpleNamespace(**dict(zip(names, refs)))
        sec = lax.axis_index("section")
        dpi = lax.axis_index("dp")
        me = lax.axis_index("expert")
        core = lax.rem(me, 2)
        xi = me // 2
        sib = xi * 2 + (1 - core)
        dec = sec == 1
        enc = sec == 0
        other = 1 - sec
        half = lax.rem(dpi, 2)
        mate = dpi + 1 - 2 * half
        row0 = pl.multiple_of(me * L, L)

        def to_expert(j):
            return (sec, dpi, j)

        def to_dp(j):
            return (sec, j, me)

        def to_section(j):
            return (other, dpi, j)

        def rcopy(src, dst, ssem, rsem, dev):
            return pltpu.make_async_remote_copy(
                src_ref=src, dst_ref=dst, send_sem=ssem, recv_sem=rsem, device_id=dev,
                device_id_type=MESH,
            )

        def chip(x):
            return x * 2 + core

        def q_copy(a, kind, block, to, slot):
            ref = r.wqr if kind == 0 else r.wo_all
            ref = ref.at[a, pl.ds(pl.multiple_of(block * QB, QB), QB)]
            return rcopy(ref, ref, r.q_s.at[a, kind, slot], r.q_r.at[a, kind, block], to_expert(to))

        def w_ref(kind, c):
            return (r.win_all if kind == 0 else r.wback_all).at[c]

        def w_piece(kind, c, p):
            rows = (D if kind == 0 else HB) // NP
            return w_ref(kind, c).at[pl.ds(pl.multiple_of(p * rows, rows), rows)]

        def sib_copy(kind, c):
            ref = w_ref(kind, c)
            return rcopy(ref, ref, r.sib_s.at[kind], r.sib_r.at[kind], to_expert(sib))

        def shared(q, parity):
            return NS * parity + q

        def over_x_at(q):
            return shared(q, half) if q < NS else NS + q

        def wx_copy(kind, c, q, to_x, frm_x):
            ref = w_piece(kind, c, over_x_at(q))
            return rcopy(
                ref, ref, r.wx_s.at[kind, to_x, q], r.wx_r.at[kind, frm_x, q],
                to_expert(chip(to_x)),
            )

        def wz_copy(kind, x, q, parity):
            ref = w_piece(kind, chip(x), shared(q, parity))
            return rcopy(ref, ref, r.wz_s.at[kind, x, q], r.wz_r.at[kind, x, q], to_dp(mate))

        def wf_copy(kind, c, x, p):
            ref = w_piece(kind, c, p)
            return rcopy(ref, ref, r.wf_s.at[kind, x, p], r.wf_r.at[kind, x, p], to_expert(sib))

        def rows_of(ref, i, j):
            return ref.at[i, pl.ds(pl.multiple_of(j * L, L), L)]

        def kv_copy(i, block, to, slot):
            ref = rows_of(r.kv_s, i, block)
            return rcopy(ref, ref, r.kv_ss.at[i, slot], r.kv_rs.at[i, block], to_expert(to))

        def ckv_copy(i, to):
            return rcopy(
                r.ckv_own.at[i], rows_of(r.kv_c, i, me), r.ckv_s.at[i, to], r.ckv_r.at[i, me],
                to_section(to),
            )

        def ckv_relay(i, block):
            ref = rows_of(r.kv_c, i, block)
            return rcopy(ref, ref, r.ckv_s.at[i, block], r.ckv_r.at[i, block], to_expert(sib))

        def ckv_gather(i):
            same = xpeers() + [xi]
            for x in same:
                ckv_relay(i, chip(x)).wait_recv()
                ckv_relay(i, chip(x)).start()
            for x in same:
                ckv_relay(i, x * 2 + 1 - core).wait_recv()

        def dsum_copy(i, x):
            at = x * 2 + 1 - core
            return rcopy(
                rows_of(r.dckv_send, i, at), r.dsum_r.at[i, x], r.dsum_ss.at[i, x],
                r.dsum_rs.at[i, x], to_expert(sib),
            )

        def dckv_copy(i, to_x, frm_x):
            return rcopy(
                rows_of(r.dckv_send, i, chip(to_x)), r.dckv_recv.at[i, frm_x],
                r.dckv_s.at[i, to_x], r.dckv_r.at[i, frm_x], to_section(chip(to_x)),
            )

        def dckv_out(i):
            order = xpeers() + [xi]
            for x in order:
                dsum_copy(i, x).start()
            for x in order:
                dsum_copy(i, x).wait_recv()
                at = pl.ds(pl.multiple_of(chip(x) * L, L), L)
                r.dckv_send[i, at] = (
                    r.dkv_acc[at] + r.dsum_r[i, x].astype(F32)
                ).astype(BF16)
                dckv_copy(i, x, xi).start()

        def dksum_copy(i, x):
            at = x * 2 + 1 - core
            return rcopy(
                rows_of(r.dkv_send, i, at), r.dksum_r.at[i, x], r.dksum_ss.at[i, x],
                r.dksum_rs.at[i, x], to_expert(sib),
            )

        def dkv_copy(i, to_x, frm_x):
            return rcopy(
                rows_of(r.dkv_send, i, chip(to_x)), r.dkv_recv.at[i, frm_x], r.dkv_s.at[i, to_x],
                r.dkv_r.at[i, frm_x], to_expert(chip(to_x)),
            )

        def dkv_out(i):
            for x in xpeers() + [xi]:
                dksum_copy(i, x).start()
            r.dkv_own[i] = r.dkv_acc[pl.ds(row0, L)]
            for x in xpeers():
                dksum_copy(i, x).wait_recv()
                at = pl.ds(pl.multiple_of(chip(x) * L, L), L)
                r.dkv_send[i, at] = (r.dkv_acc[at] + r.dksum_r[i, x].astype(F32)).astype(BF16)
                dkv_copy(i, x, xi).start()

        def dkv_in(i):
            dksum_copy(i, xi).wait_recv()
            total = r.dkv_own[i] + r.dksum_r[i, xi].astype(F32)
            for x in xpeers():
                dkv_copy(i, x, x).wait_recv()
                total = total + r.dkv_recv[i, x].astype(F32)
            return total

        def over_x(src, dst, ssem, rsem, o):
            return rcopy(src, dst, ssem, rsem, to_expert(chip(lax.rem(xi + o + 1, X))))

        def to_mate(src, dst, ssem, rsem):
            return rcopy(src, dst, ssem, rsem, to_dp(mate))

        def mates_at(k):
            return lax.rem(dpi // 2 + k, HP) * 2 + 1 - half

        def mine_at(k):
            return lax.rem(dpi // 2 + k, HP) * 2 + half

        def over_dp(src, dst, ssem, rsem, k):
            return rcopy(src, dst, ssem, rsem, to_dp(mine_at(k)))

        def over_sib(src, dst, ssem, rsem):
            return rcopy(src, dst, ssem, rsem, to_expert(sib))

        def a_copy(kind, x):
            return over_sib(
                r.a_big.at[kind, x], r.a_big_r.at[kind, x], r.a_s.at[kind, x], r.a_r.at[kind, x]
            )

        def block_rows(d):
            return pl.ds(pl.multiple_of(d * DB, DB), DB)

        def b_copy(kind, o, d):
            return over_x(
                r.b_big.at[o, kind, block_rows(d)], r.b_big_r.at[o, kind, block_rows(d)],
                r.b_s.at[o, kind, d], r.b_r.at[o, kind, d], o,
            )

        def zab_copy(kind, k):
            return to_mate(
                r.za_big.at[kind, k], r.za_big_r.at[kind, k], r.zab_s.at[kind, k],
                r.zab_r.at[kind, k],
            )

        def zbb_copy(kind, k):
            return over_dp(
                r.zb_big.at[kind, k - 1], r.zb_big_r.at[kind, k - 1], r.zbb_s.at[kind, k],
                r.zbb_r.at[kind, k], k,
            )

        def aq_copy(a):
            return over_sib(r.a_qo.at[a], r.a_qo_r.at[a], r.aq_s.at[a], r.aq_r.at[a])

        def zaq_copy(a):
            return to_mate(r.za_qo.at[a], r.za_qo_r.at[a], r.zaq_s.at[a], r.zaq_r.at[a])

        def zbq_copy(a, k):
            return over_dp(
                r.zb_qo.at[a, k - 1], r.zb_qo_r.at[a, k - 1], r.zbq_s.at[a, k], r.zbq_r.at[a, k], k
            )

        def bq_copy(a, o):
            return over_x(
                r.b_qo.at[a, o], r.b_qo_r.at[a, o], r.bq_s.at[a, o], r.bq_r.at[a, o], o
            )

        def ka_copy():
            return over_sib(r.g_kv.at[1 - core], r.kv_ar, r.ka_s.at[0], r.ka_r.at[0])

        def kb_copy(o):
            return over_x(r.kv_b, r.kv_br.at[o], r.kb_s.at[o], r.kb_r.at[o], o)

        def zak_copy():
            return to_mate(r.za_kv, r.za_kv_r, r.zak_s.at[0], r.zak_r.at[0])

        def zbk_copy(k):
            return over_dp(r.zb_kv.at[k - 1], r.zb_kv_r.at[k - 1], r.zbk_s.at[k], r.zbk_r.at[k], k)

        def kf_copy():
            return over_sib(r.kv_fin, r.kv_sib, r.kf_s.at[0], r.kf_r.at[0])

        def ks_copy(to_core):
            return rcopy(
                r.kv_fin, r.kv_sec, r.kf_s.at[1 + to_core], r.kf_r.at[1],
                to_section(xi * 2 + to_core),
            )

        def sa_copy():
            return over_sib(r.small, r.sm_ar, r.sa_s.at[0], r.sa_r.at[0])

        def sb_copy(o):
            return over_x(r.sm_b, r.sm_br.at[o], r.sb_s.at[o], r.sb_r.at[o], o)

        def zs_copy(o):
            return rcopy(
                r.za_sm, r.za_sm_r.at[o], r.zs_s.at[o], r.zs_r.at[o],
                to_dp(lax.rem(dpi + o + 1, DP)),
            )

        def sec_copy(kind):
            src, dst = ((r.qo_fin, r.qo_sec), (r.sm_fin, r.sm_sec))[kind]
            return rcopy(src, dst, r.sec_s.at[kind], r.sec_r.at[kind], to_section(me))

        def peers():
            return [lax.rem(me + o, E) for o in range(1, E)]

        def xpeers():
            return [lax.rem(xi + o, X) for o in range(1, X)]

        def dpeers():
            return [lax.rem(dpi + o, DP) for o in range(1, DP)]

        def load(name):
            src = getattr(r, "in_" + name)
            if name in PLACED:
                dst = w_ref(PLACED.index(name), me)
            else:
                dst = getattr(r, name)
            return pltpu.make_async_copy(src, dst, r.ld.at[ins.index(name)])

        def store(name):
            k = ("layer", "ig").index(name)
            src, dst = getattr(r, "o_" + name), getattr(r, "out_" + name)
            return pltpu.make_async_copy(src, dst, r.ld.at[len(ins) + k])

        soon = ["x", "ng", "nb", "wkv", "wq", "wo"]
        early = soon + ["win", "wback", "pairs", "routes_s"]
        late = [n for n in ins if n not in early and n not in STAY]
        for name in early + late:
            load(name).start()
        barrier = pltpu.get_barrier_semaphore()
        for j in peers():
            pl.semaphore_signal(barrier, inc=1, device_id=to_expert(j), device_id_type=MESH)
        for j in dpeers():
            pl.semaphore_signal(barrier, inc=1, device_id=to_dp(j), device_id_type=MESH)
        for j in range(E):
            pl.semaphore_signal(barrier, inc=1, device_id=to_section(j), device_id_type=MESH)

        def gather_send(copy):
            copy(me, sib, sib).start()
            for x in xpeers():
                copy(me, chip(x), chip(x)).start()

        def gather_relay(copy):
            for x in xpeers():
                copy(chip(x), sib, x * 2 + 1 - core).wait_recv()
                copy(chip(x), sib, x * 2 + 1 - core).start()

        def gather_take(copy):
            copy(sib, sib, sib).wait_recv()
            for x in xpeers():
                c = x * 2 + 1 - core
                copy(c, sib, c).wait_recv()

        def gather_sent(copy):
            copy(me, sib, sib).wait_send()
            for x in xpeers():
                copy(me, chip(x), chip(x)).wait_send()
                copy(chip(x), sib, x * 2 + 1 - core).wait_send()

        def q_of(a, kind):
            return lambda block, to, slot: q_copy(a, kind, block, to, slot)

        def kv_of(i):
            return lambda block, to, slot: kv_copy(i, block, to, slot)

        def norm_rows(x, gain, shift):
            return norm_stats(x)[0] * gain + shift

        def gain_of(which):
            if which == 1:
                return r.cg[...], r.cb[...]
            return r.ng[which // 2 : which // 2 + 1], r.nb[which // 2 : which // 2 + 1]

        def own_query_weights(a, q_ref, o_ref, wr_ref):
            for j in range(npd):
                at = pl.multiple_of(me * QB + j * HD, HD)
                r.wqr[a, pl.ds(at, HD)] = q_ref[j]
                r.wo_all[a, pl.ds(at, HD)] = o_ref[j]
            r.wr_pad[...] = jnp.zeros_like(r.wr_pad)
            r.wr_pad[:NE] = wr_ref[...].astype(F32)
            r.wqr[a, pl.ds(NQ, RT)] = r.wr_pad[...].astype(BF16)

        def first_norm(i):
            g, b = gain_of(0)
            n = norm_rows(r.x[i].astype(F32), g, b).astype(BF16)
            r.n[i, 0] = n
            r.kv_s[i, pl.ds(row0, L)] = nn(n, r.wkv[...]).astype(BF16)

        for name in soon:
            load(name).wait()
        own_query_weights(0, r.wq, r.wo, r.wr)
        first_norm(0)
        pl.semaphore_wait(barrier, (E - 1) + (DP - 1) + E)

        gather_send(q_of(0, 0))
        gather_send(kv_of(0))
        gather_send(q_of(0, 1))
        for name in PLACED:
            load(name).wait()
        for kind in (0, 1):
            sib_copy(kind, me).start()
        for part in (range(NS), range(NS, NX)):
            for kind in (0, 1):
                for q in part:
                    for x in xpeers():
                        wx_copy(kind, me, q, x, xi).start()

        def later_norms(i, _):
            first_norm(i)
            gather_send(kv_of(i))
            return 0

        lax.fori_loop(1, NI, later_norms, 0)
        for name in late + ["pairs", "routes_s"]:
            load(name).wait()
        own_query_weights(1, r.cq, r.co, r.cr)

        @pl.when(dec)
        def _():
            for kind in (0, 1):
                gather_send(q_of(1, kind))

        def weights_over_x(kind, q):
            for x in xpeers():
                wx_copy(kind, chip(x), q, x, x).wait_recv()
                if q < NS:
                    wz_copy(kind, x, q, half).start()
                wf_copy(kind, chip(x), x, over_x_at(q)).start()

        def weights_over_z(kind, q):
            for x in xpeers():
                wz_copy(kind, x, q, 1 - half).wait_recv()
                wf_copy(kind, chip(x), x, shared(q, 1 - half)).start()

        def weights_over_sib(kind):
            for x in xpeers():
                for p in range(NP):
                    wf_copy(kind, x * 2 + 1 - core, x, p).wait_recv()

        def weights_sent():
            for kind in (0, 1):
                sib_copy(kind, me).wait_send()
                for x in xpeers():
                    for q in range(NX):
                        wx_copy(kind, me, q, x, xi).wait_send()
                    for q in range(NS):
                        wz_copy(kind, x, q, half).wait_send()
                    for p in range(NP):
                        wf_copy(kind, chip(x), x, p).wait_send()

        zeros_h = jnp.zeros((HD, L), BF16)

        def set_bias(i, a):
            own = r.pairs[sec, i, :, pl.ds(row0, L)].astype(F32)
            if a == 0:
                keys = r.pairs[sec, i].astype(F32)
            else:
                keys = r.pairs[0, i].astype(F32)
            kc = jnp.broadcast_to(keys, (128, SEQ)).T
            if L > 128:
                kc = jnp.concatenate([kc] * (L // 128), 1)
            same = kc == own
            if a == 0:
                qpos = row0 + lax.broadcasted_iota(jnp.int32, (1, L), 1)
                limit = jnp.where(dec, qpos, SEQ)
                same = same & (lax.broadcasted_iota(jnp.int32, (SEQ, L), 0) <= limit)
            r.bias[...] = jnp.where(same, 0.0, -1e30)

        def route_rows(i, a):
            ref = r.routes_s if a == 0 else r.routes_c
            return [ref[i, k : k + 1, pl.ds(row0, L)] for k in range(T)]

        def pick(rows, route, size):
            total = jnp.zeros((size, L), F32)
            for e in range(NE):
                total = jnp.where(route == e, rows[e * size : (e + 1) * size], total)
            return total

        def project_queries(i, a):
            n = r.n[i, a]
            ql = nt(r.wqr[a], n)
            routes = route_rows(i, a)
            chosen = []
            for k in range(T):
                r.qt[a, i, k] = (pick(ql[:NQ], routes[k], HD).astype(BF16).astype(F32) * scale).astype(BF16)
                chosen.append(pick(ql[NQ : NQ + NE], routes[k], 1))
            top = chosen[0]
            for k in range(1, T):
                top = jnp.maximum(top, chosen[k])
            ex = [jnp.exp(c - top) for c in chosen]
            total = ex[0]
            for k in range(1, T):
                total = total + ex[k]
            for k in range(T):
                r.gate[a, i, k] = jnp.broadcast_to(ex[k] / total, (8, L))

        def attend(i, a, kv_ref, base):
            kv = kv_ref[i]
            r.kvt[a, i] = kv.astype(F32).T.astype(BF16)

            def one(k, _):
                q = jnp.concatenate([r.qt[a, i, k], zeros_h], 0)
                s = nn(kv, q) + r.bias[...]
                m = jnp.max(s, 0, keepdims=True)
                ex = jnp.exp(s - m)
                p = (ex * (1.0 / jnp.sum(ex, 0, keepdims=True))).astype(BF16)
                r.p[a, i, k] = p
                r.heads[a, i, k] = nn(r.kvt[a, i, HD:], p)
                return 0

            lax.fori_loop(0, T, one, 0, unroll=True)
            routes = route_rows(i, a)
            gated = [
                r.heads[a, i, k].astype(BF16).astype(F32) * r.gate[a, i, k, 0:1] for k in range(T)
            ]
            for e in range(NE):
                block = jnp.zeros((HD, L), F32)
                for k in range(T):
                    block = jnp.where(routes[k] == e, gated[k], block)
                r.ht[a, i, e * HD : (e + 1) * HD] = block.astype(BF16)
            return base + tn(r.ht[a, i], r.wo_all[a])

        def attend_back(i, a, kv_ref, dx, send_ref):
            dxb = dx.astype(BF16)
            routes = route_rows(i, a)
            r.g_o[a] += nn(r.ht[a, i], dxb)
            gt = nt(r.wo_all[a], dxb)
            dgates = []
            for k in range(T):
                g = pick(gt, routes[k], HD)
                dgates.append(
                    jnp.sum(r.heads[a, i, k].astype(BF16).astype(F32) * g, 0, keepdims=True)
                )
                r.dq[k] = (g * r.gate[a, i, k, 0:1]).astype(BF16)
            gates = [r.gate[a, i, k, 0:1] for k in range(T)]
            mid = gates[0] * dgates[0]
            for k in range(1, T):
                mid = mid + gates[k] * dgates[k]
            dchosen = [gates[k] * (dgates[k] - mid) for k in range(T)]
            kv = kv_ref[i]
            r.dkv_acc[...] = jnp.zeros_like(r.dkv_acc)

            def one(k, _):
                dheads = r.dq[k]
                p = r.p[a, i, k]
                dv = jnp.concatenate([zeros_h, dheads], 0)
                dp = nn(kv, dv)
                pf = p.astype(F32)
                delta = jnp.sum(dp * pf, 0, keepdims=True)
                ds = (pf * (dp - delta)).astype(BF16)
                qk = jnp.concatenate([r.qt[a, i, k], zeros_h], 0)
                r.dkv_acc[...] += nt(ds, qk) + nt(p, dv)
                r.dq[k] = (nn(r.kvt[a, i, :HD], ds) * scale).astype(BF16)
                return 0

            lax.fori_loop(0, T, one, 0, unroll=True)
            send_ref[i] = r.dkv_acc[...].astype(BF16)
            blocks = []
            for e in range(NE):
                block = jnp.zeros((HD, L), F32)
                for k in range(T):
                    block = jnp.where(routes[k] == e, r.dq[k].astype(F32), block)
                blocks.append(block)
            logit_rows = jnp.zeros((RT, L), F32)
            rows = lax.broadcasted_iota(jnp.int32, (RT, L), 0)
            for k in range(T):
                logit_rows = jnp.where(rows == routes[k], dchosen[k], logit_rows)
            dql = jnp.concatenate(blocks + [logit_rows], 0).astype(BF16)
            r.g_qr[a] += nn(dql, r.n[i, a])
            return tn(dql, r.wqr[a])

        def chunk_at(s):
            return lax.rem(xi + s // 2, X) * 2 + jnp.where(lax.rem(s, 2) == 0, core, 1 - core)

        def chunk_out(s):
            return lax.rem(xi + s // 2 + 1, X) * 2 + jnp.where(lax.rem(s, 2) == 0, 1 - core, core)

        def ffn_forward(i, low, high):
            n = r.n[i, 2]

            def one(s, _):
                c = chunk_at(s)
                act, slope = gelu_parts(nn(n, r.win_all[c]))
                act = act.astype(BF16)
                r.act[i, c] = act
                r.dh[i, c] = slope.astype(BF16)
                r.acc[...] += nn(act, r.wback_all[c])
                return 0

            lax.fori_loop(low, high, one, 0, unroll=True)

        def ffn_middle(i):
            n = r.n[i, 2]
            r.acc[...] = jnp.zeros_like(r.acc)

            def one(c, _):
                act, slope = gelu_parts(nn(n, r.win_all[c]))
                r.act[i, c] = act.astype(BF16)
                dh = (r.dh[i, c].astype(F32) * slope).astype(BF16)
                r.dh[i, c] = dh
                r.acc[...] += nt(dh, r.win_all[c])
                return 0

            lax.fori_loop(0, E, one, 0, unroll=True)
            return r.acc[...]

        def big_sib(kind):
            for o, x in enumerate(xpeers()):
                a_copy(kind, x).wait_recv()
                r.b_big[o, kind] = (
                    r.g_big[chip(x), kind] + r.a_big_r[kind, x].astype(F32)
                ).astype(BF16)

        def big_sib_own(kind):
            a_copy(kind, xi).wait_recv()
            r.g_big[me, kind] += r.a_big_r[kind, xi].astype(F32)

        def dp_at(s):
            return mates_at(s) if s < HP else mine_at((s - HP + 1) % HP)

        def big_send(kind, low, high):
            for s in range(low, high):
                for o in range(X - 1):
                    b_copy(kind, o, dp_at(s)).start()

        def big_over_x(kind, s):
            d = dp_at(s)
            total = r.g_big[me, kind, block_rows(d)]
            for o in range(X - 1):
                b_copy(kind, o, d).wait_recv()
                total = total + r.b_big_r[o, kind, block_rows(d)].astype(F32)
            if s < HP:
                r.za_big[kind, s] = total.astype(BF16)
                zab_copy(kind, s).start()
                return
            k = (s - HP + 1) % HP
            zab_copy(kind, k).wait_recv()
            total = total + r.za_big_r[kind, k].astype(F32)
            if k > 0:
                r.zb_big[kind, k - 1] = total.astype(BF16)
                zbb_copy(kind, k).start()
            else:
                r.g_big[me, kind, block_rows(d)] = total

        def big_end(kind, out):
            total = r.g_big[me, kind, block_rows(dpi)]
            for k in range(1, HP):
                zbb_copy(kind, k).wait_recv()
                total = total + r.zb_big_r[kind, k - 1].astype(F32)
            out[...] = total

        def hand_out(i, s, c, kind):
            @pl.when(jnp.logical_and(i == NI - 1, lax.rem(s, 2) == 0))
            def _():
                x = c // 2
                r.a_big[kind, x] = r.g_big[c, kind].astype(BF16)
                a_copy(kind, x).start()

        def ffn_back(i):
            dz = r.dz[i]
            dzt = dz.astype(F32).T.astype(BF16)
            nt_ = r.n[i, 2].astype(F32).T.astype(BF16)
            r.acc[...] = jnp.zeros_like(r.acc)

            def back(s, _):
                c = chunk_out(s)
                r.g_big[c, 1] += nn(dzt, r.act[i, c])
                hand_out(i, s, c, 1)
                return 0

            lax.fori_loop(0, E, back, 0, unroll=True)

            @pl.when(i == NI - 1)
            def _():
                big_sib(1)
                big_send(1, 0, HP)

            def inward(s, _):
                c = chunk_out(s)
                dh = (nt(dz, r.wback_all[c]) * r.dh[i, c].astype(F32)).astype(BF16)
                r.acc[...] += nt(dh, r.win_all[c])
                r.g_big[c, 0] += nn(nt_, dh)
                hand_out(i, s, c, 0)
                return 0

            lax.fori_loop(0, E, inward, 0, unroll=True)
            return r.acc[...]

        def ffn_weights(kind):
            for i in range(NI):
                r.turned[i] = (r.cot[i] if kind == 1 else r.n[i, 2]).astype(F32).T.astype(BF16)

            def one(s, _):
                c = chunk_out(s)
                total = jnp.zeros((D, HB), F32)
                for i in range(NI):
                    total += nn(r.turned[i], (r.act if kind == 1 else r.dh)[i, c])
                r.g_big[c, kind] = total
                hand_out(NI - 1, s, c, kind)
                return 0

            lax.fori_loop(0, E, one, 0)

        def ffn_output(i):
            r.acc[...] = r.x2[i]

            def one(c, _):
                r.acc[...] += nn(r.act[i, c], r.wback_all[c])
                return 0

            lax.fori_loop(0, E, one, 0, unroll=True)
            r.o_layer[i] = r.acc[...].astype(BF16)

        def add_small(which, dgain, dshift):
            r.small[2 * which : 2 * which + 1] += dgain
            r.small[2 * which + 1 : 2 * which + 2] += dshift

        def qo_rows(a, c):
            at = pl.ds(pl.multiple_of(c * QB, QB), QB)
            return jnp.concatenate([r.g_qr[a, at], r.g_o[a, at]], 0)

        def qo_send(a):
            for x in range(X):
                r.a_qo[a, x] = qo_rows(a, x * 2 + (1 - core)).astype(BF16)
            aq_copy(a).start()

        def qo_sib(a):
            aq_copy(a).wait_recv()
            for x in range(X):
                total = qo_rows(a, chip(x)) + r.a_qo_r[a, x].astype(F32)
                r.own_qo[a, x] = total.T
            for k in range(HP):
                r.za_qo[a, k] = r.own_qo[a, :, block_rows(mates_at(k))].astype(BF16)
            zaq_copy(a).start()

        def qo_mate(a):
            zaq_copy(a).wait_recv()
            for k in range(HP):
                total = r.own_qo[a, :, block_rows(mine_at(k))] + r.za_qo_r[a, k].astype(F32)
                if k > 0:
                    r.zb_qo[a, k - 1] = total.astype(BF16)
                    zbq_copy(a, k).start()
                else:
                    r.own_qo[a, :, block_rows(dpi)] = total

        def qo_over_dp(a):
            total = r.own_qo[a, :, block_rows(dpi)]
            for k in range(1, HP):
                zbq_copy(a, k).wait_recv()
                total = total + r.zb_qo_r[a, k - 1].astype(F32)
            r.own_qo[a, :, block_rows(dpi)] = total
            for o, x in enumerate(xpeers()):
                r.b_qo[a, o] = r.own_qo[a, x, block_rows(dpi)].astype(BF16)
                bq_copy(a, o).start()

        def qo_end(a):
            total = r.own_qo[a, xi, block_rows(dpi)]
            for o in range(X - 1):
                bq_copy(a, o).wait_recv()
                total = total + r.b_qo_r[a, o].astype(F32)
            return total

        kv_busy = enc | (core == 0)
        kv_sib_busy = enc | (core == 1)

        def kv_send():
            @pl.when(kv_sib_busy)
            def _():
                ka_copy().start()

        def kv_sib():
            @pl.when(kv_busy)
            def _():
                ka_copy().wait_recv()
                r.kv_sum[...] = r.g_kv[core] + r.kv_ar[...]
                for k in range(HP):
                    r.za_kv[k] = r.kv_sum[block_rows(mates_at(k))].astype(BF16)
                zak_copy().start()

        def kv_mate():
            @pl.when(kv_busy)
            def _():
                zak_copy().wait_recv()
                for k in range(HP):
                    total = r.kv_sum[block_rows(mine_at(k))] + r.za_kv_r[k].astype(F32)
                    if k > 0:
                        r.zb_kv[k - 1] = total.astype(BF16)
                        zbk_copy(k).start()
                    else:
                        r.kv_fin[...] = total

        def kv_over_dp():
            @pl.when(kv_busy)
            def _():
                total = r.kv_fin[...]
                for k in range(1, HP):
                    zbk_copy(k).wait_recv()
                    total = total + r.zb_kv_r[k - 1].astype(F32)
                r.kv_fin[...] = total
                r.kv_b[...] = total.astype(BF16)
                for o in range(X - 1):
                    kb_copy(o).start()

        def kv_over_x():
            @pl.when(kv_busy)
            def _():
                total = r.kv_fin[...]
                for o in range(X - 1):
                    kb_copy(o).wait_recv()
                    total = total + r.kv_br[o].astype(F32)
                r.kv_fin[...] = total
                kf_copy().start()

            @pl.when(enc & (core == 1))
            def _():
                ks_copy(0).start()
                ks_copy(1).start()

        def kv_end():
            @pl.when(kv_sib_busy)
            def _():
                kf_copy().wait_recv()

            @pl.when(dec)
            def _():
                ks_copy(core).wait_recv()
                r.o_kv[0] = jnp.where(core == 0, r.kv_fin[...], r.kv_sib[...])
                r.o_kv[1] = r.kv_sec[...]

            @pl.when(enc)
            def _():
                r.o_kv[0] = jnp.where(core == 0, r.kv_fin[...], r.kv_sib[...])
                r.o_kv[1] = jnp.where(core == 0, r.kv_sib[...], r.kv_fin[...])

        def small_sib():
            sa_copy().wait_recv()
            r.sm_fin[...] = r.small[...] + r.sm_ar[...]
            r.sm_b[...] = r.sm_fin[...].astype(BF16)
            for o in range(X - 1):
                sb_copy(o).start()

        def small_over_x():
            total = r.sm_fin[...]
            for o in range(X - 1):
                sb_copy(o).wait_recv()
                total = total + r.sm_br[o].astype(F32)
            r.sm_fin[...] = total
            r.za_sm[...] = total.astype(BF16)
            for o in range(DP - 1):
                zs_copy(o).start()

        def small_over_dp():
            total = r.sm_fin[...]
            for o in range(DP - 1):
                zs_copy(o).wait_recv()
                total = total + r.za_sm_r[o].astype(F32)
            r.sm_fin[...] = total

        def self_forward(i):
            x1 = attend(i, 0, r.kv_s, r.x[i].astype(F32))
            r.x1[i] = x1

            @pl.when(enc)
            def _():
                g, b = gain_of(2)
                r.n[i, 2] = norm_rows(r.x1[i], g, b).astype(BF16)

            @pl.when(dec)
            def _():
                g, b = gain_of(1)
                r.n[i, 1] = norm_rows(r.x1[i], g, b).astype(BF16)

        def encoded(i):
            mem = r.acc[...].astype(BF16)
            r.o_layer[i] = mem
            r.ckv_own[i] = nn(mem, r.ckv[...]).astype(BF16)
            for x in xpeers():
                ckv_copy(i, chip(x)).start()
            ckv_copy(i, me).start()

        gather_relay(q_of(0, 0))
        gather_take(q_of(0, 0))
        project_queries(0, 0)
        set_bias(0, 0)
        gather_relay(kv_of(0))
        gather_relay(q_of(0, 1))
        gather_take(kv_of(0))
        gather_take(q_of(0, 1))
        self_forward(0)
        for q in range(NS):
            weights_over_x(0, q)
        for kind in (0, 1):
            sib_copy(kind, sib).wait_recv()

        @pl.when(enc)
        def _():
            r.acc[...] = r.x1[0]
            ffn_forward(0, 0, 2)

        for q in range(NS):
            weights_over_x(1, q)
            weights_over_z(0, q)
        for q in range(NS, NX):
            weights_over_x(0, q)
        for q in range(NS):
            weights_over_z(1, q)
        for q in range(NS, NX):
            weights_over_x(1, q)
        @pl.when(enc)
        def _():
            ffn_forward(0, 2, 3)

        for kind in (0, 1):
            weights_over_sib(kind)

        @pl.when(enc)
        def _():
            ffn_forward(0, 3, E)
            encoded(0)

        def later_rows(i, _):
            project_queries(i, 0)
            set_bias(i, 0)
            gather_relay(kv_of(i))
            gather_take(kv_of(i))
            self_forward(i)

            @pl.when(enc)
            def _():
                r.acc[...] = r.x1[i]
                ffn_forward(i, 0, E)
                encoded(i)

            return 0

        lax.fori_loop(1, NI, later_rows, 0)

        @pl.when(enc)
        def _():
            store("layer").start()

        r.small[...] = jnp.zeros_like(r.small)
        r.g_qr[...] = jnp.zeros_like(r.g_qr)
        r.g_o[...] = jnp.zeros_like(r.g_o)
        r.g_kv[...] = jnp.zeros_like(r.g_kv)

        def zero_big(c, _):
            r.g_big[c] = jnp.zeros((2, D, HB), F32)
            return 0

        lax.fori_loop(0, E, zero_big, 0)

        @pl.when(dec)
        def _():
            for kind in (0, 1):
                gather_relay(q_of(1, kind))
            for kind in (0, 1):
                gather_take(q_of(1, kind))

            def ahead(i, _):
                project_queries(i, 1)
                dz = r.cot[i]

                def one(c, _):
                    r.dh[i, c] = nt(dz, r.wback_all[c]).astype(BF16)
                    return 0

                lax.fori_loop(0, E, one, 0)
                return 0

            lax.fori_loop(0, NI, ahead, 0)

            def middle(i, _):
                set_bias(i, 1)
                ckv_gather(i)
                x2 = attend(i, 1, r.kv_c, r.x1[i])
                r.x2[i] = x2
                g, b = gain_of(2)
                r.n[i, 2] = norm_rows(x2, g, b).astype(BF16)
                dn = ffn_middle(i)
                dx, dg, db = norm_back(r.x2[i], g, dn)
                add_small(2, dg, db)
                r.o_ig[i] = r.cot[i].astype(F32) + dx
                dn = attend_back(i, 1, r.kv_c, r.o_ig[i], r.dckv_send)
                dckv_out(i)
                g, b = gain_of(1)
                dx, dg, db = norm_back(r.x1[i], g, dn)
                add_small(1, dg, db)
                r.o_ig[i] += dx
                return 0

            lax.fori_loop(0, NI, middle, 0)

            qo_send(1)

        def backward(i, _):
            @pl.when(enc)
            def _():
                total = jnp.zeros((L, 2 * HD), F32)
                for x in range(X):
                    dckv_copy(i, x, x).wait_recv()
                    total = total + r.dckv_recv[i, x].astype(F32)
                dkv = total.astype(BF16)
                dmem = nt(dkv, r.ckv[...]).astype(BF16).astype(F32)
                dx = r.cot[i].astype(F32) + dmem
                r.o_ig[i] = dx
                r.dz[i] = dx.astype(BF16)
                dn = ffn_back(i)
                r.g_kv[1] += tn(r.o_layer[i], dkv)
                g, b = gain_of(2)
                dx, dg, db = norm_back(r.x1[i], g, dn)
                add_small(2, dg, db)
                r.o_ig[i] += dx

            first = i == 0
            last = i == NI - 1

            @pl.when(dec & first)
            def _():
                ffn_weights(1)

            r.dn[i] = attend_back(i, 0, r.kv_s, r.o_ig[i], r.dkv_send)

            @pl.when(dec & first)
            def _():
                big_sib(1)
                qo_sib(1)
                big_send(1, 0, HP)

            dkv_out(i)

            @pl.when(dec & first)
            def _():
                ffn_weights(0)
                big_send(1, HP, DP)
                big_sib(0)

            @pl.when(enc & last)
            def _():
                big_send(1, HP, DP)
                big_sib(0)

            @pl.when(dec & last)
            def _():
                big_send(0, 0, HP)

            @pl.when(last)
            def _():
                qo_send(0)

            return 0

        lax.fori_loop(0, NI, backward, 0)
        for kind in (1, 0):
            big_sib_own(kind)
        for s in range(HP):
            big_over_x(1, s)

        @pl.when(dec)
        def _():
            qo_mate(1)
            for s in range(HP, DP - 1):
                big_over_x(1, s)

        def first_layer(i, _):
            dkv = dkv_in(i).astype(BF16)
            r.g_kv[0] += tn(r.n[i, 0], dkv)
            dn = r.dn[i] + nt(dkv, r.wkv[...])
            g, b = gain_of(0)
            dx, dg, db = norm_back(r.x[i].astype(F32), g, dn)
            add_small(0, dg, db)
            r.o_ig[i] += dx
            return 0

        lax.fori_loop(0, NI, first_layer, 0)
        store("ig").start()

        for a in range(2):
            r.small[6 + a * NE : 6 + (a + 1) * NE] = r.g_qr[a, NQ : NQ + NE]
        sa_copy().start()
        kv_send()

        qo_sib(0)
        small_sib()
        kv_sib()

        @pl.when(enc)
        def _():
            big_send(0, 0, DP)
            for s in range(HP, DP - 1):
                big_over_x(1, s)

        @pl.when(dec)
        def _():
            big_send(0, HP, DP)

            def output(i, _):
                ffn_output(i)
                return 0

            lax.fori_loop(0, NI, output, 0)
            store("layer").start()

        small_over_x()
        big_over_x(1, DP - 1)
        for s in range(HP):
            big_over_x(0, s)
        kv_mate()
        qo_mate(0)

        @pl.when(dec)
        def _():
            qo_over_dp(1)

        for s in range(HP, DP - 1):
            big_over_x(0, s)
        small_over_dp()

        @pl.when(dec)
        def _():
            sec_copy(1).start()
            r.qo_fin[...] = qo_end(1)
            sec_copy(0).start()
            r.o_qo[1] = r.qo_fin[...]
            r.o_small[...] = r.sm_fin[...]

        kv_over_dp()
        qo_over_dp(0)
        big_over_x(0, DP - 1)
        kv_over_x()
        r.o_qo[0] = qo_end(0)
        big_end(1, r.o_back)
        big_end(0, r.o_in)
        kv_end()

        @pl.when(enc)
        def _():
            sec_copy(1).wait_recv()
            sec_copy(0).wait_recv()
            r.o_qo[1] = r.qo_sec[...]
            rows = lax.broadcasted_iota(jnp.int32, (SR, D), 0)
            theirs = ((rows >= 2) & (rows < 4)) | ((rows >= 6 + NE) & (rows < 6 + 2 * NE))
            r.o_small[...] = jnp.where(theirs, r.sm_sec[...], r.sm_fin[...])

        store("layer").wait()
        store("ig").wait()
        for kind in (0, 1):
            gather_sent(q_of(0, kind))
            for x in range(X):
                a_copy(kind, x).wait_send()
            for o in range(X - 1):
                for d in range(DP):
                    b_copy(kind, o, d).wait_send()
            for k in range(HP):
                zab_copy(kind, k).wait_send()
            for k in range(1, HP):
                zbb_copy(kind, k).wait_send()
        weights_sent()
        sa_copy().wait_send()
        for o in range(X - 1):
            sb_copy(o).wait_send()
        for o in range(DP - 1):
            zs_copy(o).wait_send()

        def qo_sent(a):
            aq_copy(a).wait_send()
            for o in range(X - 1):
                bq_copy(a, o).wait_send()
            zaq_copy(a).wait_send()
            for k in range(1, HP):
                zbq_copy(a, k).wait_send()

        qo_sent(0)

        @pl.when(dec)
        def _():
            for kind in (0, 1):
                gather_sent(q_of(1, kind))
                sec_copy(kind).wait_send()
            qo_sent(1)

        @pl.when(kv_sib_busy)
        def _():
            ka_copy().wait_send()

        @pl.when(kv_busy)
        def _():
            for o in range(X - 1):
                kb_copy(o).wait_send()
            zak_copy().wait_send()
            for k in range(1, HP):
                zbk_copy(k).wait_send()
            kf_copy().wait_send()

        @pl.when(enc & (core == 1))
        def _():
            ks_copy(0).wait_send()
            ks_copy(1).wait_send()

        def sent(i, _):
            gather_sent(kv_of(i))
            for x in xpeers():
                dkv_copy(i, x, xi).wait_send()
            for x in range(X):
                dksum_copy(i, x).wait_send()

            @pl.when(enc)
            def _():
                for x in range(X):
                    ckv_copy(i, chip(x)).wait_send()

            @pl.when(dec)
            def _():
                for x in range(X):
                    ckv_relay(i, chip(x)).wait_send()
                    dsum_copy(i, x).wait_send()
                    dckv_copy(i, x, xi).wait_send()

            return 0

        lax.fori_loop(0, NI, sent, 0)

    return kernel


def make_finish(E, NE, EB, QB):
    def kernel(
        layer, grads, w_in, w_back, qo, kv, small, o_layer, o_grads, o_gain, o_bias, o_kv, o_router,
        o_query, o_out, o_w_in, o_w_back, o_cgain, o_cbias, o_ckv, o_crouter, o_cquery, o_cout,
    ):
        me = lax.axis_index("expert")
        o_layer[...] = layer[...]
        o_grads[...] = grads[...]
        o_w_in[...] = w_in[...]
        o_w_back[...] = w_back[...].T
        for a, (q, o) in enumerate(((o_query, o_out), (o_cquery, o_cout))):
            both = qo[a].T
            q[...] = both[:QB]
            o[...] = both[QB:]
        for a, out in enumerate((o_kv, o_ckv)):
            total = kv[a, :EB]
            for j in range(1, E):
                total = jnp.where(me == j, kv[a, j * EB : (j + 1) * EB], total)
            out[...] = total
        off = (lax.axis_index("dp") * E + me) * EB
        part = small[:, pl.ds(pl.multiple_of(off // 128 * 128, 128), 128)]
        part = pltpu.roll(part, lax.rem(128 - lax.rem(off, 128), 128), 1)[:, :EB]
        o_gain[0] = jnp.concatenate([part[0:1], part[4:5]], 0)
        o_bias[0] = jnp.concatenate([part[1:2], part[5:6]], 0)
        o_cgain[...] = part[2:3]
        o_cbias[...] = part[3:4]
        o_router[...] = part[6 : 6 + NE]
        o_crouter[...] = part[6 + NE : 6 + 2 * NE]

    return kernel


def body(
    inputs, cotangents, pair_ids, self_routes, cross_routes, norm_gain, norm_bias, w_kv, w_router,
    w_query, w_out, w_in, w_back, cross_gain, cross_bias, cross_kv, cross_router, cross_query,
    cross_out,
):
    E = lax.axis_size("expert")
    DP = lax.axis_size("dp")
    _, MB, R, L, D = inputs.shape
    NI = MB * R
    SEQ = pair_ids.shape[-1]
    T = self_routes.shape[-1]
    NE = w_router.shape[-1]
    HD = w_query.shape[-1]
    HB = w_in.shape[-1]
    npd = NE // E
    QB = npd * HD
    dims = (NI, L, D, SEQ, T, NE, HD, HB, E, DP)
    ins, outs, bufs, sems = make_plan(dims)

    operands = [
        inputs.reshape(NI, L, D),
        cotangents.reshape(NI, L, D),
        pair_ids.reshape(2, NI, 1, SEQ),
        jnp.swapaxes(self_routes.reshape(NI, SEQ, T), 1, 2),
        jnp.swapaxes(cross_routes.reshape(NI, SEQ, T), 1, 2),
        norm_gain[0],
        norm_bias[0],
        w_kv[0],
        w_router[0].T,
        jnp.swapaxes(w_query[0], 1, 2),
        w_out[0],
        w_in[0],
        w_back[0],
        cross_gain[None],
        cross_bias[None],
        cross_kv,
        cross_router.T,
        jnp.swapaxes(cross_query, 1, 2),
        cross_out,
    ]
    vmem = pl.BlockSpec(memory_space=pltpu.VMEM)
    anywhere = pl.BlockSpec(memory_space=pl.ANY)
    res = pl.pallas_call(
        make_kernel(dims),
        out_shape=[jax.ShapeDtypeStruct(s, t) for s, t in outs.values()],
        in_specs=[vmem if n in STAY else anywhere for n in ins],
        out_specs=[anywhere if n[:4] == "out_" else vmem for n in outs],
        scratch_shapes=[pltpu.VMEM(s, t) for s, t in bufs.values()]
        + [pltpu.SemaphoreType.DMA(s) for s in sems.values()]
        + [pltpu.VMEM(o.shape, o.dtype) for n, o in zip(ins, operands) if n in fetched(ins)],
        compiler_params=pltpu.CompilerParams(
            collective_id=0, has_side_effects=True, vmem_limit_bytes=62 * 1024 * 1024
        ),
        name="layers",
    )(*operands)
    DB = D // DP
    EB = DB // E
    shapes = [
        ((NI, L, D), BF16),
        ((NI, L, D), F32),
        ((1, 2, EB), F32),
        ((1, 2, EB), F32),
        ((EB, 2 * HD), F32),
        ((NE, EB), F32),
        ((QB, DB), F32),
        ((QB, DB), F32),
        ((DB, HB), F32),
        ((HB, DB), F32),
        ((1, EB), F32),
        ((1, EB), F32),
        ((EB, 2 * HD), F32),
        ((NE, EB), F32),
        ((QB, DB), F32),
        ((QB, DB), F32),
    ]
    (
        layer, grads, gain, bias, kv, router, query, out, w_in_g, w_back_g, c_gain, c_bias, c_kv,
        c_router, c_query, c_out,
    ) = pl.pallas_call(
        make_finish(E, NE, EB, QB),
        out_shape=[jax.ShapeDtypeStruct(s, t) for s, t in shapes],
        in_specs=[vmem] * len(outs),
        out_specs=[vmem] * len(shapes),
        name="results",
    )(*res)

    def of_query(g):
        return jnp.swapaxes(g.reshape(npd, HD, DB), 1, 2)

    def of_out(g):
        return g.reshape(npd, HD, DB)

    return (
        layer.reshape(inputs.shape),
        grads.reshape(inputs.shape),
        gain,
        bias,
        kv[None],
        router.T[None],
        of_query(query)[None],
        of_out(out)[None],
        w_in_g[None],
        w_back_g[None],
        c_gain[0],
        c_bias[0],
        c_kv,
        c_router.T,
        of_query(c_query),
        of_out(c_out),
    )


def solution(mesh):
    placed = (
        P("section", None, "dp", "expert", None),
        P("section", None, "dp", "expert", None),
        P(None, None, "dp", None),
        P("section", None, "dp", None, None),
        P(None, "dp", None, None),
        P("section", None, None),
        P("section", None, None),
        P("section", None, None),
        P("section", None, None),
        P("section", "expert", None, None),
        P("section", "expert", None, None),
        P("section", None, "expert"),
        P("section", "expert", None),
        P(),
        P(),
        P(),
        P(),
        P("expert", None, None),
        P("expert", None, None),
    )
    return jax.shard_map(
        body,
        mesh=mesh,
        in_specs=placed,
        out_specs=(
            P("section", None, "dp", "expert", None),
            P("section", None, "dp", "expert", None),
            P("section", None, ("dp", "expert")),
            P("section", None, ("dp", "expert")),
            P("section", ("dp", "expert"), None),
            P("section", ("dp", "expert"), None),
            P("section", "expert", "dp", None),
            P("section", "expert", None, "dp"),
            P("section", "dp", "expert"),
            P("section", "expert", "dp"),
            P(("dp", "expert")),
            P(("dp", "expert")),
            P(("dp", "expert"), None),
            P(("dp", "expert"), None),
            P("expert", "dp", None),
            P("expert", None, "dp"),
        ),
        check_vma=False,
    )
```

```python
from types import SimpleNamespace

import jax
import jax.numpy as jnp
from jax import lax
from jax.experimental import pallas as pl
from jax.experimental.pallas import tpu as pltpu
from jax.sharding import PartitionSpec as P

F32 = jnp.float32
BF16 = jnp.bfloat16
MESH = pl.DeviceIdType.MESH
RT = 16
SR = 32
NP = 8
NS = 3
NX = NP - NS
NH = 2


def nn(a, b):
    return lax.dot_general(a, b, (((1,), (0,)), ((), ())), preferred_element_type=F32)


def nt(a, b):
    return lax.dot_general(a, b, (((1,), (1,)), ((), ())), preferred_element_type=F32)


def tn(a, b):
    return lax.dot_general(a, b, (((0,), (0,)), ((), ())), preferred_element_type=F32)


def gelu_parts(h):
    c = 0.7978845608028654
    a = c + (c * 0.044715) * (h * h)
    t = jnp.tanh(h * a)
    half = 0.5 + 0.5 * t
    act = h * half
    return act, half + act * ((1.0 - t) * (3.0 * a - 2.0 * c))


def norm_stats(x):
    centred = x - jnp.mean(x, -1, keepdims=True)
    r = lax.rsqrt(jnp.mean(centred * centred, -1, keepdims=True) + 1e-05)
    return centred * r, r


def norm_back(x, gain, grad):
    xhat, r = norm_stats(x)
    gg = grad * gain
    m1 = jnp.mean(gg, -1, keepdims=True)
    m2 = jnp.mean(gg * xhat, -1, keepdims=True)
    return (
        r * (gg - m1 - xhat * m2),
        jnp.sum(grad * xhat, 0, keepdims=True),
        jnp.sum(grad, 0, keepdims=True),
    )


INS = [
    "x", "cot", "pairs", "routes_s", "routes_c", "ng", "nb", "wkv", "wr", "wq", "wo", "win",
    "wback", "cg", "cb", "ckv", "cr", "cq", "co",
]
STAY = ("wr", "cr")
PLACED = ("win", "wback")


def fetched(ins):
    return [n for n in ins if n not in STAY + PLACED]


def make_plan(dims):
    (NI, L, D, SEQ, T, NE, HD, HB, E, DP) = dims
    npd = NE // E
    QB = npd * HD
    NQ = NE * HD
    X = E // 2
    DB = D // DP
    HP = DP // 2
    ins = INS
    outs = dict(
        out_layer=((NI, L, D), BF16),
        out_ig=((NI, L, D), F32),
        o_in=((DB, HB), F32),
        o_back=((DB, HB), F32),
        o_qo=((2, DB, 2 * QB), F32),
        o_kv=((2, DB, 2 * HD), F32),
        o_small=((SR, 128), F32),
    )
    bufs = dict(
        o_layer=((NI, L, D), BF16),
        o_ig=((NI, L, D), F32),
        win_all=((E, D, HB), BF16),
        wback_all=((E, HB, D), BF16),
        wqr=((2, NQ + RT, D), BF16),
        wo_all=((2, NQ, D), BF16),
        wr_pad=((RT, D), F32),
        x1=((NI, L, D), F32),
        x2=((NI, L, D), F32),
        n=((NI, 3, L, D), BF16),
        dz=((NI, L, D), BF16),
        acc=((L, D), F32),
        dn=((NI, L, D), F32),
        act=((NI, E, L, HB), BF16),
        turned=((NI, D, L), BF16),
        dh=((NI, E, L, HB), BF16),
        kv_s=((NI, SEQ, 2 * HD), BF16),
        kv_c=((NI, SEQ, 2 * HD), BF16),
        kvt=((2, NI, 2 * HD, SEQ), BF16),
        bias=((SEQ, L), F32),
        qt=((2, NI, T, HD, L), BF16),
        gate=((2, NI, T, 8, L), F32),
        inv=((2, NI, T, 8, L), F32),
        p=((2, NI, T, SEQ, L), BF16),
        heads=((2, NI, T, HD, L), F32),
        ht=((2, NI, NQ, L), BF16),
        dq=((T, HD, L), BF16),
        dkv_acc=((SEQ, 2 * HD), F32),
        dkv_own=((NI, L, 2 * HD), F32),
        dkv_send=((NI, SEQ, 2 * HD), BF16),
        dkv_recv=((NI, X, L, 2 * HD), BF16),
        dksum_r=((NI, X, L, 2 * HD), BF16),
        dckv_send=((NI, SEQ, 2 * HD), BF16),
        dckv_recv=((NI, X, L, 2 * HD), BF16),
        dsum_r=((NI, X, L, 2 * HD), BF16),
        ckv_own=((NI, L, 2 * HD), BF16),
        g_big=((E, 2, D, HB), F32),
        g_qr=((2, NQ + RT, D), F32),
        g_o=((2, NQ, D), F32),
        g_kv=((2, D, 2 * HD), F32),
        small=((SR, D), F32),
        a_big=((2, X, D, HB), BF16),
        a_big_r=((2, X, D, HB), BF16),
        a_qo=((2, X, 2 * QB, D), BF16),
        a_qo_r=((2, X, 2 * QB, D), BF16),
        b_big=((X - 1, 2, D, HB), BF16),
        b_big_r=((X - 1, 2, D, HB), BF16),
        za_big=((2, HP, DB, HB), BF16),
        za_big_r=((2, HP, DB, HB), BF16),
        zb_big=((2, HP - 1, DB, HB), BF16),
        zb_big_r=((2, HP - 1, DB, HB), BF16),
        b_qo=((2, X - 1, 2 * QB, D), BF16),
        b_qo_r=((2, X - 1, 2 * QB, D), BF16),
        own_qo=((D, 2 * QB), F32),
        c_qo=((2, DP - 1, DB, 2 * QB), BF16),
        c_qo_r=((2, DP - 1, DB, 2 * QB), BF16),
        qo_own=((2, DB, 2 * QB), F32),
        kv_ar=((D, 2 * HD), F32),
        kv_sum=((D, 2 * HD), F32),
        c_kv=((DP - 1, DB, 2 * HD), BF16),
        c_kv_r=((DP - 1, DB, 2 * HD), BF16),
        kv_b=((DB, 2 * HD), BF16),
        kv_br=((X - 1, DB, 2 * HD), BF16),
        kv_fin=((DB, 2 * HD), F32),
        kv_sib=((DB, 2 * HD), F32),
        kv_sec=((DB, 2 * HD), F32),
        sm_ar=((SR, D), F32),
        sm_b=((SR, D), BF16),
        sm_br=((X - 1, SR, D), BF16),
        za_sm=((SR, D), BF16),
        za_sm_r=((DP - 1, SR, 128), BF16),
        sm_own=((SR, 128), F32),
        sm_fin=((SR, D), F32),
        sm_sec=((SR, 128), F32),
        qo_fin=((DB, 2 * QB), F32),
        qo_sec=((DB, 2 * QB), F32),
    )
    sems = dict(
        q_s=(2, 2, E), q_r=(2, 2, E),
        sib_s=(2,), sib_r=(2,),
        wx_s=(2, X, NX), wx_r=(2, X, NX),
        wz_s=(2, X, NS), wz_r=(2, X, NS),
        wf_s=(2, X, NP), wf_r=(2, X, NP),
        kv_ss=(NI, E), kv_rs=(NI, E),
        ckv_s=(NI, E), ckv_r=(NI, E),
        dckv_s=(NI, X), dckv_r=(NI, X),
        dsum_ss=(NI, X), dsum_rs=(NI, X),
        dkv_s=(NI, X), dkv_r=(NI, X),
        dksum_ss=(NI, X), dksum_rs=(NI, X),
        a_s=(2, X), a_r=(2, X),
        b_s=(X - 1, 2, DP, NH), b_r=(X - 1, 2, DP, NH),
        zab_s=(2, HP, NH), zab_r=(2, HP, NH),
        zbb_s=(2, HP, NH), zbb_r=(2, HP, NH),
        aq_s=(2,), aq_r=(2,),
        cq_s=(2, DP - 1), cq_r=(2, DP - 1),
        bq_s=(2, X - 1), bq_r=(2, X - 1),
        ka_s=(1,), ka_r=(1,),
        kb_s=(X - 1,), kb_r=(X - 1,),
        ck_s=(DP - 1,), ck_r=(DP - 1,),
        kf_s=(3,), kf_r=(2,),
        sa_s=(1,), sa_r=(1,),
        sb_s=(X - 1,), sb_r=(X - 1,),
        zs_s=(DP - 1,), zs_r=(DP - 1,),
        sec_s=(2,), sec_r=(2,),
        ld=(len(ins) + 2,),
    )
    return ins, outs, bufs, sems


def make_kernel(dims):
    (NI, L, D, SEQ, T, NE, HD, HB, E, DP) = dims
    npd = NE // E
    QB = npd * HD
    NQ = NE * HD
    X = E // 2
    DB = D // DP
    HP = DP // 2
    scale = HD ** -0.5
    ins, outs, bufs, sems = make_plan(dims)
    names = [n if n in STAY else "in_" + n for n in ins]
    names += list(outs) + list(bufs) + list(sems) + fetched(ins)

    def kernel(*refs):
        r = SimpleNamespace(**dict(zip(names, refs)))
        sec = lax.axis_index("section")
        dpi = lax.axis_index("dp")
        me = lax.axis_index("expert")
        core = lax.rem(me, 2)
        xi = me // 2
        sib = xi * 2 + (1 - core)
        dec = sec == 1
        enc = sec == 0
        other = 1 - sec
        half = lax.rem(dpi, 2)
        mate = dpi + 1 - 2 * half
        row0 = pl.multiple_of(me * L, L)

        def to_expert(j):
            return (sec, dpi, j)

        def to_dp(j):
            return (sec, j, me)

        def to_section(j):
            return (other, dpi, j)

        def rcopy(src, dst, ssem, rsem, dev):
            return pltpu.make_async_remote_copy(
                src_ref=src, dst_ref=dst, send_sem=ssem, recv_sem=rsem, device_id=dev,
                device_id_type=MESH,
            )

        def chip(x):
            return x * 2 + core

        def q_copy(a, kind, block, to, slot):
            ref = r.wqr if kind == 0 else r.wo_all
            ref = ref.at[a, pl.ds(pl.multiple_of(block * QB, QB), QB)]
            return rcopy(ref, ref, r.q_s.at[a, kind, slot], r.q_r.at[a, kind, block], to_expert(to))

        def w_ref(kind, c):
            return (r.win_all if kind == 0 else r.wback_all).at[c]

        def w_piece(kind, c, p):
            rows = (D if kind == 0 else HB) // NP
            return w_ref(kind, c).at[pl.ds(pl.multiple_of(p * rows, rows), rows)]

        def sib_copy(kind, c):
            ref = w_ref(kind, c)
            return rcopy(ref, ref, r.sib_s.at[kind], r.sib_r.at[kind], to_expert(sib))

        def shared(q, parity):
            return NS * parity + q

        def over_x_at(q):
            return shared(q, half) if q < NS else NS + q

        def wx_copy(kind, c, q, to_x, frm_x):
            ref = w_piece(kind, c, over_x_at(q))
            return rcopy(
                ref, ref, r.wx_s.at[kind, to_x, q], r.wx_r.at[kind, frm_x, q],
                to_expert(chip(to_x)),
            )

        def wz_copy(kind, x, q, parity):
            ref = w_piece(kind, chip(x), shared(q, parity))
            return rcopy(ref, ref, r.wz_s.at[kind, x, q], r.wz_r.at[kind, x, q], to_dp(mate))

        def wf_copy(kind, c, x, p):
            ref = w_piece(kind, c, p)
            return rcopy(ref, ref, r.wf_s.at[kind, x, p], r.wf_r.at[kind, x, p], to_expert(sib))

        def rows_of(ref, i, j):
            return ref.at[i, pl.ds(pl.multiple_of(j * L, L), L)]

        def kv_copy(i, block, to, slot):
            ref = rows_of(r.kv_s, i, block)
            return rcopy(ref, ref, r.kv_ss.at[i, slot], r.kv_rs.at[i, block], to_expert(to))

        def ckv_copy(i, to):
            return rcopy(
                r.ckv_own.at[i], rows_of(r.kv_c, i, me), r.ckv_s.at[i, to], r.ckv_r.at[i, me],
                to_section(to),
            )

        def ckv_relay(i, block):
            ref = rows_of(r.kv_c, i, block)
            return rcopy(ref, ref, r.ckv_s.at[i, block], r.ckv_r.at[i, block], to_expert(sib))

        def ckv_gather(i):
            same = xpeers() + [xi]
            for x in same:
                ckv_relay(i, chip(x)).wait_recv()
                ckv_relay(i, chip(x)).start()
            for x in same:
                ckv_relay(i, x * 2 + 1 - core).wait_recv()

        def dsum_copy(i, x):
            at = x * 2 + 1 - core
            return rcopy(
                rows_of(r.dckv_send, i, at), r.dsum_r.at[i, x], r.dsum_ss.at[i, x],
                r.dsum_rs.at[i, x], to_expert(sib),
            )

        def dckv_copy(i, to_x, frm_x):
            return rcopy(
                rows_of(r.dckv_send, i, chip(to_x)), r.dckv_recv.at[i, frm_x],
                r.dckv_s.at[i, to_x], r.dckv_r.at[i, frm_x], to_section(chip(to_x)),
            )

        def dckv_out(i):
            order = xpeers() + [xi]
            for x in order:
                dsum_copy(i, x).start()
            for x in order:
                dsum_copy(i, x).wait_recv()
                at = pl.ds(pl.multiple_of(chip(x) * L, L), L)
                r.dckv_send[i, at] = (
                    r.dkv_acc[at] + r.dsum_r[i, x].astype(F32)
                ).astype(BF16)
                dckv_copy(i, x, xi).start()

        def dksum_copy(i, x):
            at = x * 2 + 1 - core
            return rcopy(
                rows_of(r.dkv_send, i, at), r.dksum_r.at[i, x], r.dksum_ss.at[i, x],
                r.dksum_rs.at[i, x], to_expert(sib),
            )

        def dkv_copy(i, to_x, frm_x):
            return rcopy(
                rows_of(r.dkv_send, i, chip(to_x)), r.dkv_recv.at[i, frm_x], r.dkv_s.at[i, to_x],
                r.dkv_r.at[i, frm_x], to_expert(chip(to_x)),
            )

        def dkv_out(i):
            for x in xpeers() + [xi]:
                dksum_copy(i, x).start()
            r.dkv_own[i] = r.dkv_acc[pl.ds(row0, L)]
            for x in xpeers():
                dksum_copy(i, x).wait_recv()
                at = pl.ds(pl.multiple_of(chip(x) * L, L), L)
                r.dkv_send[i, at] = (r.dkv_acc[at] + r.dksum_r[i, x].astype(F32)).astype(BF16)
                dkv_copy(i, x, xi).start()

        def dkv_in(i):
            dksum_copy(i, xi).wait_recv()
            total = r.dkv_own[i] + r.dksum_r[i, xi].astype(F32)
            for x in xpeers():
                dkv_copy(i, x, x).wait_recv()
                total = total + r.dkv_recv[i, x].astype(F32)
            return total

        def over_x(src, dst, ssem, rsem, o):
            return rcopy(src, dst, ssem, rsem, to_expert(chip(lax.rem(xi + o + 1, X))))

        def to_mate(src, dst, ssem, rsem):
            return rcopy(src, dst, ssem, rsem, to_dp(mate))

        def mates_at(k):
            return lax.rem(dpi // 2 + k, HP) * 2 + 1 - half

        def mine_at(k):
            return lax.rem(dpi // 2 + k, HP) * 2 + half

        def over_dp(src, dst, ssem, rsem, k):
            return rcopy(src, dst, ssem, rsem, to_dp(mine_at(k)))

        def over_sib(src, dst, ssem, rsem):
            return rcopy(src, dst, ssem, rsem, to_expert(sib))

        def a_copy(kind, x):
            return over_sib(
                r.a_big.at[kind, x], r.a_big_r.at[kind, x], r.a_s.at[kind, x], r.a_r.at[kind, x]
            )

        def block_rows(d):
            return pl.ds(pl.multiple_of(d * DB, DB), DB)

        HB_ROWS = DB // NH

        def part_rows(d, h):
            return pl.ds(pl.multiple_of(d * DB + h * HB_ROWS, HB_ROWS), HB_ROWS)

        def sub_rows(h):
            return pl.ds(h * HB_ROWS, HB_ROWS)

        def b_copy(kind, o, d, h):
            return over_x(
                r.b_big.at[o, kind, part_rows(d, h)], r.b_big_r.at[o, kind, part_rows(d, h)],
                r.b_s.at[o, kind, d, h], r.b_r.at[o, kind, d, h], o,
            )

        def zab_copy(kind, k, h):
            return to_mate(
                r.za_big.at[kind, k, sub_rows(h)], r.za_big_r.at[kind, k, sub_rows(h)],
                r.zab_s.at[kind, k, h], r.zab_r.at[kind, k, h],
            )

        def zbb_copy(kind, k, h):
            return over_dp(
                r.zb_big.at[kind, k - 1, sub_rows(h)], r.zb_big_r.at[kind, k - 1, sub_rows(h)],
                r.zbb_s.at[kind, k, h], r.zbb_r.at[kind, k, h], k,
            )

        def aq_copy(a):
            return over_sib(r.a_qo.at[a], r.a_qo_r.at[a], r.aq_s.at[a], r.aq_r.at[a])

        def around(src, dst, ssem, rsem, o):
            return rcopy(src, dst, ssem, rsem, to_dp(lax.rem(dpi + o + 1, DP)))

        def cq_copy(a, o):
            return around(
                r.c_qo.at[a, o], r.c_qo_r.at[a, o], r.cq_s.at[a, o], r.cq_r.at[a, o], o
            )

        def bq_copy(a, o):
            return over_x(
                r.b_qo.at[a, o], r.b_qo_r.at[a, o], r.bq_s.at[a, o], r.bq_r.at[a, o], o
            )

        def ka_copy():
            return over_sib(r.g_kv.at[1 - core], r.kv_ar, r.ka_s.at[0], r.ka_r.at[0])

        def kb_copy(o):
            return over_x(r.kv_b, r.kv_br.at[o], r.kb_s.at[o], r.kb_r.at[o], o)

        def ck_copy(o):
            return around(r.c_kv.at[o], r.c_kv_r.at[o], r.ck_s.at[o], r.ck_r.at[o], o)

        def kf_copy():
            return over_sib(r.kv_fin, r.kv_sib, r.kf_s.at[0], r.kf_r.at[0])

        def ks_copy(to_core):
            return rcopy(
                r.kv_fin, r.kv_sec, r.kf_s.at[1 + to_core], r.kf_r.at[1],
                to_section(xi * 2 + to_core),
            )

        def sa_copy():
            return over_sib(r.small, r.sm_ar, r.sa_s.at[0], r.sa_r.at[0])

        def sb_copy(o):
            return over_x(r.sm_b, r.sm_br.at[o], r.sb_s.at[o], r.sb_r.at[o], o)

        def lanes(d):
            return pl.ds(pl.multiple_of(d * DB // 128 * 128, 128), 128)

        def zs_copy(o):
            src = r.za_sm.at[:, lanes(lax.rem(dpi + o + 1, DP))]
            return around(src, r.za_sm_r.at[o], r.zs_s.at[o], r.zs_r.at[o], o)

        def sec_copy(kind):
            src, dst = ((r.qo_fin, r.qo_sec), (r.sm_own, r.sm_sec))[kind]
            return rcopy(src, dst, r.sec_s.at[kind], r.sec_r.at[kind], to_section(me))

        def peers():
            return [lax.rem(me + o, E) for o in range(1, E)]

        def xpeers():
            return [lax.rem(xi + o, X) for o in range(1, X)]

        def dpeers():
            return [lax.rem(dpi + o, DP) for o in range(1, DP)]

        def load(name):
            src = getattr(r, "in_" + name)
            if name in PLACED:
                dst = w_ref(PLACED.index(name), me)
            else:
                dst = getattr(r, name)
            return pltpu.make_async_copy(src, dst, r.ld.at[ins.index(name)])

        def store(name):
            k = ("layer", "ig").index(name)
            src, dst = getattr(r, "o_" + name), getattr(r, "out_" + name)
            return pltpu.make_async_copy(src, dst, r.ld.at[len(ins) + k])

        soon = ["x", "ng", "nb", "wkv", "wq", "wo"]
        early = soon + ["win", "wback", "pairs", "routes_s"]
        late = [n for n in ins if n not in early and n not in STAY]
        for name in early + late:
            load(name).start()
        barrier = pltpu.get_barrier_semaphore()
        for j in peers():
            pl.semaphore_signal(barrier, inc=1, device_id=to_expert(j), device_id_type=MESH)
        for j in dpeers():
            pl.semaphore_signal(barrier, inc=1, device_id=to_dp(j), device_id_type=MESH)
        for j in range(E):
            pl.semaphore_signal(barrier, inc=1, device_id=to_section(j), device_id_type=MESH)

        def gather_send(copy):
            copy(me, sib, sib).start()
            for x in xpeers():
                copy(me, chip(x), chip(x)).start()

        def gather_relay(copy):
            for x in xpeers():
                copy(chip(x), sib, x * 2 + 1 - core).wait_recv()
                copy(chip(x), sib, x * 2 + 1 - core).start()

        def gather_take(copy):
            copy(sib, sib, sib).wait_recv()
            for x in xpeers():
                c = x * 2 + 1 - core
                copy(c, sib, c).wait_recv()

        def gather_sent(copy):
            copy(me, sib, sib).wait_send()
            for x in xpeers():
                copy(me, chip(x), chip(x)).wait_send()
                copy(chip(x), sib, x * 2 + 1 - core).wait_send()

        def q_of(a, kind):
            return lambda block, to, slot: q_copy(a, kind, block, to, slot)

        def kv_of(i):
            return lambda block, to, slot: kv_copy(i, block, to, slot)

        def norm_rows(x, gain, shift):
            return norm_stats(x)[0] * gain + shift

        def gain_of(which):
            if which == 1:
                return r.cg[...], r.cb[...]
            return r.ng[which // 2 : which // 2 + 1], r.nb[which // 2 : which // 2 + 1]

        def own_query_weights(a, q_ref, o_ref, wr_ref):
            for j in range(npd):
                at = pl.multiple_of(me * QB + j * HD, HD)
                r.wqr[a, pl.ds(at, HD)] = q_ref[j]
                r.wo_all[a, pl.ds(at, HD)] = o_ref[j]
            r.wr_pad[...] = jnp.zeros_like(r.wr_pad)
            r.wr_pad[:NE] = wr_ref[...].astype(F32)
            r.wqr[a, pl.ds(NQ, RT)] = r.wr_pad[...].astype(BF16)

        def first_norm(i):
            g, b = gain_of(0)
            n = norm_rows(r.x[i].astype(F32), g, b).astype(BF16)
            r.n[i, 0] = n
            r.kv_s[i, pl.ds(row0, L)] = nn(n, r.wkv[...]).astype(BF16)

        for name in soon:
            load(name).wait()
        own_query_weights(0, r.wq, r.wo, r.wr)
        first_norm(0)
        pl.semaphore_wait(barrier, (E - 1) + (DP - 1) + E)

        gather_send(q_of(0, 0))
        gather_send(kv_of(0))
        gather_send(q_of(0, 1))
        def later_norms(i, _):
            first_norm(i)
            gather_send(kv_of(i))
            return 0

        @pl.when(dec)
        def _():
            lax.fori_loop(1, NI, later_norms, 0)

        for name in PLACED:
            load(name).wait()
        for kind in (0, 1):
            sib_copy(kind, me).start()
        for part in (range(NS), range(NS, NX)):
            for kind in (0, 1):
                for q in part:
                    for x in xpeers():
                        wx_copy(kind, me, q, x, xi).start()

        @pl.when(enc)
        def _():
            lax.fori_loop(1, NI, later_norms, 0)

        for name in late + ["pairs", "routes_s"]:
            load(name).wait()
        own_query_weights(1, r.cq, r.co, r.cr)

        @pl.when(dec)
        def _():
            for kind in (0, 1):
                gather_send(q_of(1, kind))

        def weights_over_x(kind, q):
            for x in xpeers():
                wx_copy(kind, chip(x), q, x, x).wait_recv()
                if q < NS:
                    wz_copy(kind, x, q, half).start()
                wf_copy(kind, chip(x), x, over_x_at(q)).start()

        def weights_over_z(kind, q):
            for x in xpeers():
                wz_copy(kind, x, q, 1 - half).wait_recv()
                wf_copy(kind, chip(x), x, shared(q, 1 - half)).start()

        def weights_over_sib(kind):
            for x in xpeers():
                for p in range(NP):
                    wf_copy(kind, x * 2 + 1 - core, x, p).wait_recv()

        def weights_sent():
            for kind in (0, 1):
                sib_copy(kind, me).wait_send()
                for x in xpeers():
                    for q in range(NX):
                        wx_copy(kind, me, q, x, xi).wait_send()
                    for q in range(NS):
                        wz_copy(kind, x, q, half).wait_send()
                    for p in range(NP):
                        wf_copy(kind, chip(x), x, p).wait_send()

        zeros_h = jnp.zeros((HD, L), BF16)

        def set_bias(i, a):
            own = r.pairs[sec, i, :, pl.ds(row0, L)].astype(F32)
            if a == 0:
                keys = r.pairs[sec, i].astype(F32)
            else:
                keys = r.pairs[0, i].astype(F32)
            kc = jnp.broadcast_to(keys, (128, SEQ)).T
            if L > 128:
                kc = jnp.concatenate([kc] * (L // 128), 1)
            same = kc == own
            if a == 0:
                qpos = row0 + lax.broadcasted_iota(jnp.int32, (1, L), 1)
                limit = jnp.where(dec, qpos, SEQ)
                same = same & (lax.broadcasted_iota(jnp.int32, (SEQ, L), 0) <= limit)
            r.bias[...] = jnp.where(same, 0.0, -1e30)

        def route_rows(i, a):
            ref = r.routes_s if a == 0 else r.routes_c
            return [ref[i, k : k + 1, pl.ds(row0, L)] for k in range(T)]

        def pick(rows, route, size):
            total = jnp.zeros((size, L), F32)
            for e in range(NE):
                total = jnp.where(route == e, rows[e * size : (e + 1) * size], total)
            return total

        def project_queries(i, a):
            n = r.n[i, a]
            ql = nt(r.wqr[a], n)
            routes = route_rows(i, a)
            chosen = []
            for k in range(T):
                r.qt[a, i, k] = (pick(ql[:NQ], routes[k], HD).astype(BF16).astype(F32) * scale).astype(BF16)
                chosen.append(pick(ql[NQ : NQ + NE], routes[k], 1))
            top = chosen[0]
            for k in range(1, T):
                top = jnp.maximum(top, chosen[k])
            ex = [jnp.exp(c - top) for c in chosen]
            total = ex[0]
            for k in range(1, T):
                total = total + ex[k]
            for k in range(T):
                r.gate[a, i, k] = jnp.broadcast_to(ex[k] / total, (8, L))

        def attend(i, a, kv_ref, base):
            kv = kv_ref[i]
            r.kvt[a, i] = kv.astype(F32).T.astype(BF16)

            def one(k, _):
                q = jnp.concatenate([r.qt[a, i, k], zeros_h], 0)
                s = nn(kv, q) + r.bias[...]
                m = jnp.max(s, 0, keepdims=True)
                ex = jnp.exp(s - m)
                inv = 1.0 / jnp.sum(ex, 0, keepdims=True)
                p = ex.astype(BF16)
                r.p[a, i, k] = p
                r.inv[a, i, k] = jnp.broadcast_to(inv, (8, L))
                r.heads[a, i, k] = nn(r.kvt[a, i, HD:], p) * inv
                return 0

            lax.fori_loop(0, T, one, 0, unroll=True)
            routes = route_rows(i, a)
            gated = [
                r.heads[a, i, k].astype(BF16).astype(F32) * r.gate[a, i, k, 0:1] for k in range(T)
            ]
            for e in range(NE):
                block = jnp.zeros((HD, L), F32)
                for k in range(T):
                    block = jnp.where(routes[k] == e, gated[k], block)
                r.ht[a, i, e * HD : (e + 1) * HD] = block.astype(BF16)
            return base + tn(r.ht[a, i], r.wo_all[a])

        def attend_back(i, a, kv_ref, dx, send_ref):
            dxb = dx.astype(BF16)
            routes = route_rows(i, a)
            r.g_o[a] += nn(r.ht[a, i], dxb)
            gt = nt(r.wo_all[a], dxb)
            dgates = []
            for k in range(T):
                g = pick(gt, routes[k], HD)
                dgates.append(
                    jnp.sum(r.heads[a, i, k].astype(BF16).astype(F32) * g, 0, keepdims=True)
                )
                r.dq[k] = (g * r.gate[a, i, k, 0:1]).astype(BF16)
            gates = [r.gate[a, i, k, 0:1] for k in range(T)]
            mid = gates[0] * dgates[0]
            for k in range(1, T):
                mid = mid + gates[k] * dgates[k]
            dchosen = [gates[k] * (dgates[k] - mid) for k in range(T)]
            kv = kv_ref[i]
            r.dkv_acc[...] = jnp.zeros_like(r.dkv_acc)

            def one(k, _):
                dheads = (r.dq[k].astype(F32) * r.inv[a, i, k, 0:1]).astype(BF16)
                p = r.p[a, i, k]
                dv = jnp.concatenate([zeros_h, dheads], 0)
                delta = jnp.sum(dheads.astype(F32) * r.heads[a, i, k], 0, keepdims=True)
                ds = (p.astype(F32) * (nn(kv, dv) - delta)).astype(BF16)
                qk = jnp.concatenate([r.qt[a, i, k], zeros_h], 0)
                r.dkv_acc[...] += nt(ds, qk) + nt(p, dv)
                r.dq[k] = (nn(r.kvt[a, i, :HD], ds) * scale).astype(BF16)
                return 0

            lax.fori_loop(0, T, one, 0, unroll=True)
            send_ref[i] = r.dkv_acc[...].astype(BF16)
            blocks = []
            for e in range(NE):
                block = jnp.zeros((HD, L), F32)
                for k in range(T):
                    block = jnp.where(routes[k] == e, r.dq[k].astype(F32), block)
                blocks.append(block)
            logit_rows = jnp.zeros((RT, L), F32)
            rows = lax.broadcasted_iota(jnp.int32, (RT, L), 0)
            for k in range(T):
                logit_rows = jnp.where(rows == routes[k], dchosen[k], logit_rows)
            dql = jnp.concatenate(blocks + [logit_rows], 0).astype(BF16)
            r.g_qr[a] += nn(dql, r.n[i, a])
            return tn(dql, r.wqr[a])

        def chunk_at(s):
            return lax.rem(xi + s // 2, X) * 2 + jnp.where(lax.rem(s, 2) == 0, core, 1 - core)

        def chunk_out(s):
            return lax.rem(xi + s // 2 + 1, X) * 2 + jnp.where(lax.rem(s, 2) == 0, 1 - core, core)

        def ffn_forward(i, low, high):
            n = r.n[i, 2]

            def one(s, _):
                c = chunk_at(s)
                act, slope = gelu_parts(nn(n, r.win_all[c]))
                act = act.astype(BF16)
                r.act[i, c] = act
                r.dh[i, c] = slope.astype(BF16)
                r.acc[...] += nn(act, r.wback_all[c])
                return 0

            lax.fori_loop(low, high, one, 0, unroll=True)

        def ffn_middle(i):
            n = r.n[i, 2]
            r.acc[...] = jnp.zeros_like(r.acc)

            def one(c, _):
                act, slope = gelu_parts(nn(n, r.win_all[c]))
                r.act[i, c] = act.astype(BF16)
                dh = (r.dh[i, c].astype(F32) * slope).astype(BF16)
                r.dh[i, c] = dh
                r.acc[...] += nt(dh, r.win_all[c])
                return 0

            lax.fori_loop(0, E, one, 0, unroll=True)
            return r.acc[...]

        def big_sib(kind):
            for o, x in enumerate(xpeers()):
                a_copy(kind, x).wait_recv()
                r.b_big[o, kind] = (
                    r.g_big[chip(x), kind] + r.a_big_r[kind, x].astype(F32)
                ).astype(BF16)

        def big_sib_own(kind):
            a_copy(kind, xi).wait_recv()
            r.g_big[me, kind] += r.a_big_r[kind, xi].astype(F32)

        def dp_at(s):
            return mates_at(s) if s < HP else mine_at((s - HP + 1) % HP)

        def big_send(kind, low, high):
            for s in range(low, high):
                for h in range(NH):
                    for o in range(X - 1):
                        b_copy(kind, o, dp_at(s), h).start()

        def big_over_x(kind, s):
            for h in range(NH):
                big_part_over_x(kind, s, h)

        def big_part_over_x(kind, s, h):
            d = dp_at(s)
            total = r.g_big[me, kind, part_rows(d, h)]
            for o in range(X - 1):
                b_copy(kind, o, d, h).wait_recv()
                total = total + r.b_big_r[o, kind, part_rows(d, h)].astype(F32)
            if s < HP:
                r.za_big[kind, s, sub_rows(h)] = total.astype(BF16)
                zab_copy(kind, s, h).start()
                return
            k = (s - HP + 1) % HP
            zab_copy(kind, k, h).wait_recv()
            total = total + r.za_big_r[kind, k, sub_rows(h)].astype(F32)
            if k > 0:
                r.zb_big[kind, k - 1, sub_rows(h)] = total.astype(BF16)
                zbb_copy(kind, k, h).start()
            else:
                r.g_big[me, kind, part_rows(d, h)] = total

        def big_end(kind, out):
            for h in range(NH):
                total = r.g_big[me, kind, part_rows(dpi, h)]
                for k in range(1, HP):
                    zbb_copy(kind, k, h).wait_recv()
                    total = total + r.zb_big_r[kind, k - 1, sub_rows(h)].astype(F32)
                out[sub_rows(h)] = total

        def hand_out(i, s, c, kind):
            @pl.when(jnp.logical_and(i == NI - 1, lax.rem(s, 2) == 0))
            def _():
                x = c // 2
                r.a_big[kind, x] = r.g_big[c, kind].astype(BF16)
                a_copy(kind, x).start()

        def ffn_back(i):
            dz = r.dz[i]
            dzt = dz.astype(F32).T.astype(BF16)
            nt_ = r.n[i, 2].astype(F32).T.astype(BF16)
            r.acc[...] = jnp.zeros_like(r.acc)

            def back(s, _):
                c = chunk_out(s)
                r.g_big[c, 1] += nn(dzt, r.act[i, c])
                hand_out(i, s, c, 1)
                return 0

            lax.fori_loop(0, E, back, 0, unroll=True)

            @pl.when(i == NI - 1)
            def _():
                big_sib(1)
                big_send(1, 0, HP)

            def inward(s, _):
                c = chunk_out(s)
                dh = (nt(dz, r.wback_all[c]) * r.dh[i, c].astype(F32)).astype(BF16)
                r.acc[...] += nt(dh, r.win_all[c])
                r.g_big[c, 0] += nn(nt_, dh)
                hand_out(i, s, c, 0)
                return 0

            lax.fori_loop(0, E, inward, 0, unroll=True)
            return r.acc[...]

        def ffn_weights(kind):
            for i in range(NI):
                r.turned[i] = (r.cot[i] if kind == 1 else r.n[i, 2]).astype(F32).T.astype(BF16)

            def one(s, _):
                c = chunk_out(s)
                total = jnp.zeros((D, HB), F32)
                for i in range(NI):
                    total += nn(r.turned[i], (r.act if kind == 1 else r.dh)[i, c])
                r.g_big[c, kind] = total
                hand_out(NI - 1, s, c, kind)
                return 0

            lax.fori_loop(0, E, one, 0)

        def ffn_output(i):
            r.acc[...] = r.x2[i]

            def one(c, _):
                r.acc[...] += nn(r.act[i, c], r.wback_all[c])
                return 0

            lax.fori_loop(0, E, one, 0, unroll=True)
            r.o_layer[i] = r.acc[...].astype(BF16)

        def add_small(which, dgain, dshift):
            r.small[2 * which : 2 * which + 1] += dgain
            r.small[2 * which + 1 : 2 * which + 2] += dshift

        def qo_rows(a, c):
            at = pl.ds(pl.multiple_of(c * QB, QB), QB)
            return jnp.concatenate([r.g_qr[a, at], r.g_o[a, at]], 0)

        def qo_send(a):
            for x in range(X):
                r.a_qo[a, x] = qo_rows(a, x * 2 + (1 - core)).astype(BF16)
            aq_copy(a).start()

        def rows_around(o):
            return block_rows(lax.rem(dpi + o + 1, DP))

        def qo_sib(a):
            aq_copy(a).wait_recv()
            for o, x in enumerate(xpeers()):
                r.b_qo[a, o] = (qo_rows(a, chip(x)) + r.a_qo_r[a, x].astype(F32)).astype(BF16)
                bq_copy(a, o).start()

        def qo_over_x(a):
            total = qo_rows(a, me) + r.a_qo_r[a, xi].astype(F32)
            for o in range(X - 1):
                bq_copy(a, o).wait_recv()
                total = total + r.b_qo_r[a, o].astype(F32)
            r.own_qo[...] = total.T
            for o in range(DP - 1):
                r.c_qo[a, o] = r.own_qo[rows_around(o)].astype(BF16)
                cq_copy(a, o).start()
            r.qo_own[a] = r.own_qo[block_rows(dpi)]

        def qo_end(a):
            total = r.qo_own[a]
            for o in range(DP - 1):
                cq_copy(a, o).wait_recv()
                total = total + r.c_qo_r[a, o].astype(F32)
            return total

        kv_busy = enc | (core == 0)
        kv_sib_busy = enc | (core == 1)

        def kv_send():
            @pl.when(kv_sib_busy)
            def _():
                ka_copy().start()

        def kv_sib():
            @pl.when(kv_busy)
            def _():
                ka_copy().wait_recv()
                r.kv_sum[...] = r.g_kv[core] + r.kv_ar[...]
                for o in range(DP - 1):
                    r.c_kv[o] = r.kv_sum[rows_around(o)].astype(BF16)
                    ck_copy(o).start()

        def kv_over_dp():
            @pl.when(kv_busy)
            def _():
                total = r.kv_sum[block_rows(dpi)]
                for o in range(DP - 1):
                    ck_copy(o).wait_recv()
                    total = total + r.c_kv_r[o].astype(F32)
                r.kv_fin[...] = total
                r.kv_b[...] = total.astype(BF16)
                for o in range(X - 1):
                    kb_copy(o).start()

        def kv_over_x():
            @pl.when(kv_busy)
            def _():
                total = r.kv_fin[...]
                for o in range(X - 1):
                    kb_copy(o).wait_recv()
                    total = total + r.kv_br[o].astype(F32)
                r.kv_fin[...] = total
                kf_copy().start()

            @pl.when(enc & (core == 1))
            def _():
                ks_copy(0).start()
                ks_copy(1).start()

        def kv_end():
            @pl.when(kv_sib_busy)
            def _():
                kf_copy().wait_recv()

            @pl.when(dec)
            def _():
                ks_copy(core).wait_recv()
                r.o_kv[0] = jnp.where(core == 0, r.kv_fin[...], r.kv_sib[...])
                r.o_kv[1] = r.kv_sec[...]

            @pl.when(enc)
            def _():
                r.o_kv[0] = jnp.where(core == 0, r.kv_fin[...], r.kv_sib[...])
                r.o_kv[1] = jnp.where(core == 0, r.kv_sib[...], r.kv_fin[...])

        def small_sib():
            sa_copy().wait_recv()
            r.sm_fin[...] = r.small[...] + r.sm_ar[...]
            r.sm_b[...] = r.sm_fin[...].astype(BF16)
            for o in range(X - 1):
                sb_copy(o).start()

        def small_over_x():
            total = r.sm_fin[...]
            for o in range(X - 1):
                sb_copy(o).wait_recv()
                total = total + r.sm_br[o].astype(F32)
            r.sm_fin[...] = total
            r.za_sm[...] = total.astype(BF16)
            for o in range(DP - 1):
                zs_copy(o).start()

        def small_over_dp():
            total = r.sm_fin[:, lanes(dpi)]
            for o in range(DP - 1):
                zs_copy(o).wait_recv()
                total = total + r.za_sm_r[o].astype(F32)
            r.sm_own[...] = total

        def self_forward(i):
            x1 = attend(i, 0, r.kv_s, r.x[i].astype(F32))
            r.x1[i] = x1

            @pl.when(enc)
            def _():
                g, b = gain_of(2)
                r.n[i, 2] = norm_rows(r.x1[i], g, b).astype(BF16)

            @pl.when(dec)
            def _():
                g, b = gain_of(1)
                r.n[i, 1] = norm_rows(r.x1[i], g, b).astype(BF16)

        def encoded(i):
            mem = r.acc[...].astype(BF16)
            r.o_layer[i] = mem
            r.ckv_own[i] = nn(mem, r.ckv[...]).astype(BF16)
            for x in xpeers():
                ckv_copy(i, chip(x)).start()
            ckv_copy(i, me).start()

        gather_relay(q_of(0, 0))
        gather_take(q_of(0, 0))
        project_queries(0, 0)
        set_bias(0, 0)
        gather_relay(kv_of(0))
        gather_relay(q_of(0, 1))
        gather_take(kv_of(0))
        gather_take(q_of(0, 1))
        self_forward(0)
        def later_rows(i, _):
            project_queries(i, 0)
            set_bias(i, 0)
            gather_relay(kv_of(i))
            gather_take(kv_of(i))
            self_forward(i)
            return 0

        @pl.when(dec)
        def _():
            lax.fori_loop(1, NI, later_rows, 0)

        for q in range(NS):
            weights_over_x(0, q)
        for kind in (0, 1):
            sib_copy(kind, sib).wait_recv()

        @pl.when(enc)
        def _():
            r.acc[...] = r.x1[0]
            ffn_forward(0, 0, 2)

        for q in range(NS):
            weights_over_x(1, q)
            weights_over_z(0, q)
        for q in range(NS, NX):
            weights_over_x(0, q)
        for q in range(NS):
            weights_over_z(1, q)
        for q in range(NS, NX):
            weights_over_x(1, q)
        @pl.when(enc)
        def _():
            ffn_forward(0, 2, 3)

        for kind in (0, 1):
            weights_over_sib(kind)

        @pl.when(enc)
        def _():
            ffn_forward(0, 3, E)
            encoded(0)

        @pl.when(enc)
        def _():
            def later_outputs(i, _):
                later_rows(i, 0)
                r.acc[...] = r.x1[i]
                ffn_forward(i, 0, E)
                encoded(i)
                return 0

            lax.fori_loop(1, NI, later_outputs, 0)
            store("layer").start()

        r.small[...] = jnp.zeros_like(r.small)
        r.g_qr[...] = jnp.zeros_like(r.g_qr)
        r.g_o[...] = jnp.zeros_like(r.g_o)
        r.g_kv[...] = jnp.zeros_like(r.g_kv)

        def zero_big(c, _):
            r.g_big[c] = jnp.zeros((2, D, HB), F32)
            return 0

        lax.fori_loop(0, E, zero_big, 0)

        @pl.when(dec)
        def _():
            for kind in (0, 1):
                gather_relay(q_of(1, kind))
            for kind in (0, 1):
                gather_take(q_of(1, kind))

            def ahead(i, _):
                project_queries(i, 1)
                dz = r.cot[i]

                def one(c, _):
                    r.dh[i, c] = nt(dz, r.wback_all[c]).astype(BF16)
                    return 0

                lax.fori_loop(0, E, one, 0)
                return 0

            lax.fori_loop(0, NI, ahead, 0)

            def middle(i, _):
                set_bias(i, 1)
                ckv_gather(i)
                x2 = attend(i, 1, r.kv_c, r.x1[i])
                r.x2[i] = x2
                g, b = gain_of(2)
                r.n[i, 2] = norm_rows(x2, g, b).astype(BF16)
                dn = ffn_middle(i)
                dx, dg, db = norm_back(r.x2[i], g, dn)
                add_small(2, dg, db)
                r.o_ig[i] = r.cot[i].astype(F32) + dx
                dn = attend_back(i, 1, r.kv_c, r.o_ig[i], r.dckv_send)
                dckv_out(i)
                g, b = gain_of(1)
                dx, dg, db = norm_back(r.x1[i], g, dn)
                add_small(1, dg, db)
                r.o_ig[i] += dx
                return 0

            lax.fori_loop(0, NI, middle, 0)

            qo_send(1)

        def backward(i, _):
            @pl.when(enc)
            def _():
                total = jnp.zeros((L, 2 * HD), F32)
                for x in range(X):
                    dckv_copy(i, x, x).wait_recv()
                    total = total + r.dckv_recv[i, x].astype(F32)
                dkv = total.astype(BF16)
                dmem = nt(dkv, r.ckv[...]).astype(BF16).astype(F32)
                dx = r.cot[i].astype(F32) + dmem
                r.o_ig[i] = dx
                r.dz[i] = dx.astype(BF16)
                dn = ffn_back(i)
                r.g_kv[1] += tn(r.o_layer[i], dkv)
                g, b = gain_of(2)
                dx, dg, db = norm_back(r.x1[i], g, dn)
                add_small(2, dg, db)
                r.o_ig[i] += dx

            first = i == 0
            last = i == NI - 1

            @pl.when(dec & first)
            def _():
                ffn_weights(1)

            r.dn[i] = attend_back(i, 0, r.kv_s, r.o_ig[i], r.dkv_send)

            @pl.when(dec & first)
            def _():
                big_sib(1)
                qo_sib(1)
                big_send(1, 0, HP)

            dkv_out(i)

            @pl.when(dec & first)
            def _():
                ffn_weights(0)

            @pl.when(last)
            def _():
                big_sib(0)
                big_send(0, 0, HP)
                qo_send(0)

            return 0

        lax.fori_loop(0, NI, backward, 0)
        for kind in (1, 0):
            big_sib_own(kind)
        for s in range(HP):
            big_over_x(1, s)

        @pl.when(dec)
        def _():
            qo_over_x(1)

        def first_layer(i, _):
            dkv = dkv_in(i).astype(BF16)
            r.g_kv[0] += tn(r.n[i, 0], dkv)
            dn = r.dn[i] + nt(dkv, r.wkv[...])
            g, b = gain_of(0)
            dx, dg, db = norm_back(r.x[i].astype(F32), g, dn)
            add_small(0, dg, db)
            r.o_ig[i] += dx
            return 0

        lax.fori_loop(0, NI, first_layer, 0)
        store("ig").start()

        for a in range(2):
            r.small[6 + a * NE : 6 + (a + 1) * NE] = r.g_qr[a, NQ : NQ + NE]
        sa_copy().start()
        kv_send()

        qo_sib(0)
        small_sib()
        kv_sib()

        for s in range(HP, DP):
            for kind in (1, 0):
                big_send(kind, s, s + 1)
        for s in range(HP):
            big_over_x(0, s)

        @pl.when(dec)
        def _():
            def output(i, _):
                ffn_output(i)
                return 0

            lax.fori_loop(0, NI, output, 0)
            store("layer").start()

        small_over_x()

        qo_over_x(0)
        for s in range(HP, DP - 1):
            for kind in (1, 0):
                big_over_x(kind, s)
        kv_over_dp()
        small_over_dp()

        @pl.when(dec)
        def _():
            sec_copy(1).start()
            r.qo_fin[...] = qo_end(1)
            sec_copy(0).start()
            r.o_qo[1] = r.qo_fin[...]
            r.o_small[...] = r.sm_own[...]

        for kind in (1, 0):
            big_over_x(kind, DP - 1)
        kv_over_x()
        r.o_qo[0] = qo_end(0)
        big_end(1, r.o_back)
        big_end(0, r.o_in)
        kv_end()

        @pl.when(enc)
        def _():
            sec_copy(1).wait_recv()
            sec_copy(0).wait_recv()
            r.o_qo[1] = r.qo_sec[...]
            rows = lax.broadcasted_iota(jnp.int32, (SR, 128), 0)
            theirs = ((rows >= 2) & (rows < 4)) | ((rows >= 6 + NE) & (rows < 6 + 2 * NE))
            r.o_small[...] = jnp.where(theirs, r.sm_sec[...], r.sm_own[...])

        store("layer").wait()
        store("ig").wait()
        for kind in (0, 1):
            gather_sent(q_of(0, kind))
            for x in range(X):
                a_copy(kind, x).wait_send()
            for h in range(NH):
                for o in range(X - 1):
                    for d in range(DP):
                        b_copy(kind, o, d, h).wait_send()
                for k in range(HP):
                    zab_copy(kind, k, h).wait_send()
                for k in range(1, HP):
                    zbb_copy(kind, k, h).wait_send()
        weights_sent()
        sa_copy().wait_send()
        for o in range(X - 1):
            sb_copy(o).wait_send()
        for o in range(DP - 1):
            zs_copy(o).wait_send()

        def qo_sent(a):
            aq_copy(a).wait_send()
            for o in range(X - 1):
                bq_copy(a, o).wait_send()
            for o in range(DP - 1):
                cq_copy(a, o).wait_send()

        qo_sent(0)

        @pl.when(dec)
        def _():
            for kind in (0, 1):
                gather_sent(q_of(1, kind))
                sec_copy(kind).wait_send()
            qo_sent(1)

        @pl.when(kv_sib_busy)
        def _():
            ka_copy().wait_send()

        @pl.when(kv_busy)
        def _():
            for o in range(X - 1):
                kb_copy(o).wait_send()
            for o in range(DP - 1):
                ck_copy(o).wait_send()
            kf_copy().wait_send()

        @pl.when(enc & (core == 1))
        def _():
            ks_copy(0).wait_send()
            ks_copy(1).wait_send()

        def sent(i, _):
            gather_sent(kv_of(i))
            for x in xpeers():
                dkv_copy(i, x, xi).wait_send()
            for x in range(X):
                dksum_copy(i, x).wait_send()

            @pl.when(enc)
            def _():
                for x in range(X):
                    ckv_copy(i, chip(x)).wait_send()

            @pl.when(dec)
            def _():
                for x in range(X):
                    ckv_relay(i, chip(x)).wait_send()
                    dsum_copy(i, x).wait_send()
                    dckv_copy(i, x, xi).wait_send()

            return 0

        lax.fori_loop(0, NI, sent, 0)

    return kernel


def make_finish(E, NE, EB, QB):
    def kernel(
        layer, grads, w_in, w_back, qo, kv, small, o_layer, o_grads, o_gain, o_bias, o_kv, o_router,
        o_query, o_out, o_w_in, o_w_back, o_cgain, o_cbias, o_ckv, o_crouter, o_cquery, o_cout,
    ):
        me = lax.axis_index("expert")
        o_layer[...] = layer[...]
        o_grads[...] = grads[...]
        o_w_in[...] = w_in[...]
        o_w_back[...] = w_back[...].T
        for a, (q, o) in enumerate(((o_query, o_out), (o_cquery, o_cout))):
            both = qo[a].T
            q[...] = both[:QB]
            o[...] = both[QB:]
        for a, out in enumerate((o_kv, o_ckv)):
            total = kv[a, :EB]
            for j in range(1, E):
                total = jnp.where(me == j, kv[a, j * EB : (j + 1) * EB], total)
            out[...] = total
        off = (lax.axis_index("dp") * E + me) * EB
        part = pltpu.roll(small[...], lax.rem(128 - lax.rem(off, 128), 128), 1)[:, :EB]
        o_gain[0] = jnp.concatenate([part[0:1], part[4:5]], 0)
        o_bias[0] = jnp.concatenate([part[1:2], part[5:6]], 0)
        o_cgain[...] = part[2:3]
        o_cbias[...] = part[3:4]
        o_router[...] = part[6 : 6 + NE]
        o_crouter[...] = part[6 + NE : 6 + 2 * NE]

    return kernel


def body(
    inputs, cotangents, pair_ids, self_routes, cross_routes, norm_gain, norm_bias, w_kv, w_router,
    w_query, w_out, w_in, w_back, cross_gain, cross_bias, cross_kv, cross_router, cross_query,
    cross_out,
):
    E = lax.axis_size("expert")
    DP = lax.axis_size("dp")
    _, MB, R, L, D = inputs.shape
    NI = MB * R
    SEQ = pair_ids.shape[-1]
    T = self_routes.shape[-1]
    NE = w_router.shape[-1]
    HD = w_query.shape[-1]
    HB = w_in.shape[-1]
    npd = NE // E
    QB = npd * HD
    dims = (NI, L, D, SEQ, T, NE, HD, HB, E, DP)
    ins, outs, bufs, sems = make_plan(dims)

    operands = [
        inputs.reshape(NI, L, D),
        cotangents.reshape(NI, L, D),
        pair_ids.reshape(2, NI, 1, SEQ),
        jnp.swapaxes(self_routes.reshape(NI, SEQ, T), 1, 2),
        jnp.swapaxes(cross_routes.reshape(NI, SEQ, T), 1, 2),
        norm_gain[0],
        norm_bias[0],
        w_kv[0],
        w_router[0].T,
        jnp.swapaxes(w_query[0], 1, 2),
        w_out[0],
        w_in[0],
        w_back[0],
        cross_gain[None],
        cross_bias[None],
        cross_kv,
        cross_router.T,
        jnp.swapaxes(cross_query, 1, 2),
        cross_out,
    ]
    vmem = pl.BlockSpec(memory_space=pltpu.VMEM)
    anywhere = pl.BlockSpec(memory_space=pl.ANY)
    res = pl.pallas_call(
        make_kernel(dims),
        out_shape=[jax.ShapeDtypeStruct(s, t) for s, t in outs.values()],
        in_specs=[vmem if n in STAY else anywhere for n in ins],
        out_specs=[anywhere if n[:4] == "out_" else vmem for n in outs],
        scratch_shapes=[pltpu.VMEM(s, t) for s, t in bufs.values()]
        + [pltpu.SemaphoreType.DMA(s) for s in sems.values()]
        + [pltpu.VMEM(o.shape, o.dtype) for n, o in zip(ins, operands) if n in fetched(ins)],
        compiler_params=pltpu.CompilerParams(
            collective_id=0, has_side_effects=True, vmem_limit_bytes=62 * 1024 * 1024
        ),
        name="layers",
    )(*operands)
    DB = D // DP
    EB = DB // E
    shapes = [
        ((NI, L, D), BF16),
        ((NI, L, D), F32),
        ((1, 2, EB), F32),
        ((1, 2, EB), F32),
        ((EB, 2 * HD), F32),
        ((NE, EB), F32),
        ((QB, DB), F32),
        ((QB, DB), F32),
        ((DB, HB), F32),
        ((HB, DB), F32),
        ((1, EB), F32),
        ((1, EB), F32),
        ((EB, 2 * HD), F32),
        ((NE, EB), F32),
        ((QB, DB), F32),
        ((QB, DB), F32),
    ]
    (
        layer, grads, gain, bias, kv, router, query, out, w_in_g, w_back_g, c_gain, c_bias, c_kv,
        c_router, c_query, c_out,
    ) = pl.pallas_call(
        make_finish(E, NE, EB, QB),
        out_shape=[jax.ShapeDtypeStruct(s, t) for s, t in shapes],
        in_specs=[vmem] * len(outs),
        out_specs=[vmem] * len(shapes),
        name="results",
    )(*res)

    def of_query(g):
        return jnp.swapaxes(g.reshape(npd, HD, DB), 1, 2)

    def of_out(g):
        return g.reshape(npd, HD, DB)

    return (
        layer.reshape(inputs.shape),
        grads.reshape(inputs.shape),
        gain,
        bias,
        kv[None],
        router.T[None],
        of_query(query)[None],
        of_out(out)[None],
        w_in_g[None],
        w_back_g[None],
        c_gain[0],
        c_bias[0],
        c_kv,
        c_router.T,
        of_query(c_query),
        of_out(c_out),
    )


def solution(mesh):
    placed = (
        P("section", None, "dp", "expert", None),
        P("section", None, "dp", "expert", None),
        P(None, None, "dp", None),
        P("section", None, "dp", None, None),
        P(None, "dp", None, None),
        P("section", None, None),
        P("section", None, None),
        P("section", None, None),
        P("section", None, None),
        P("section", "expert", None, None),
        P("section", "expert", None, None),
        P("section", None, "expert"),
        P("section", "expert", None),
        P(),
        P(),
        P(),
        P(),
        P("expert", None, None),
        P("expert", None, None),
    )
    return jax.shard_map(
        body,
        mesh=mesh,
        in_specs=placed,
        out_specs=(
            P("section", None, "dp", "expert", None),
            P("section", None, "dp", "expert", None),
            P("section", None, ("dp", "expert")),
            P("section", None, ("dp", "expert")),
            P("section", ("dp", "expert"), None),
            P("section", ("dp", "expert"), None),
            P("section", "expert", "dp", None),
            P("section", "expert", None, "dp"),
            P("section", "dp", "expert"),
            P("section", "expert", "dp"),
            P(("dp", "expert")),
            P(("dp", "expert")),
            P(("dp", "expert"), None),
            P(("dp", "expert"), None),
            P("expert", "dp", None),
            P("expert", None, "dp"),
        ),
        check_vma=False,
    )
```

```python
from types import SimpleNamespace

import jax
import jax.numpy as jnp
from jax import lax
from jax.experimental import pallas as pl
from jax.experimental.pallas import tpu as pltpu
from jax.sharding import PartitionSpec as P

F32 = jnp.float32
BF16 = jnp.bfloat16
MESH = pl.DeviceIdType.MESH
RT = 16
SR = 32
NP = 8
NS = 3
NX = NP - NS
NH = 2


def nn(a, b):
    return lax.dot_general(a, b, (((1,), (0,)), ((), ())), preferred_element_type=F32)


def nt(a, b):
    return lax.dot_general(a, b, (((1,), (1,)), ((), ())), preferred_element_type=F32)


def tn(a, b):
    return lax.dot_general(a, b, (((0,), (0,)), ((), ())), preferred_element_type=F32)


def gelu_parts(h):
    c = 0.7978845608028654
    a = c + (c * 0.044715) * (h * h)
    t = jnp.tanh(h * a)
    half = 0.5 + 0.5 * t
    act = h * half
    return act, half + act * ((1.0 - t) * (3.0 * a - 2.0 * c))


def norm_stats(x):
    centred = x - jnp.mean(x, -1, keepdims=True)
    r = lax.rsqrt(jnp.mean(centred * centred, -1, keepdims=True) + 1e-05)
    return centred * r, r


def norm_back(x, gain, grad):
    xhat, r = norm_stats(x)
    gg = grad * gain
    m1 = jnp.mean(gg, -1, keepdims=True)
    m2 = jnp.mean(gg * xhat, -1, keepdims=True)
    return (
        r * (gg - m1 - xhat * m2),
        jnp.sum(grad * xhat, 0, keepdims=True),
        jnp.sum(grad, 0, keepdims=True),
    )


INS = [
    "x", "cot", "pairs", "routes_s", "routes_c", "ng", "nb", "wkv", "wr", "wq", "wo", "win",
    "wback", "cg", "cb", "ckv", "cr", "cq", "co",
]
STAY = ("wr", "cr")
PLACED = ("win", "wback")


def fetched(ins):
    return [n for n in ins if n not in STAY + PLACED]


def make_plan(dims):
    (NI, L, D, SEQ, T, NE, HD, HB, E, DP) = dims
    npd = NE // E
    QB = npd * HD
    NQ = NE * HD
    X = E // 2
    DB = D // DP
    HP = DP // 2
    ins = INS
    outs = dict(
        out_layer=((NI, L, D), BF16),
        out_ig=((NI, L, D), F32),
        o_in=((DB, HB), F32),
        o_back=((DB, HB), F32),
        o_qo=((2, DB, 2 * QB), F32),
        o_kv=((2, DB, 2 * HD), F32),
        o_small=((SR, 128), F32),
    )
    bufs = dict(
        o_layer=((NI, L, D), BF16),
        o_ig=((NI, L, D), F32),
        win_all=((E, D, HB), BF16),
        wback_all=((E, HB, D), BF16),
        wqr=((2, NQ + RT, D), BF16),
        wo_all=((2, NQ, D), BF16),
        wr_pad=((RT, D), F32),
        x1=((NI, L, D), F32),
        x2=((NI, L, D), F32),
        n=((NI, 3, L, D), BF16),
        dz=((NI, L, D), BF16),
        acc=((L, D), F32),
        dn=((NI, L, D), F32),
        act=((NI, E, L, HB), BF16),
        turned=((NI, D, L), BF16),
        dh=((NI, E, L, HB), BF16),
        kv_s=((NI, SEQ, 2 * HD), BF16),
        kv_c=((NI, SEQ, 2 * HD), BF16),
        kvt=((2, NI, 2 * HD, SEQ), BF16),
        bias=((SEQ, L), F32),
        qt=((2, NI, T, HD, L), BF16),
        gate=((2, NI, T, 8, L), F32),
        inv=((2, NI, T, 8, L), F32),
        p=((2, NI, T, SEQ, L), BF16),
        heads=((2, NI, T, HD, L), F32),
        ht=((2, NI, NQ, L), BF16),
        dq=((T, HD, L), BF16),
        dkv_acc=((SEQ, 2 * HD), F32),
        dkv_own=((NI, L, 2 * HD), F32),
        dkv_send=((NI, SEQ, 2 * HD), BF16),
        dkv_recv=((NI, X, L, 2 * HD), BF16),
        dksum_r=((NI, X, L, 2 * HD), BF16),
        dckv_send=((NI, SEQ, 2 * HD), BF16),
        dckv_recv=((NI, X, L, 2 * HD), BF16),
        dsum_r=((NI, X, L, 2 * HD), BF16),
        ckv_own=((NI, L, 2 * HD), BF16),
        g_big=((E, 2, D, HB), F32),
        g_qr=((2, NQ + RT, D), F32),
        g_o=((2, NQ, D), F32),
        g_kv=((2, D, 2 * HD), F32),
        small=((SR, D), F32),
        a_big=((2, X, D, HB), BF16),
        a_big_r=((2, X, D, HB), BF16),
        a_qo=((2, X, 2 * QB, D), BF16),
        a_qo_r=((2, X, 2 * QB, D), BF16),
        b_big=((X - 1, 2, D, HB), BF16),
        b_big_r=((X - 1, 2, D, HB), BF16),
        za_big=((2, HP, DB, HB), BF16),
        za_big_r=((2, HP, DB, HB), BF16),
        zb_big=((2, HP - 1, DB, HB), BF16),
        zb_big_r=((2, HP - 1, DB, HB), BF16),
        b_qo=((2, X - 1, 2 * QB, D), BF16),
        b_qo_r=((2, X - 1, 2 * QB, D), BF16),
        own_qo=((D, 2 * QB), F32),
        c_qo=((2, DP - 1, DB, 2 * QB), BF16),
        c_qo_r=((2, DP - 1, DB, 2 * QB), BF16),
        qo_own=((2, DB, 2 * QB), F32),
        kv_ar=((D, 2 * HD), F32),
        kv_sum=((D, 2 * HD), F32),
        c_kv=((DP - 1, DB, 2 * HD), BF16),
        c_kv_r=((DP - 1, DB, 2 * HD), BF16),
        kv_b=((DB, 2 * HD), BF16),
        kv_br=((X - 1, DB, 2 * HD), BF16),
        kv_fin=((DB, 2 * HD), F32),
        kv_sib=((DB, 2 * HD), F32),
        kv_sec=((DB, 2 * HD), F32),
        sm_ar=((SR, D), F32),
        sm_b=((SR, D), BF16),
        sm_br=((X - 1, SR, D), BF16),
        za_sm=((SR, D), BF16),
        za_sm_r=((DP - 1, SR, 128), BF16),
        sm_own=((SR, 128), F32),
        sm_fin=((SR, D), F32),
        sm_sec=((SR, 128), F32),
        qo_fin=((DB, 2 * QB), F32),
        qo_sec=((DB, 2 * QB), F32),
    )
    sems = dict(
        q_s=(2, 2, E), q_r=(2, 2, E),
        sib_s=(2,), sib_r=(2,),
        wx_s=(2, X, NX), wx_r=(2, X, NX),
        wz_s=(2, X, NS), wz_r=(2, X, NS),
        wf_s=(2, X, NP), wf_r=(2, X, NP),
        kv_ss=(NI, E), kv_rs=(NI, E),
        ckv_s=(NI, E), ckv_r=(NI, E),
        dckv_s=(NI, X), dckv_r=(NI, X),
        dsum_ss=(NI, X), dsum_rs=(NI, X),
        dkv_s=(NI, X), dkv_r=(NI, X),
        dksum_ss=(NI, X), dksum_rs=(NI, X),
        a_s=(2, X), a_r=(2, X),
        b_s=(X - 1, 2, DP, NH), b_r=(X - 1, 2, DP, NH),
        zab_s=(2, HP, NH), zab_r=(2, HP, NH),
        zbb_s=(2, HP, NH), zbb_r=(2, HP, NH),
        aq_s=(2,), aq_r=(2,),
        cq_s=(2, DP - 1), cq_r=(2, DP - 1),
        bq_s=(2, X - 1), bq_r=(2, X - 1),
        ka_s=(1,), ka_r=(1,),
        kb_s=(X - 1,), kb_r=(X - 1,),
        ck_s=(DP - 1,), ck_r=(DP - 1,),
        kf_s=(3,), kf_r=(2,),
        sa_s=(1,), sa_r=(1,),
        sb_s=(X - 1,), sb_r=(X - 1,),
        zs_s=(DP - 1,), zs_r=(DP - 1,),
        sec_s=(2,), sec_r=(2,),
        ld=(len(ins) + 2,),
    )
    return ins, outs, bufs, sems


def make_kernel(dims):
    (NI, L, D, SEQ, T, NE, HD, HB, E, DP) = dims
    npd = NE // E
    QB = npd * HD
    NQ = NE * HD
    X = E // 2
    DB = D // DP
    HP = DP // 2
    scale = HD ** -0.5
    ins, outs, bufs, sems = make_plan(dims)
    names = [n if n in STAY else "in_" + n for n in ins]
    names += list(outs) + list(bufs) + list(sems) + fetched(ins)

    def kernel(*refs):
        r = SimpleNamespace(**dict(zip(names, refs)))
        sec = lax.axis_index("section")
        dpi = lax.axis_index("dp")
        me = lax.axis_index("expert")
        core = lax.rem(me, 2)
        xi = me // 2
        sib = xi * 2 + (1 - core)
        dec = sec == 1
        enc = sec == 0
        other = 1 - sec
        half = lax.rem(dpi, 2)
        mate = dpi + 1 - 2 * half
        row0 = pl.multiple_of(me * L, L)

        def to_expert(j):
            return (sec, dpi, j)

        def to_dp(j):
            return (sec, j, me)

        def to_section(j):
            return (other, dpi, j)

        def rcopy(src, dst, ssem, rsem, dev):
            return pltpu.make_async_remote_copy(
                src_ref=src, dst_ref=dst, send_sem=ssem, recv_sem=rsem, device_id=dev,
                device_id_type=MESH,
            )

        def chip(x):
            return x * 2 + core

        def q_copy(a, kind, block, to, slot):
            ref = r.wqr if kind == 0 else r.wo_all
            ref = ref.at[a, pl.ds(pl.multiple_of(block * QB, QB), QB)]
            return rcopy(ref, ref, r.q_s.at[a, kind, slot], r.q_r.at[a, kind, block], to_expert(to))

        def w_ref(kind, c):
            return (r.win_all if kind == 0 else r.wback_all).at[c]

        def w_piece(kind, c, p):
            rows = (D if kind == 0 else HB) // NP
            return w_ref(kind, c).at[pl.ds(pl.multiple_of(p * rows, rows), rows)]

        def sib_copy(kind, c):
            ref = w_ref(kind, c)
            return rcopy(ref, ref, r.sib_s.at[kind], r.sib_r.at[kind], to_expert(sib))

        def shared(q, parity):
            return NS * parity + q

        def over_x_at(q):
            return shared(q, half) if q < NS else NS + q

        def wx_copy(kind, c, q, to_x, frm_x):
            ref = w_piece(kind, c, over_x_at(q))
            return rcopy(
                ref, ref, r.wx_s.at[kind, to_x, q], r.wx_r.at[kind, frm_x, q],
                to_expert(chip(to_x)),
            )

        def wz_copy(kind, x, q, parity):
            ref = w_piece(kind, chip(x), shared(q, parity))
            return rcopy(ref, ref, r.wz_s.at[kind, x, q], r.wz_r.at[kind, x, q], to_dp(mate))

        def wf_copy(kind, c, x, p):
            ref = w_piece(kind, c, p)
            return rcopy(ref, ref, r.wf_s.at[kind, x, p], r.wf_r.at[kind, x, p], to_expert(sib))

        def rows_of(ref, i, j):
            return ref.at[i, pl.ds(pl.multiple_of(j * L, L), L)]

        def kv_copy(i, block, to, slot):
            ref = rows_of(r.kv_s, i, block)
            return rcopy(ref, ref, r.kv_ss.at[i, slot], r.kv_rs.at[i, block], to_expert(to))

        def ckv_copy(i, to):
            return rcopy(
                r.ckv_own.at[i], rows_of(r.kv_c, i, me), r.ckv_s.at[i, to], r.ckv_r.at[i, me],
                to_section(to),
            )

        def ckv_relay(i, block):
            ref = rows_of(r.kv_c, i, block)
            return rcopy(ref, ref, r.ckv_s.at[i, block], r.ckv_r.at[i, block], to_expert(sib))

        def ckv_gather(i):
            same = xpeers() + [xi]
            for x in same:
                ckv_relay(i, chip(x)).wait_recv()
                ckv_relay(i, chip(x)).start()
            for x in same:
                ckv_relay(i, x * 2 + 1 - core).wait_recv()

        def dsum_copy(i, x):
            at = x * 2 + 1 - core
            return rcopy(
                rows_of(r.dckv_send, i, at), r.dsum_r.at[i, x], r.dsum_ss.at[i, x],
                r.dsum_rs.at[i, x], to_expert(sib),
            )

        def dckv_copy(i, to_x, frm_x):
            return rcopy(
                rows_of(r.dckv_send, i, chip(to_x)), r.dckv_recv.at[i, frm_x],
                r.dckv_s.at[i, to_x], r.dckv_r.at[i, frm_x], to_section(chip(to_x)),
            )

        def dckv_out(i):
            order = xpeers() + [xi]
            for x in order:
                dsum_copy(i, x).start()
            for x in order:
                dsum_copy(i, x).wait_recv()
                at = pl.ds(pl.multiple_of(chip(x) * L, L), L)
                r.dckv_send[i, at] = (
                    r.dkv_acc[at] + r.dsum_r[i, x].astype(F32)
                ).astype(BF16)
                dckv_copy(i, x, xi).start()

        def dksum_copy(i, x):
            at = x * 2 + 1 - core
            return rcopy(
                rows_of(r.dkv_send, i, at), r.dksum_r.at[i, x], r.dksum_ss.at[i, x],
                r.dksum_rs.at[i, x], to_expert(sib),
            )

        def dkv_copy(i, to_x, frm_x):
            return rcopy(
                rows_of(r.dkv_send, i, chip(to_x)), r.dkv_recv.at[i, frm_x], r.dkv_s.at[i, to_x],
                r.dkv_r.at[i, frm_x], to_expert(chip(to_x)),
            )

        def dkv_out(i):
            for x in xpeers() + [xi]:
                dksum_copy(i, x).start()
            r.dkv_own[i] = r.dkv_acc[pl.ds(row0, L)]
            for x in xpeers():
                dksum_copy(i, x).wait_recv()
                at = pl.ds(pl.multiple_of(chip(x) * L, L), L)
                r.dkv_send[i, at] = (r.dkv_acc[at] + r.dksum_r[i, x].astype(F32)).astype(BF16)
                dkv_copy(i, x, xi).start()

        def dkv_in(i):
            dksum_copy(i, xi).wait_recv()
            total = r.dkv_own[i] + r.dksum_r[i, xi].astype(F32)
            for x in xpeers():
                dkv_copy(i, x, x).wait_recv()
                total = total + r.dkv_recv[i, x].astype(F32)
            return total

        def over_x(src, dst, ssem, rsem, o):
            return rcopy(src, dst, ssem, rsem, to_expert(chip(lax.rem(xi + o + 1, X))))

        def to_mate(src, dst, ssem, rsem):
            return rcopy(src, dst, ssem, rsem, to_dp(mate))

        def mates_at(k):
            return lax.rem(dpi // 2 + k, HP) * 2 + 1 - half

        def mine_at(k):
            return lax.rem(dpi // 2 + k, HP) * 2 + half

        def over_dp(src, dst, ssem, rsem, k):
            return rcopy(src, dst, ssem, rsem, to_dp(mine_at(k)))

        def over_sib(src, dst, ssem, rsem):
            return rcopy(src, dst, ssem, rsem, to_expert(sib))

        def a_copy(kind, x):
            return over_sib(
                r.a_big.at[kind, x], r.a_big_r.at[kind, x], r.a_s.at[kind, x], r.a_r.at[kind, x]
            )

        def block_rows(d):
            return pl.ds(pl.multiple_of(d * DB, DB), DB)

        HB_ROWS = DB // NH

        def part_rows(d, h):
            return pl.ds(pl.multiple_of(d * DB + h * HB_ROWS, HB_ROWS), HB_ROWS)

        def sub_rows(h):
            return pl.ds(h * HB_ROWS, HB_ROWS)

        def b_copy(kind, o, d, h):
            return over_x(
                r.b_big.at[o, kind, part_rows(d, h)], r.b_big_r.at[o, kind, part_rows(d, h)],
                r.b_s.at[o, kind, d, h], r.b_r.at[o, kind, d, h], o,
            )

        def zab_copy(kind, k, h):
            return to_mate(
                r.za_big.at[kind, k, sub_rows(h)], r.za_big_r.at[kind, k, sub_rows(h)],
                r.zab_s.at[kind, k, h], r.zab_r.at[kind, k, h],
            )

        def zbb_copy(kind, k, h):
            return over_dp(
                r.zb_big.at[kind, k - 1, sub_rows(h)], r.zb_big_r.at[kind, k - 1, sub_rows(h)],
                r.zbb_s.at[kind, k, h], r.zbb_r.at[kind, k, h], k,
            )

        def aq_copy(a):
            return over_sib(r.a_qo.at[a], r.a_qo_r.at[a], r.aq_s.at[a], r.aq_r.at[a])

        def around(src, dst, ssem, rsem, o):
            return rcopy(src, dst, ssem, rsem, to_dp(lax.rem(dpi + o + 1, DP)))

        def cq_copy(a, o):
            return around(
                r.c_qo.at[a, o], r.c_qo_r.at[a, o], r.cq_s.at[a, o], r.cq_r.at[a, o], o
            )

        def bq_copy(a, o):
            return over_x(
                r.b_qo.at[a, o], r.b_qo_r.at[a, o], r.bq_s.at[a, o], r.bq_r.at[a, o], o
            )

        def ka_copy():
            return over_sib(r.g_kv.at[1 - core], r.kv_ar, r.ka_s.at[0], r.ka_r.at[0])

        def kb_copy(o):
            return over_x(r.kv_b, r.kv_br.at[o], r.kb_s.at[o], r.kb_r.at[o], o)

        def ck_copy(o):
            return around(r.c_kv.at[o], r.c_kv_r.at[o], r.ck_s.at[o], r.ck_r.at[o], o)

        def kf_copy():
            return over_sib(r.kv_fin, r.kv_sib, r.kf_s.at[0], r.kf_r.at[0])

        def ks_copy(to_core):
            return rcopy(
                r.kv_fin, r.kv_sec, r.kf_s.at[1 + to_core], r.kf_r.at[1],
                to_section(xi * 2 + to_core),
            )

        def sa_copy():
            return over_sib(r.small, r.sm_ar, r.sa_s.at[0], r.sa_r.at[0])

        def sb_copy(o):
            return over_x(r.sm_b, r.sm_br.at[o], r.sb_s.at[o], r.sb_r.at[o], o)

        def lanes(d):
            return pl.ds(pl.multiple_of(d * DB // 128 * 128, 128), 128)

        def zs_copy(o):
            src = r.za_sm.at[:, lanes(lax.rem(dpi + o + 1, DP))]
            return around(src, r.za_sm_r.at[o], r.zs_s.at[o], r.zs_r.at[o], o)

        def sec_copy(kind):
            src, dst = ((r.qo_fin, r.qo_sec), (r.sm_own, r.sm_sec))[kind]
            return rcopy(src, dst, r.sec_s.at[kind], r.sec_r.at[kind], to_section(me))

        def peers():
            return [lax.rem(me + o, E) for o in range(1, E)]

        def xpeers():
            return [lax.rem(xi + o, X) for o in range(1, X)]

        def dpeers():
            return [lax.rem(dpi + o, DP) for o in range(1, DP)]

        def load(name):
            src = getattr(r, "in_" + name)
            if name in PLACED:
                dst = w_ref(PLACED.index(name), me)
            else:
                dst = getattr(r, name)
            return pltpu.make_async_copy(src, dst, r.ld.at[ins.index(name)])

        def store(name):
            k = ("layer", "ig").index(name)
            src, dst = getattr(r, "o_" + name), getattr(r, "out_" + name)
            return pltpu.make_async_copy(src, dst, r.ld.at[len(ins) + k])

        soon = ["x", "ng", "nb", "wkv", "wq", "wo"]
        early = soon + ["win", "wback", "pairs", "routes_s"]
        late = [n for n in ins if n not in early and n not in STAY]
        for name in early + late:
            load(name).start()
        barrier = pltpu.get_barrier_semaphore()
        for j in peers():
            pl.semaphore_signal(barrier, inc=1, device_id=to_expert(j), device_id_type=MESH)
        for j in dpeers():
            pl.semaphore_signal(barrier, inc=1, device_id=to_dp(j), device_id_type=MESH)
        for j in range(E):
            pl.semaphore_signal(barrier, inc=1, device_id=to_section(j), device_id_type=MESH)

        def gather_send(copy):
            copy(me, sib, sib).start()
            for x in xpeers():
                copy(me, chip(x), chip(x)).start()

        def gather_relay(copy):
            for x in xpeers():
                copy(chip(x), sib, x * 2 + 1 - core).wait_recv()
                copy(chip(x), sib, x * 2 + 1 - core).start()

        def gather_take(copy):
            copy(sib, sib, sib).wait_recv()
            for x in xpeers():
                c = x * 2 + 1 - core
                copy(c, sib, c).wait_recv()

        def gather_sent(copy):
            copy(me, sib, sib).wait_send()
            for x in xpeers():
                copy(me, chip(x), chip(x)).wait_send()
                copy(chip(x), sib, x * 2 + 1 - core).wait_send()

        def q_of(a, kind):
            return lambda block, to, slot: q_copy(a, kind, block, to, slot)

        def kv_of(i):
            return lambda block, to, slot: kv_copy(i, block, to, slot)

        def norm_rows(x, gain, shift):
            return norm_stats(x)[0] * gain + shift

        def gain_of(which):
            if which == 1:
                return r.cg[...], r.cb[...]
            return r.ng[which // 2 : which // 2 + 1], r.nb[which // 2 : which // 2 + 1]

        def own_query_weights(a, q_ref, o_ref, wr_ref):
            for j in range(npd):
                at = pl.multiple_of(me * QB + j * HD, HD)
                r.wqr[a, pl.ds(at, HD)] = q_ref[j]
                r.wo_all[a, pl.ds(at, HD)] = o_ref[j]
            r.wr_pad[...] = jnp.zeros_like(r.wr_pad)
            r.wr_pad[:NE] = wr_ref[...].astype(F32)
            r.wqr[a, pl.ds(NQ, RT)] = r.wr_pad[...].astype(BF16)

        def first_norm(i):
            g, b = gain_of(0)
            n = norm_rows(r.x[i].astype(F32), g, b).astype(BF16)
            r.n[i, 0] = n
            r.kv_s[i, pl.ds(row0, L)] = nn(n, r.wkv[...]).astype(BF16)

        for name in soon:
            load(name).wait()
        own_query_weights(0, r.wq, r.wo, r.wr)
        first_norm(0)
        pl.semaphore_wait(barrier, (E - 1) + (DP - 1) + E)

        gather_send(q_of(0, 0))
        gather_send(kv_of(0))
        gather_send(q_of(0, 1))
        def later_norms(i, _):
            first_norm(i)
            gather_send(kv_of(i))
            return 0

        @pl.when(dec)
        def _():
            lax.fori_loop(1, NI, later_norms, 0)

        for name in PLACED:
            load(name).wait()
        for kind in (0, 1):
            sib_copy(kind, me).start()
        for part in (range(NS), range(NS, NX)):
            for kind in (0, 1):
                for q in part:
                    for x in xpeers():
                        wx_copy(kind, me, q, x, xi).start()

        @pl.when(enc)
        def _():
            lax.fori_loop(1, NI, later_norms, 0)

        for name in late + ["pairs", "routes_s"]:
            load(name).wait()
        own_query_weights(1, r.cq, r.co, r.cr)

        @pl.when(dec)
        def _():
            for kind in (0, 1):
                gather_send(q_of(1, kind))

        def weights_over_x(kind, q):
            for x in xpeers():
                wx_copy(kind, chip(x), q, x, x).wait_recv()
                if q < NS:
                    wz_copy(kind, x, q, half).start()
                wf_copy(kind, chip(x), x, over_x_at(q)).start()

        def weights_over_z(kind, q):
            for x in xpeers():
                wz_copy(kind, x, q, 1 - half).wait_recv()
                wf_copy(kind, chip(x), x, shared(q, 1 - half)).start()

        def weights_over_sib(kind):
            for x in xpeers():
                for p in range(NP):
                    wf_copy(kind, x * 2 + 1 - core, x, p).wait_recv()

        def weights_sent():
            for kind in (0, 1):
                sib_copy(kind, me).wait_send()
                for x in xpeers():
                    for q in range(NX):
                        wx_copy(kind, me, q, x, xi).wait_send()
                    for q in range(NS):
                        wz_copy(kind, x, q, half).wait_send()
                    for p in range(NP):
                        wf_copy(kind, chip(x), x, p).wait_send()

        zeros_h = jnp.zeros((HD, L), BF16)

        def set_bias(i, a):
            own = r.pairs[sec, i, :, pl.ds(row0, L)].astype(F32)
            if a == 0:
                keys = r.pairs[sec, i].astype(F32)
            else:
                keys = r.pairs[0, i].astype(F32)
            kc = jnp.broadcast_to(keys, (128, SEQ)).T
            if L > 128:
                kc = jnp.concatenate([kc] * (L // 128), 1)
            same = kc == own
            if a == 0:
                qpos = row0 + lax.broadcasted_iota(jnp.int32, (1, L), 1)
                limit = jnp.where(dec, qpos, SEQ)
                same = same & (lax.broadcasted_iota(jnp.int32, (SEQ, L), 0) <= limit)
            r.bias[...] = jnp.where(same, 0.0, -1e30)

        def route_rows(i, a):
            ref = r.routes_s if a == 0 else r.routes_c
            return [ref[i, k : k + 1, pl.ds(row0, L)] for k in range(T)]

        def pick(rows, route, size):
            total = jnp.zeros((size, L), F32)
            for e in range(NE):
                total = jnp.where(route == e, rows[e * size : (e + 1) * size], total)
            return total

        def project_queries(i, a):
            n = r.n[i, a]
            ql = nt(r.wqr[a], n)
            routes = route_rows(i, a)
            chosen = []
            for k in range(T):
                r.qt[a, i, k] = (pick(ql[:NQ], routes[k], HD).astype(BF16).astype(F32) * scale).astype(BF16)
                chosen.append(pick(ql[NQ : NQ + NE], routes[k], 1))
            top = chosen[0]
            for k in range(1, T):
                top = jnp.maximum(top, chosen[k])
            ex = [jnp.exp(c - top) for c in chosen]
            total = ex[0]
            for k in range(1, T):
                total = total + ex[k]
            for k in range(T):
                r.gate[a, i, k] = jnp.broadcast_to(ex[k] / total, (8, L))

        def attend(i, a, kv_ref, base):
            kv = kv_ref[i]
            r.kvt[a, i] = kv.astype(F32).T.astype(BF16)

            def one(k, _):
                q = jnp.concatenate([r.qt[a, i, k], zeros_h], 0)
                s = nn(kv, q) + r.bias[...]
                m = jnp.max(s, 0, keepdims=True)
                ex = jnp.exp(s - m)
                inv = 1.0 / jnp.sum(ex, 0, keepdims=True)
                p = ex.astype(BF16)
                r.p[a, i, k] = p
                r.inv[a, i, k] = jnp.broadcast_to(inv, (8, L))
                r.heads[a, i, k] = nn(r.kvt[a, i, HD:], p) * inv
                return 0

            lax.fori_loop(0, T, one, 0, unroll=True)
            routes = route_rows(i, a)
            gated = [
                r.heads[a, i, k].astype(BF16).astype(F32) * r.gate[a, i, k, 0:1] for k in range(T)
            ]
            for e in range(NE):
                block = jnp.zeros((HD, L), F32)
                for k in range(T):
                    block = jnp.where(routes[k] == e, gated[k], block)
                r.ht[a, i, e * HD : (e + 1) * HD] = block.astype(BF16)
            return base + tn(r.ht[a, i], r.wo_all[a])

        def attend_back(i, a, kv_ref, dx, send_ref):
            dxb = dx.astype(BF16)
            routes = route_rows(i, a)
            r.g_o[a] += nn(r.ht[a, i], dxb)
            gt = nt(r.wo_all[a], dxb)
            dgates = []
            for k in range(T):
                g = pick(gt, routes[k], HD)
                dgates.append(
                    jnp.sum(r.heads[a, i, k].astype(BF16).astype(F32) * g, 0, keepdims=True)
                )
                r.dq[k] = (g * r.gate[a, i, k, 0:1]).astype(BF16)
            gates = [r.gate[a, i, k, 0:1] for k in range(T)]
            mid = gates[0] * dgates[0]
            for k in range(1, T):
                mid = mid + gates[k] * dgates[k]
            dchosen = [gates[k] * (dgates[k] - mid) for k in range(T)]
            kv = kv_ref[i]
            r.dkv_acc[...] = jnp.zeros_like(r.dkv_acc)

            def one(k, _):
                dheads = (r.dq[k].astype(F32) * r.inv[a, i, k, 0:1]).astype(BF16)
                p = r.p[a, i, k]
                dv = jnp.concatenate([zeros_h, dheads], 0)
                delta = jnp.sum(dheads.astype(F32) * r.heads[a, i, k], 0, keepdims=True)
                ds = (p.astype(F32) * (nn(kv, dv) - delta)).astype(BF16)
                qk = jnp.concatenate([r.qt[a, i, k], zeros_h], 0)
                r.dkv_acc[...] += nt(ds, qk) + nt(p, dv)
                r.dq[k] = (nn(r.kvt[a, i, :HD], ds) * scale).astype(BF16)
                return 0

            lax.fori_loop(0, T, one, 0, unroll=True)
            send_ref[i] = r.dkv_acc[...].astype(BF16)
            blocks = []
            for e in range(NE):
                block = jnp.zeros((HD, L), F32)
                for k in range(T):
                    block = jnp.where(routes[k] == e, r.dq[k].astype(F32), block)
                blocks.append(block)
            logit_rows = jnp.zeros((RT, L), F32)
            rows = lax.broadcasted_iota(jnp.int32, (RT, L), 0)
            for k in range(T):
                logit_rows = jnp.where(rows == routes[k], dchosen[k], logit_rows)
            dql = jnp.concatenate(blocks + [logit_rows], 0).astype(BF16)
            r.g_qr[a] += nn(dql, r.n[i, a])
            return tn(dql, r.wqr[a])

        def chunk_at(s):
            return lax.rem(xi + s // 2, X) * 2 + jnp.where(lax.rem(s, 2) == 0, core, 1 - core)

        def chunk_out(s):
            return lax.rem(xi + s // 2 + 1, X) * 2 + jnp.where(lax.rem(s, 2) == 0, 1 - core, core)

        def ffn_forward(i, low, high):
            n = r.n[i, 2]

            def one(s, _):
                c = chunk_at(s)
                act, slope = gelu_parts(nn(n, r.win_all[c]))
                act = act.astype(BF16)
                r.act[i, c] = act
                r.dh[i, c] = slope.astype(BF16)
                r.acc[...] += nn(act, r.wback_all[c])
                return 0

            lax.fori_loop(low, high, one, 0, unroll=True)

        def ffn_middle(i):
            n = r.n[i, 2]
            r.acc[...] = jnp.zeros_like(r.acc)

            def one(c, _):
                act, slope = gelu_parts(nn(n, r.win_all[c]))
                r.act[i, c] = act.astype(BF16)
                dh = (r.dh[i, c].astype(F32) * slope).astype(BF16)
                r.dh[i, c] = dh
                r.acc[...] += nt(dh, r.win_all[c])
                return 0

            lax.fori_loop(0, E, one, 0, unroll=True)
            return r.acc[...]

        def big_sib(kind):
            for o, x in enumerate(xpeers()):
                a_copy(kind, x).wait_recv()
                r.b_big[o, kind] = (
                    r.g_big[chip(x), kind] + r.a_big_r[kind, x].astype(F32)
                ).astype(BF16)

        def big_sib_own(kind):
            a_copy(kind, xi).wait_recv()
            r.g_big[me, kind] += r.a_big_r[kind, xi].astype(F32)

        def dp_at(s):
            return mates_at(s) if s < HP else mine_at((s - HP + 1) % HP)

        def big_send(kind, low, high):
            for s in range(low, high):
                for h in range(NH):
                    for o in range(X - 1):
                        b_copy(kind, o, dp_at(s), h).start()

        def big_over_x(kind, s):
            for h in range(NH):
                big_part_over_x(kind, s, h)

        def big_part_over_x(kind, s, h):
            d = dp_at(s)
            total = r.g_big[me, kind, part_rows(d, h)]
            for o in range(X - 1):
                b_copy(kind, o, d, h).wait_recv()
                total = total + r.b_big_r[o, kind, part_rows(d, h)].astype(F32)
            if s < HP:
                r.za_big[kind, s, sub_rows(h)] = total.astype(BF16)
                zab_copy(kind, s, h).start()
                return
            k = (s - HP + 1) % HP
            zab_copy(kind, k, h).wait_recv()
            total = total + r.za_big_r[kind, k, sub_rows(h)].astype(F32)
            if k > 0:
                r.zb_big[kind, k - 1, sub_rows(h)] = total.astype(BF16)
                zbb_copy(kind, k, h).start()
            else:
                r.g_big[me, kind, part_rows(d, h)] = total

        def big_end(kind, out):
            for h in range(NH):
                total = r.g_big[me, kind, part_rows(dpi, h)]
                for k in range(1, HP):
                    zbb_copy(kind, k, h).wait_recv()
                    total = total + r.zb_big_r[kind, k - 1, sub_rows(h)].astype(F32)
                out[sub_rows(h)] = total

        def hand_out(i, s, c, kind):
            @pl.when(jnp.logical_and(i == NI - 1, lax.rem(s, 2) == 0))
            def _():
                x = c // 2
                r.a_big[kind, x] = r.g_big[c, kind].astype(BF16)
                a_copy(kind, x).start()

        def ffn_back(i):
            dz = r.dz[i]
            dzt = dz.astype(F32).T.astype(BF16)

            def back(s, _):
                c = chunk_out(s)
                r.g_big[c, 1] += nn(dzt, r.act[i, c])
                hand_out(i, s, c, 1)
                return 0

            lax.fori_loop(0, E, back, 0, unroll=True)

            @pl.when(i == NI - 1)
            def _():
                big_sib(1)
                big_send(1, 0, HP)

            nt_ = r.n[i, 2].astype(F32).T.astype(BF16)
            r.acc[...] = jnp.zeros_like(r.acc)

            def inward(s, _):
                c = chunk_out(s)
                dh = (nt(dz, r.wback_all[c]) * r.dh[i, c].astype(F32)).astype(BF16)
                r.acc[...] += nt(dh, r.win_all[c])
                r.g_big[c, 0] += nn(nt_, dh)
                hand_out(i, s, c, 0)
                return 0

            lax.fori_loop(0, E, inward, 0, unroll=True)
            return r.acc[...]

        def ffn_weights(kind):
            for i in range(NI):
                r.turned[i] = (r.cot[i] if kind == 1 else r.n[i, 2]).astype(F32).T.astype(BF16)

            def one(s, _):
                c = chunk_out(s)
                total = jnp.zeros((D, HB), F32)
                for i in range(NI):
                    total += nn(r.turned[i], (r.act if kind == 1 else r.dh)[i, c])
                r.g_big[c, kind] = total
                hand_out(NI - 1, s, c, kind)
                return 0

            lax.fori_loop(0, E, one, 0)

        def ffn_output(i):
            r.acc[...] = r.x2[i]

            def one(c, _):
                r.acc[...] += nn(r.act[i, c], r.wback_all[c])
                return 0

            lax.fori_loop(0, E, one, 0, unroll=True)
            r.o_layer[i] = r.acc[...].astype(BF16)

        def add_small(which, dgain, dshift):
            r.small[2 * which : 2 * which + 1] += dgain
            r.small[2 * which + 1 : 2 * which + 2] += dshift

        def qo_rows(a, c):
            at = pl.ds(pl.multiple_of(c * QB, QB), QB)
            return jnp.concatenate([r.g_qr[a, at], r.g_o[a, at]], 0)

        def qo_send(a):
            for x in range(X):
                r.a_qo[a, x] = qo_rows(a, x * 2 + (1 - core)).astype(BF16)
            aq_copy(a).start()

        def rows_around(o):
            return block_rows(lax.rem(dpi + o + 1, DP))

        def qo_sib(a):
            aq_copy(a).wait_recv()
            for o, x in enumerate(xpeers()):
                r.b_qo[a, o] = (qo_rows(a, chip(x)) + r.a_qo_r[a, x].astype(F32)).astype(BF16)
                bq_copy(a, o).start()

        def qo_over_x(a):
            total = qo_rows(a, me) + r.a_qo_r[a, xi].astype(F32)
            for o in range(X - 1):
                bq_copy(a, o).wait_recv()
                total = total + r.b_qo_r[a, o].astype(F32)
            r.own_qo[...] = total.T
            for o in range(DP - 1):
                r.c_qo[a, o] = r.own_qo[rows_around(o)].astype(BF16)
                cq_copy(a, o).start()
            r.qo_own[a] = r.own_qo[block_rows(dpi)]

        def qo_end(a):
            total = r.qo_own[a]
            for o in range(DP - 1):
                cq_copy(a, o).wait_recv()
                total = total + r.c_qo_r[a, o].astype(F32)
            return total

        kv_busy = enc | (core == 0)
        kv_sib_busy = enc | (core == 1)

        def kv_send():
            @pl.when(kv_sib_busy)
            def _():
                ka_copy().start()

        def kv_sib():
            @pl.when(kv_busy)
            def _():
                ka_copy().wait_recv()
                r.kv_sum[...] = r.g_kv[core] + r.kv_ar[...]
                for o in range(DP - 1):
                    r.c_kv[o] = r.kv_sum[rows_around(o)].astype(BF16)
                    ck_copy(o).start()

        def kv_over_dp():
            @pl.when(kv_busy)
            def _():
                total = r.kv_sum[block_rows(dpi)]
                for o in range(DP - 1):
                    ck_copy(o).wait_recv()
                    total = total + r.c_kv_r[o].astype(F32)
                r.kv_fin[...] = total
                r.kv_b[...] = total.astype(BF16)
                for o in range(X - 1):
                    kb_copy(o).start()

        def kv_over_x():
            @pl.when(kv_busy)
            def _():
                total = r.kv_fin[...]
                for o in range(X - 1):
                    kb_copy(o).wait_recv()
                    total = total + r.kv_br[o].astype(F32)
                r.kv_fin[...] = total
                kf_copy().start()

            @pl.when(enc & (core == 1))
            def _():
                ks_copy(0).start()
                ks_copy(1).start()

        def kv_end():
            @pl.when(kv_sib_busy)
            def _():
                kf_copy().wait_recv()

            @pl.when(dec)
            def _():
                ks_copy(core).wait_recv()
                r.o_kv[0] = jnp.where(core == 0, r.kv_fin[...], r.kv_sib[...])
                r.o_kv[1] = r.kv_sec[...]

            @pl.when(enc)
            def _():
                r.o_kv[0] = jnp.where(core == 0, r.kv_fin[...], r.kv_sib[...])
                r.o_kv[1] = jnp.where(core == 0, r.kv_sib[...], r.kv_fin[...])

        def small_sib():
            sa_copy().wait_recv()
            r.sm_fin[...] = r.small[...] + r.sm_ar[...]
            r.sm_b[...] = r.sm_fin[...].astype(BF16)
            for o in range(X - 1):
                sb_copy(o).start()

        def small_over_x():
            total = r.sm_fin[...]
            for o in range(X - 1):
                sb_copy(o).wait_recv()
                total = total + r.sm_br[o].astype(F32)
            r.sm_fin[...] = total
            r.za_sm[...] = total.astype(BF16)
            for o in range(DP - 1):
                zs_copy(o).start()

        def small_over_dp():
            total = r.sm_fin[:, lanes(dpi)]
            for o in range(DP - 1):
                zs_copy(o).wait_recv()
                total = total + r.za_sm_r[o].astype(F32)
            r.sm_own[...] = total

        def self_forward(i):
            x1 = attend(i, 0, r.kv_s, r.x[i].astype(F32))
            r.x1[i] = x1

            @pl.when(enc)
            def _():
                g, b = gain_of(2)
                r.n[i, 2] = norm_rows(r.x1[i], g, b).astype(BF16)

            @pl.when(dec)
            def _():
                g, b = gain_of(1)
                r.n[i, 1] = norm_rows(r.x1[i], g, b).astype(BF16)

        def encoded(i):
            mem = r.acc[...].astype(BF16)
            r.o_layer[i] = mem
            r.ckv_own[i] = nn(mem, r.ckv[...]).astype(BF16)
            for x in xpeers():
                ckv_copy(i, chip(x)).start()
            ckv_copy(i, me).start()

        gather_relay(q_of(0, 0))
        gather_take(q_of(0, 0))
        project_queries(0, 0)
        set_bias(0, 0)
        gather_relay(kv_of(0))
        gather_relay(q_of(0, 1))
        gather_take(kv_of(0))
        gather_take(q_of(0, 1))
        self_forward(0)
        def later_rows(i, _):
            project_queries(i, 0)
            set_bias(i, 0)
            gather_relay(kv_of(i))
            gather_take(kv_of(i))
            self_forward(i)
            return 0

        @pl.when(dec)
        def _():
            lax.fori_loop(1, NI, later_rows, 0)

        for q in range(NS):
            weights_over_x(0, q)
        for kind in (0, 1):
            sib_copy(kind, sib).wait_recv()

        @pl.when(enc)
        def _():
            r.acc[...] = r.x1[0]
            ffn_forward(0, 0, 2)

        for q in range(NS):
            weights_over_x(1, q)
            weights_over_z(0, q)
        for q in range(NS, NX):
            weights_over_x(0, q)
        for q in range(NS):
            weights_over_z(1, q)
        for q in range(NS, NX):
            weights_over_x(1, q)
        @pl.when(enc)
        def _():
            ffn_forward(0, 2, 3)

        for kind in (0, 1):
            weights_over_sib(kind)

        @pl.when(enc)
        def _():
            ffn_forward(0, 3, E)
            encoded(0)

        @pl.when(enc)
        def _():
            def later_outputs(i, _):
                later_rows(i, 0)
                r.acc[...] = r.x1[i]
                ffn_forward(i, 0, E)
                encoded(i)
                return 0

            lax.fori_loop(1, NI, later_outputs, 0)
            store("layer").start()

        r.small[...] = jnp.zeros_like(r.small)
        r.g_qr[...] = jnp.zeros_like(r.g_qr)
        r.g_o[...] = jnp.zeros_like(r.g_o)
        r.g_kv[...] = jnp.zeros_like(r.g_kv)

        def zero_big(c, _):
            r.g_big[c] = jnp.zeros((2, D, HB), F32)
            return 0

        lax.fori_loop(0, E, zero_big, 0)

        @pl.when(dec)
        def _():
            for kind in (0, 1):
                gather_relay(q_of(1, kind))
            for kind in (0, 1):
                gather_take(q_of(1, kind))

            def ahead(i, _):
                project_queries(i, 1)
                dz = r.cot[i]

                def one(c, _):
                    r.dh[i, c] = nt(dz, r.wback_all[c]).astype(BF16)
                    return 0

                lax.fori_loop(0, E, one, 0)
                return 0

            lax.fori_loop(0, NI, ahead, 0)

            def middle(i, _):
                set_bias(i, 1)
                ckv_gather(i)
                x2 = attend(i, 1, r.kv_c, r.x1[i])
                r.x2[i] = x2
                g, b = gain_of(2)
                r.n[i, 2] = norm_rows(x2, g, b).astype(BF16)
                dn = ffn_middle(i)
                dx, dg, db = norm_back(r.x2[i], g, dn)
                add_small(2, dg, db)
                r.o_ig[i] = r.cot[i].astype(F32) + dx
                dn = attend_back(i, 1, r.kv_c, r.o_ig[i], r.dckv_send)
                dckv_out(i)
                g, b = gain_of(1)
                dx, dg, db = norm_back(r.x1[i], g, dn)
                add_small(1, dg, db)
                r.o_ig[i] += dx
                return 0

            lax.fori_loop(0, NI, middle, 0)

            qo_send(1)

        def backward(i, _):
            @pl.when(enc)
            def _():
                total = jnp.zeros((L, 2 * HD), F32)
                for x in range(X):
                    dckv_copy(i, x, x).wait_recv()
                    total = total + r.dckv_recv[i, x].astype(F32)
                dkv = total.astype(BF16)
                dmem = nt(dkv, r.ckv[...]).astype(BF16).astype(F32)
                dx = r.cot[i].astype(F32) + dmem
                r.o_ig[i] = dx
                r.dz[i] = dx.astype(BF16)
                dn = ffn_back(i)
                r.g_kv[1] += tn(r.o_layer[i], dkv)
                g, b = gain_of(2)
                dx, dg, db = norm_back(r.x1[i], g, dn)
                add_small(2, dg, db)
                r.o_ig[i] += dx

            first = i == 0
            last = i == NI - 1

            @pl.when(dec & first)
            def _():
                ffn_weights(1)

            r.dn[i] = attend_back(i, 0, r.kv_s, r.o_ig[i], r.dkv_send)

            @pl.when(dec & first)
            def _():
                big_sib(1)
                qo_sib(1)
                big_send(1, 0, HP)

            dkv_out(i)

            @pl.when(dec & first)
            def _():
                ffn_weights(0)

            @pl.when(last)
            def _():
                big_send(1, HP, DP - 1)
                big_sib(0)
                big_send(0, 0, HP)
                qo_send(0)

            return 0

        lax.fori_loop(0, NI, backward, 0)
        for kind in (1, 0):
            big_sib_own(kind)
        for s in range(HP):
            big_over_x(1, s)

        @pl.when(dec)
        def _():
            qo_over_x(1)

        def first_layer(i, _):
            dkv = dkv_in(i).astype(BF16)
            r.g_kv[0] += tn(r.n[i, 0], dkv)
            dn = r.dn[i] + nt(dkv, r.wkv[...])
            g, b = gain_of(0)
            dx, dg, db = norm_back(r.x[i].astype(F32), g, dn)
            add_small(0, dg, db)
            r.o_ig[i] += dx
            return 0

        lax.fori_loop(0, NI, first_layer, 0)
        store("ig").start()

        for a in range(2):
            r.small[6 + a * NE : 6 + (a + 1) * NE] = r.g_qr[a, NQ : NQ + NE]
        sa_copy().start()
        kv_send()

        qo_sib(0)
        small_sib()
        kv_sib()

        big_send(0, HP, DP - 1)
        for s in range(HP, DP - 1):
            big_over_x(1, s)
        for s in range(HP):
            big_over_x(0, s)

        @pl.when(dec)
        def _():
            def output(i, _):
                ffn_output(i)
                return 0

            lax.fori_loop(0, NI, output, 0)
            store("layer").start()

        small_over_x()

        qo_over_x(0)
        kv_over_dp()
        for kind in (1, 0):
            big_send(kind, DP - 1, DP)
        for s in range(HP, DP - 1):
            big_over_x(0, s)
        small_over_dp()

        @pl.when(dec)
        def _():
            sec_copy(1).start()
            r.qo_fin[...] = qo_end(1)
            sec_copy(0).start()
            r.o_qo[1] = r.qo_fin[...]
            r.o_small[...] = r.sm_own[...]

        for kind in (1, 0):
            big_over_x(kind, DP - 1)
        kv_over_x()
        r.o_qo[0] = qo_end(0)
        big_end(1, r.o_back)
        big_end(0, r.o_in)
        kv_end()

        @pl.when(enc)
        def _():
            sec_copy(1).wait_recv()
            sec_copy(0).wait_recv()
            r.o_qo[1] = r.qo_sec[...]
            rows = lax.broadcasted_iota(jnp.int32, (SR, 128), 0)
            theirs = ((rows >= 2) & (rows < 4)) | ((rows >= 6 + NE) & (rows < 6 + 2 * NE))
            r.o_small[...] = jnp.where(theirs, r.sm_sec[...], r.sm_own[...])

        store("layer").wait()
        store("ig").wait()
        for kind in (0, 1):
            gather_sent(q_of(0, kind))
            for x in range(X):
                a_copy(kind, x).wait_send()
            for h in range(NH):
                for o in range(X - 1):
                    for d in range(DP):
                        b_copy(kind, o, d, h).wait_send()
                for k in range(HP):
                    zab_copy(kind, k, h).wait_send()
                for k in range(1, HP):
                    zbb_copy(kind, k, h).wait_send()
        weights_sent()
        sa_copy().wait_send()
        for o in range(X - 1):
            sb_copy(o).wait_send()
        for o in range(DP - 1):
            zs_copy(o).wait_send()

        def qo_sent(a):
            aq_copy(a).wait_send()
            for o in range(X - 1):
                bq_copy(a, o).wait_send()
            for o in range(DP - 1):
                cq_copy(a, o).wait_send()

        qo_sent(0)

        @pl.when(dec)
        def _():
            for kind in (0, 1):
                gather_sent(q_of(1, kind))
                sec_copy(kind).wait_send()
            qo_sent(1)

        @pl.when(kv_sib_busy)
        def _():
            ka_copy().wait_send()

        @pl.when(kv_busy)
        def _():
            for o in range(X - 1):
                kb_copy(o).wait_send()
            for o in range(DP - 1):
                ck_copy(o).wait_send()
            kf_copy().wait_send()

        @pl.when(enc & (core == 1))
        def _():
            ks_copy(0).wait_send()
            ks_copy(1).wait_send()

        def sent(i, _):
            gather_sent(kv_of(i))
            for x in xpeers():
                dkv_copy(i, x, xi).wait_send()
            for x in range(X):
                dksum_copy(i, x).wait_send()

            @pl.when(enc)
            def _():
                for x in range(X):
                    ckv_copy(i, chip(x)).wait_send()

            @pl.when(dec)
            def _():
                for x in range(X):
                    ckv_relay(i, chip(x)).wait_send()
                    dsum_copy(i, x).wait_send()
                    dckv_copy(i, x, xi).wait_send()

            return 0

        lax.fori_loop(0, NI, sent, 0)

    return kernel


def make_finish(E, NE, EB, QB):
    def kernel(
        layer, grads, w_in, w_back, qo, kv, small, o_layer, o_grads, o_gain, o_bias, o_kv, o_router,
        o_query, o_out, o_w_in, o_w_back, o_cgain, o_cbias, o_ckv, o_crouter, o_cquery, o_cout,
    ):
        me = lax.axis_index("expert")
        o_layer[...] = layer[...]
        o_grads[...] = grads[...]
        o_w_in[...] = w_in[...]
        o_w_back[...] = w_back[...].T
        for a, (q, o) in enumerate(((o_query, o_out), (o_cquery, o_cout))):
            both = qo[a].T
            q[...] = both[:QB]
            o[...] = both[QB:]
        for a, out in enumerate((o_kv, o_ckv)):
            total = kv[a, :EB]
            for j in range(1, E):
                total = jnp.where(me == j, kv[a, j * EB : (j + 1) * EB], total)
            out[...] = total
        off = (lax.axis_index("dp") * E + me) * EB
        part = pltpu.roll(small[...], lax.rem(128 - lax.rem(off, 128), 128), 1)[:, :EB]
        o_gain[0] = jnp.concatenate([part[0:1], part[4:5]], 0)
        o_bias[0] = jnp.concatenate([part[1:2], part[5:6]], 0)
        o_cgain[...] = part[2:3]
        o_cbias[...] = part[3:4]
        o_router[...] = part[6 : 6 + NE]
        o_crouter[...] = part[6 + NE : 6 + 2 * NE]

    return kernel


def body(
    inputs, cotangents, pair_ids, self_routes, cross_routes, norm_gain, norm_bias, w_kv, w_router,
    w_query, w_out, w_in, w_back, cross_gain, cross_bias, cross_kv, cross_router, cross_query,
    cross_out,
):
    E = lax.axis_size("expert")
    DP = lax.axis_size("dp")
    _, MB, R, L, D = inputs.shape
    NI = MB * R
    SEQ = pair_ids.shape[-1]
    T = self_routes.shape[-1]
    NE = w_router.shape[-1]
    HD = w_query.shape[-1]
    HB = w_in.shape[-1]
    npd = NE // E
    QB = npd * HD
    dims = (NI, L, D, SEQ, T, NE, HD, HB, E, DP)
    ins, outs, bufs, sems = make_plan(dims)

    operands = [
        inputs.reshape(NI, L, D),
        cotangents.reshape(NI, L, D),
        pair_ids.reshape(2, NI, 1, SEQ),
        jnp.swapaxes(self_routes.reshape(NI, SEQ, T), 1, 2),
        jnp.swapaxes(cross_routes.reshape(NI, SEQ, T), 1, 2),
        norm_gain[0],
        norm_bias[0],
        w_kv[0],
        w_router[0].T,
        jnp.swapaxes(w_query[0], 1, 2),
        w_out[0],
        w_in[0],
        w_back[0],
        cross_gain[None],
        cross_bias[None],
        cross_kv,
        cross_router.T,
        jnp.swapaxes(cross_query, 1, 2),
        cross_out,
    ]
    vmem = pl.BlockSpec(memory_space=pltpu.VMEM)
    anywhere = pl.BlockSpec(memory_space=pl.ANY)
    res = pl.pallas_call(
        make_kernel(dims),
        out_shape=[jax.ShapeDtypeStruct(s, t) for s, t in outs.values()],
        in_specs=[vmem if n in STAY else anywhere for n in ins],
        out_specs=[anywhere if n[:4] == "out_" else vmem for n in outs],
        scratch_shapes=[pltpu.VMEM(s, t) for s, t in bufs.values()]
        + [pltpu.SemaphoreType.DMA(s) for s in sems.values()]
        + [pltpu.VMEM(o.shape, o.dtype) for n, o in zip(ins, operands) if n in fetched(ins)],
        compiler_params=pltpu.CompilerParams(
            collective_id=0, has_side_effects=True, vmem_limit_bytes=62 * 1024 * 1024
        ),
        name="layers",
    )(*operands)
    DB = D // DP
    EB = DB // E
    shapes = [
        ((NI, L, D), BF16),
        ((NI, L, D), F32),
        ((1, 2, EB), F32),
        ((1, 2, EB), F32),
        ((EB, 2 * HD), F32),
        ((NE, EB), F32),
        ((QB, DB), F32),
        ((QB, DB), F32),
        ((DB, HB), F32),
        ((HB, DB), F32),
        ((1, EB), F32),
        ((1, EB), F32),
        ((EB, 2 * HD), F32),
        ((NE, EB), F32),
        ((QB, DB), F32),
        ((QB, DB), F32),
    ]
    (
        layer, grads, gain, bias, kv, router, query, out, w_in_g, w_back_g, c_gain, c_bias, c_kv,
        c_router, c_query, c_out,
    ) = pl.pallas_call(
        make_finish(E, NE, EB, QB),
        out_shape=[jax.ShapeDtypeStruct(s, t) for s, t in shapes],
        in_specs=[vmem] * len(outs),
        out_specs=[vmem] * len(shapes),
        name="results",
    )(*res)

    def of_query(g):
        return jnp.swapaxes(g.reshape(npd, HD, DB), 1, 2)

    def of_out(g):
        return g.reshape(npd, HD, DB)

    return (
        layer.reshape(inputs.shape),
        grads.reshape(inputs.shape),
        gain,
        bias,
        kv[None],
        router.T[None],
        of_query(query)[None],
        of_out(out)[None],
        w_in_g[None],
        w_back_g[None],
        c_gain[0],
        c_bias[0],
        c_kv,
        c_router.T,
        of_query(c_query),
        of_out(c_out),
    )


def solution(mesh):
    placed = (
        P("section", None, "dp", "expert", None),
        P("section", None, "dp", "expert", None),
        P(None, None, "dp", None),
        P("section", None, "dp", None, None),
        P(None, "dp", None, None),
        P("section", None, None),
        P("section", None, None),
        P("section", None, None),
        P("section", None, None),
        P("section", "expert", None, None),
        P("section", "expert", None, None),
        P("section", None, "expert"),
        P("section", "expert", None),
        P(),
        P(),
        P(),
        P(),
        P("expert", None, None),
        P("expert", None, None),
    )
    return jax.shard_map(
        body,
        mesh=mesh,
        in_specs=placed,
        out_specs=(
            P("section", None, "dp", "expert", None),
            P("section", None, "dp", "expert", None),
            P("section", None, ("dp", "expert")),
            P("section", None, ("dp", "expert")),
            P("section", ("dp", "expert"), None),
            P("section", ("dp", "expert"), None),
            P("section", "expert", "dp", None),
            P("section", "expert", None, "dp"),
            P("section", "dp", "expert"),
            P("section", "expert", "dp"),
            P(("dp", "expert")),
            P(("dp", "expert")),
            P(("dp", "expert"), None),
            P(("dp", "expert"), None),
            P("expert", "dp", None),
            P("expert", None, "dp"),
        ),
        check_vma=False,
    )
```

```python
from types import SimpleNamespace

import jax
import jax.numpy as jnp
from jax import lax
from jax.experimental import pallas as pl
from jax.experimental.pallas import tpu as pltpu
from jax.sharding import PartitionSpec as P

F32 = jnp.float32
BF16 = jnp.bfloat16
MESH = pl.DeviceIdType.MESH
RT = 16
SR = 32
NP = 8
NS = 3
NX = NP - NS
NH = 2


def nn(a, b):
    return lax.dot_general(a, b, (((1,), (0,)), ((), ())), preferred_element_type=F32)


def nt(a, b):
    return lax.dot_general(a, b, (((1,), (1,)), ((), ())), preferred_element_type=F32)


def tn(a, b):
    return lax.dot_general(a, b, (((0,), (0,)), ((), ())), preferred_element_type=F32)


def gelu_parts(h):
    c = 0.7978845608028654
    a = c + (c * 0.044715) * (h * h)
    t = jnp.tanh(h * a)
    half = 0.5 + 0.5 * t
    act = h * half
    return act, half + act * ((1.0 - t) * (3.0 * a - 2.0 * c))


def norm_stats(x):
    centred = x - jnp.mean(x, -1, keepdims=True)
    r = lax.rsqrt(jnp.mean(centred * centred, -1, keepdims=True) + 1e-05)
    return centred * r, r


def norm_back(x, gain, grad):
    xhat, r = norm_stats(x)
    gg = grad * gain
    m1 = jnp.mean(gg, -1, keepdims=True)
    m2 = jnp.mean(gg * xhat, -1, keepdims=True)
    return (
        r * (gg - m1 - xhat * m2),
        jnp.sum(grad * xhat, 0, keepdims=True),
        jnp.sum(grad, 0, keepdims=True),
    )


INS = [
    "x", "cot", "pairs", "routes_s", "routes_c", "ng", "nb", "wkv", "wr", "wq", "wo", "win",
    "wback", "cg", "cb", "ckv", "cr", "cq", "co",
]
STAY = ("wr", "cr")
PLACED = ("win", "wback")


def fetched(ins):
    return [n for n in ins if n not in STAY + PLACED]


def make_plan(dims):
    (NI, L, D, SEQ, T, NE, HD, HB, E, DP) = dims
    npd = NE // E
    QB = npd * HD
    NQ = NE * HD
    X = E // 2
    DB = D // DP
    HP = DP // 2
    ins = INS
    outs = dict(
        out_layer=((NI, L, D), BF16),
        out_ig=((NI, L, D), F32),
        o_in=((DB, HB), F32),
        o_back=((DB, HB), F32),
        o_qo=((2, DB, 2 * QB), F32),
        o_kv=((2, DB, 2 * HD), F32),
        o_small=((SR, 128), F32),
    )
    bufs = dict(
        o_layer=((NI, L, D), BF16),
        o_ig=((NI, L, D), F32),
        win_all=((E, D, HB), BF16),
        wback_all=((E, HB, D), BF16),
        wqr=((2, NQ + RT, D), BF16),
        wo_all=((2, NQ, D), BF16),
        wr_pad=((RT, D), F32),
        x1=((NI, L, D), F32),
        x2=((NI, L, D), F32),
        n=((NI, 3, L, D), BF16),
        dz=((NI, L, D), BF16),
        acc=((L, D), F32),
        dn=((NI, L, D), F32),
        act=((NI, E, L, HB), BF16),
        turned=((NI, D, L), BF16),
        dh=((NI, E, L, HB), BF16),
        kv_s=((NI, SEQ, 2 * HD), BF16),
        kv_c=((NI, SEQ, 2 * HD), BF16),
        kvt=((2, NI, 2 * HD, SEQ), BF16),
        bias=((SEQ, L), F32),
        qt=((2, NI, T, HD, L), BF16),
        gate=((2, NI, T, 8, L), F32),
        inv=((2, NI, T, 8, L), F32),
        p=((2, NI, T, SEQ, L), BF16),
        heads=((2, NI, T, HD, L), F32),
        ht=((2, NI, NQ, L), BF16),
        dq=((T, HD, L), BF16),
        dkv_acc=((SEQ, 2 * HD), F32),
        dkv_own=((NI, L, 2 * HD), F32),
        dkv_send=((NI, SEQ, 2 * HD), BF16),
        dkv_recv=((NI, X, L, 2 * HD), BF16),
        dksum_r=((NI, X, L, 2 * HD), BF16),
        dckv_send=((NI, SEQ, 2 * HD), BF16),
        dckv_recv=((NI, X, L, 2 * HD), BF16),
        dsum_r=((NI, X, L, 2 * HD), BF16),
        ckv_own=((NI, L, 2 * HD), BF16),
        g_big=((E, 2, D, HB), F32),
        g_qr=((2, NQ + RT, D), F32),
        g_o=((2, NQ, D), F32),
        g_kv=((2, D, 2 * HD), F32),
        small=((SR, D), F32),
        a_big=((2, X, D, HB), BF16),
        a_big_r=((2, X, D, HB), BF16),
        a_qo=((2, X, 2 * QB, D), BF16),
        a_qo_r=((2, X, 2 * QB, D), BF16),
        b_big=((X - 1, 2, D, HB), BF16),
        b_big_r=((X - 1, 2, D, HB), BF16),
        za_big=((2, HP, DB, HB), BF16),
        za_big_r=((2, HP, DB, HB), BF16),
        zb_big=((2, HP - 1, DB, HB), BF16),
        zb_big_r=((2, HP - 1, DB, HB), BF16),
        b_qo=((2, X - 1, 2 * QB, D), BF16),
        b_qo_r=((2, X - 1, 2 * QB, D), BF16),
        own_qo=((D, 2 * QB), F32),
        c_qo=((2, DP - 1, DB, 2 * QB), BF16),
        c_qo_r=((2, DP - 1, DB, 2 * QB), BF16),
        qo_own=((2, DB, 2 * QB), F32),
        kv_ar=((D, 2 * HD), F32),
        kv_sum=((D, 2 * HD), F32),
        c_kv=((DP - 1, DB, 2 * HD), BF16),
        c_kv_r=((DP - 1, DB, 2 * HD), BF16),
        kv_b=((DB, 2 * HD), BF16),
        kv_br=((X - 1, DB, 2 * HD), BF16),
        kv_fin=((DB, 2 * HD), F32),
        kv_sib=((DB, 2 * HD), F32),
        kv_sec=((DB, 2 * HD), F32),
        sm_ar=((SR, D), F32),
        sm_b=((SR, D), BF16),
        sm_br=((X - 1, SR, D), BF16),
        za_sm=((SR, D), BF16),
        za_sm_r=((DP - 1, SR, 128), BF16),
        sm_own=((SR, 128), F32),
        sm_fin=((SR, D), F32),
        sm_sec=((SR, 128), F32),
        qo_fin=((DB, 2 * QB), F32),
        qo_sec=((DB, 2 * QB), F32),
    )
    sems = dict(
        q_s=(2, 2, E), q_r=(2, 2, E),
        sib_s=(2,), sib_r=(2,),
        wx_s=(2, X, NX), wx_r=(2, X, NX),
        wz_s=(2, X, NS), wz_r=(2, X, NS),
        wf_s=(2, X, NP), wf_r=(2, X, NP),
        kv_ss=(NI, E), kv_rs=(NI, E),
        ckv_s=(NI, E), ckv_r=(NI, E),
        dckv_s=(NI, X), dckv_r=(NI, X),
        dsum_ss=(NI, X), dsum_rs=(NI, X),
        dkv_s=(NI, X), dkv_r=(NI, X),
        dksum_ss=(NI, X), dksum_rs=(NI, X),
        a_s=(2, X), a_r=(2, X),
        b_s=(X - 1, 2, DP, NH), b_r=(X - 1, 2, DP, NH),
        zab_s=(2, HP, NH), zab_r=(2, HP, NH),
        zbb_s=(2, HP, NH), zbb_r=(2, HP, NH),
        aq_s=(2,), aq_r=(2,),
        cq_s=(2, DP - 1), cq_r=(2, DP - 1),
        bq_s=(2, X - 1), bq_r=(2, X - 1),
        ka_s=(1,), ka_r=(1,),
        kb_s=(X - 1,), kb_r=(X - 1,),
        ck_s=(DP - 1,), ck_r=(DP - 1,),
        kf_s=(3,), kf_r=(2,),
        sa_s=(1,), sa_r=(1,),
        sb_s=(X - 1,), sb_r=(X - 1,),
        zs_s=(DP - 1,), zs_r=(DP - 1,),
        sec_s=(2,), sec_r=(2,),
        ld=(len(ins) + 2,),
    )
    return ins, outs, bufs, sems


def make_kernel(dims):
    (NI, L, D, SEQ, T, NE, HD, HB, E, DP) = dims
    npd = NE // E
    QB = npd * HD
    NQ = NE * HD
    X = E // 2
    DB = D // DP
    HP = DP // 2
    scale = HD ** -0.5
    ins, outs, bufs, sems = make_plan(dims)
    names = [n if n in STAY else "in_" + n for n in ins]
    names += list(outs) + list(bufs) + list(sems) + fetched(ins)

    def kernel(*refs):
        r = SimpleNamespace(**dict(zip(names, refs)))
        sec = lax.axis_index("section")
        dpi = lax.axis_index("dp")
        me = lax.axis_index("expert")
        core = lax.rem(me, 2)
        xi = me // 2
        sib = xi * 2 + (1 - core)
        dec = sec == 1
        enc = sec == 0
        other = 1 - sec
        half = lax.rem(dpi, 2)
        mate = dpi + 1 - 2 * half
        row0 = pl.multiple_of(me * L, L)

        def to_expert(j):
            return (sec, dpi, j)

        def to_dp(j):
            return (sec, j, me)

        def to_section(j):
            return (other, dpi, j)

        def rcopy(src, dst, ssem, rsem, dev):
            return pltpu.make_async_remote_copy(
                src_ref=src, dst_ref=dst, send_sem=ssem, recv_sem=rsem, device_id=dev,
                device_id_type=MESH,
            )

        def chip(x):
            return x * 2 + core

        def q_copy(a, kind, block, to, slot):
            ref = r.wqr if kind == 0 else r.wo_all
            ref = ref.at[a, pl.ds(pl.multiple_of(block * QB, QB), QB)]
            return rcopy(ref, ref, r.q_s.at[a, kind, slot], r.q_r.at[a, kind, block], to_expert(to))

        def w_ref(kind, c):
            return (r.win_all if kind == 0 else r.wback_all).at[c]

        def w_piece(kind, c, p):
            rows = (D if kind == 0 else HB) // NP
            return w_ref(kind, c).at[pl.ds(pl.multiple_of(p * rows, rows), rows)]

        def sib_copy(kind, c):
            ref = w_ref(kind, c)
            return rcopy(ref, ref, r.sib_s.at[kind], r.sib_r.at[kind], to_expert(sib))

        def shared(q, parity):
            return NS * parity + q

        def over_x_at(q):
            return shared(q, half) if q < NS else NS + q

        def wx_copy(kind, c, q, to_x, frm_x):
            ref = w_piece(kind, c, over_x_at(q))
            return rcopy(
                ref, ref, r.wx_s.at[kind, to_x, q], r.wx_r.at[kind, frm_x, q],
                to_expert(chip(to_x)),
            )

        def wz_copy(kind, x, q, parity):
            ref = w_piece(kind, chip(x), shared(q, parity))
            return rcopy(ref, ref, r.wz_s.at[kind, x, q], r.wz_r.at[kind, x, q], to_dp(mate))

        def wf_copy(kind, c, x, p):
            ref = w_piece(kind, c, p)
            return rcopy(ref, ref, r.wf_s.at[kind, x, p], r.wf_r.at[kind, x, p], to_expert(sib))

        def rows_of(ref, i, j):
            return ref.at[i, pl.ds(pl.multiple_of(j * L, L), L)]

        def kv_copy(i, block, to, slot):
            ref = rows_of(r.kv_s, i, block)
            return rcopy(ref, ref, r.kv_ss.at[i, slot], r.kv_rs.at[i, block], to_expert(to))

        def ckv_copy(i, to):
            return rcopy(
                r.ckv_own.at[i], rows_of(r.kv_c, i, me), r.ckv_s.at[i, to], r.ckv_r.at[i, me],
                to_section(to),
            )

        def ckv_relay(i, block):
            ref = rows_of(r.kv_c, i, block)
            return rcopy(ref, ref, r.ckv_s.at[i, block], r.ckv_r.at[i, block], to_expert(sib))

        def ckv_gather(i):
            same = xpeers() + [xi]
            for x in same:
                ckv_relay(i, chip(x)).wait_recv()
                ckv_relay(i, chip(x)).start()
            for x in same:
                ckv_relay(i, x * 2 + 1 - core).wait_recv()

        def dsum_copy(i, x):
            at = x * 2 + 1 - core
            return rcopy(
                rows_of(r.dckv_send, i, at), r.dsum_r.at[i, x], r.dsum_ss.at[i, x],
                r.dsum_rs.at[i, x], to_expert(sib),
            )

        def dckv_copy(i, to_x, frm_x):
            return rcopy(
                rows_of(r.dckv_send, i, chip(to_x)), r.dckv_recv.at[i, frm_x],
                r.dckv_s.at[i, to_x], r.dckv_r.at[i, frm_x], to_section(chip(to_x)),
            )

        def dckv_out(i):
            order = xpeers() + [xi]
            for x in order:
                dsum_copy(i, x).start()
            for x in order:
                dsum_copy(i, x).wait_recv()
                at = pl.ds(pl.multiple_of(chip(x) * L, L), L)
                r.dckv_send[i, at] = (
                    r.dkv_acc[at] + r.dsum_r[i, x].astype(F32)
                ).astype(BF16)
                dckv_copy(i, x, xi).start()

        def dksum_copy(i, x):
            at = x * 2 + 1 - core
            return rcopy(
                rows_of(r.dkv_send, i, at), r.dksum_r.at[i, x], r.dksum_ss.at[i, x],
                r.dksum_rs.at[i, x], to_expert(sib),
            )

        def dkv_copy(i, to_x, frm_x):
            return rcopy(
                rows_of(r.dkv_send, i, chip(to_x)), r.dkv_recv.at[i, frm_x], r.dkv_s.at[i, to_x],
                r.dkv_r.at[i, frm_x], to_expert(chip(to_x)),
            )

        def dkv_out(i):
            for x in xpeers() + [xi]:
                dksum_copy(i, x).start()
            r.dkv_own[i] = r.dkv_acc[pl.ds(row0, L)]
            for x in xpeers():
                dksum_copy(i, x).wait_recv()
                at = pl.ds(pl.multiple_of(chip(x) * L, L), L)
                r.dkv_send[i, at] = (r.dkv_acc[at] + r.dksum_r[i, x].astype(F32)).astype(BF16)
                dkv_copy(i, x, xi).start()

        def dkv_in(i):
            dksum_copy(i, xi).wait_recv()
            total = r.dkv_own[i] + r.dksum_r[i, xi].astype(F32)
            for x in xpeers():
                dkv_copy(i, x, x).wait_recv()
                total = total + r.dkv_recv[i, x].astype(F32)
            return total

        def over_x(src, dst, ssem, rsem, o):
            return rcopy(src, dst, ssem, rsem, to_expert(chip(lax.rem(xi + o + 1, X))))

        def to_mate(src, dst, ssem, rsem):
            return rcopy(src, dst, ssem, rsem, to_dp(mate))

        def mates_at(k):
            return lax.rem(dpi // 2 + k, HP) * 2 + 1 - half

        def mine_at(k):
            return lax.rem(dpi // 2 + k, HP) * 2 + half

        def over_dp(src, dst, ssem, rsem, k):
            return rcopy(src, dst, ssem, rsem, to_dp(mine_at(k)))

        def over_sib(src, dst, ssem, rsem):
            return rcopy(src, dst, ssem, rsem, to_expert(sib))

        def a_copy(kind, x):
            return over_sib(
                r.a_big.at[kind, x], r.a_big_r.at[kind, x], r.a_s.at[kind, x], r.a_r.at[kind, x]
            )

        def block_rows(d):
            return pl.ds(pl.multiple_of(d * DB, DB), DB)

        HB_ROWS = DB // NH

        def part_rows(d, h):
            return pl.ds(pl.multiple_of(d * DB + h * HB_ROWS, HB_ROWS), HB_ROWS)

        def sub_rows(h):
            return pl.ds(h * HB_ROWS, HB_ROWS)

        def b_copy(kind, o, d, h):
            return over_x(
                r.b_big.at[o, kind, part_rows(d, h)], r.b_big_r.at[o, kind, part_rows(d, h)],
                r.b_s.at[o, kind, d, h], r.b_r.at[o, kind, d, h], o,
            )

        def zab_copy(kind, k, h):
            return to_mate(
                r.za_big.at[kind, k, sub_rows(h)], r.za_big_r.at[kind, k, sub_rows(h)],
                r.zab_s.at[kind, k, h], r.zab_r.at[kind, k, h],
            )

        def zbb_copy(kind, k, h):
            return over_dp(
                r.zb_big.at[kind, k - 1, sub_rows(h)], r.zb_big_r.at[kind, k - 1, sub_rows(h)],
                r.zbb_s.at[kind, k, h], r.zbb_r.at[kind, k, h], k,
            )

        def aq_copy(a):
            return over_sib(r.a_qo.at[a], r.a_qo_r.at[a], r.aq_s.at[a], r.aq_r.at[a])

        def around(src, dst, ssem, rsem, o):
            return rcopy(src, dst, ssem, rsem, to_dp(lax.rem(dpi + o + 1, DP)))

        def cq_copy(a, o):
            return around(
                r.c_qo.at[a, o], r.c_qo_r.at[a, o], r.cq_s.at[a, o], r.cq_r.at[a, o], o
            )

        def bq_copy(a, o):
            return over_x(
                r.b_qo.at[a, o], r.b_qo_r.at[a, o], r.bq_s.at[a, o], r.bq_r.at[a, o], o
            )

        def ka_copy():
            return over_sib(r.g_kv.at[1 - core], r.kv_ar, r.ka_s.at[0], r.ka_r.at[0])

        def kb_copy(o):
            return over_x(r.kv_b, r.kv_br.at[o], r.kb_s.at[o], r.kb_r.at[o], o)

        def ck_copy(o):
            return around(r.c_kv.at[o], r.c_kv_r.at[o], r.ck_s.at[o], r.ck_r.at[o], o)

        def kf_copy():
            return over_sib(r.kv_fin, r.kv_sib, r.kf_s.at[0], r.kf_r.at[0])

        def ks_copy(to_core):
            return rcopy(
                r.kv_fin, r.kv_sec, r.kf_s.at[1 + to_core], r.kf_r.at[1],
                to_section(xi * 2 + to_core),
            )

        def sa_copy():
            return over_sib(r.small, r.sm_ar, r.sa_s.at[0], r.sa_r.at[0])

        def sb_copy(o):
            return over_x(r.sm_b, r.sm_br.at[o], r.sb_s.at[o], r.sb_r.at[o], o)

        def lanes(d):
            return pl.ds(pl.multiple_of(d * DB // 128 * 128, 128), 128)

        def zs_copy(o):
            src = r.za_sm.at[:, lanes(lax.rem(dpi + o + 1, DP))]
            return around(src, r.za_sm_r.at[o], r.zs_s.at[o], r.zs_r.at[o], o)

        def sec_copy(kind):
            src, dst = ((r.qo_fin, r.qo_sec), (r.sm_own, r.sm_sec))[kind]
            return rcopy(src, dst, r.sec_s.at[kind], r.sec_r.at[kind], to_section(me))

        def peers():
            return [lax.rem(me + o, E) for o in range(1, E)]

        def xpeers():
            return [lax.rem(xi + o, X) for o in range(1, X)]

        def dpeers():
            return [lax.rem(dpi + o, DP) for o in range(1, DP)]

        def load(name):
            src = getattr(r, "in_" + name)
            if name in PLACED:
                dst = w_ref(PLACED.index(name), me)
            else:
                dst = getattr(r, name)
            return pltpu.make_async_copy(src, dst, r.ld.at[ins.index(name)])

        def store(name):
            k = ("layer", "ig").index(name)
            src, dst = getattr(r, "o_" + name), getattr(r, "out_" + name)
            return pltpu.make_async_copy(src, dst, r.ld.at[len(ins) + k])

        soon = ["x", "ng", "nb", "wkv", "wq", "wo"]
        early = soon + ["win", "wback", "pairs", "routes_s"]
        late = [n for n in ins if n not in early and n not in STAY]
        for name in early + late:
            load(name).start()
        barrier = pltpu.get_barrier_semaphore()
        for j in peers():
            pl.semaphore_signal(barrier, inc=1, device_id=to_expert(j), device_id_type=MESH)
        for j in dpeers():
            pl.semaphore_signal(barrier, inc=1, device_id=to_dp(j), device_id_type=MESH)
        for j in range(E):
            pl.semaphore_signal(barrier, inc=1, device_id=to_section(j), device_id_type=MESH)

        def gather_send(copy):
            copy(me, sib, sib).start()
            for x in xpeers():
                copy(me, chip(x), chip(x)).start()

        def gather_relay(copy):
            for x in xpeers():
                copy(chip(x), sib, x * 2 + 1 - core).wait_recv()
                copy(chip(x), sib, x * 2 + 1 - core).start()

        def gather_take(copy):
            copy(sib, sib, sib).wait_recv()
            for x in xpeers():
                c = x * 2 + 1 - core
                copy(c, sib, c).wait_recv()

        def gather_sent(copy):
            copy(me, sib, sib).wait_send()
            for x in xpeers():
                copy(me, chip(x), chip(x)).wait_send()
                copy(chip(x), sib, x * 2 + 1 - core).wait_send()

        def q_of(a, kind):
            return lambda block, to, slot: q_copy(a, kind, block, to, slot)

        def kv_of(i):
            return lambda block, to, slot: kv_copy(i, block, to, slot)

        def norm_rows(x, gain, shift):
            return norm_stats(x)[0] * gain + shift

        def gain_of(which):
            if which == 1:
                return r.cg[...], r.cb[...]
            return r.ng[which // 2 : which // 2 + 1], r.nb[which // 2 : which // 2 + 1]

        def own_query_weights(a, q_ref, o_ref, wr_ref):
            for j in range(npd):
                at = pl.multiple_of(me * QB + j * HD, HD)
                r.wqr[a, pl.ds(at, HD)] = q_ref[j]
                r.wo_all[a, pl.ds(at, HD)] = o_ref[j]
            r.wr_pad[...] = jnp.zeros_like(r.wr_pad)
            r.wr_pad[:NE] = wr_ref[...].astype(F32)
            r.wqr[a, pl.ds(NQ, RT)] = r.wr_pad[...].astype(BF16)

        def first_norm(i):
            g, b = gain_of(0)
            n = norm_rows(r.x[i].astype(F32), g, b).astype(BF16)
            r.n[i, 0] = n
            r.kv_s[i, pl.ds(row0, L)] = nn(n, r.wkv[...]).astype(BF16)

        for name in soon:
            load(name).wait()
        own_query_weights(0, r.wq, r.wo, r.wr)
        first_norm(0)
        pl.semaphore_wait(barrier, (E - 1) + (DP - 1) + E)

        gather_send(q_of(0, 0))
        gather_send(kv_of(0))
        gather_send(q_of(0, 1))
        def later_norms(i, _):
            first_norm(i)
            gather_send(kv_of(i))
            return 0

        @pl.when(dec)
        def _():
            lax.fori_loop(1, NI, later_norms, 0)

        for name in PLACED:
            load(name).wait()
        for kind in (0, 1):
            sib_copy(kind, me).start()
        for part in (range(NS), range(NS, NX)):
            for kind in (0, 1):
                for q in part:
                    for x in xpeers():
                        wx_copy(kind, me, q, x, xi).start()

        @pl.when(enc)
        def _():
            lax.fori_loop(1, NI, later_norms, 0)

        for name in late + ["pairs", "routes_s"]:
            load(name).wait()
        own_query_weights(1, r.cq, r.co, r.cr)

        @pl.when(dec)
        def _():
            for kind in (0, 1):
                gather_send(q_of(1, kind))

        def weights_over_x(kind, q):
            for x in xpeers():
                wx_copy(kind, chip(x), q, x, x).wait_recv()
                if q < NS:
                    wz_copy(kind, x, q, half).start()
                wf_copy(kind, chip(x), x, over_x_at(q)).start()

        def weights_over_z(kind, q):
            for x in xpeers():
                wz_copy(kind, x, q, 1 - half).wait_recv()
                wf_copy(kind, chip(x), x, shared(q, 1 - half)).start()

        def weights_over_sib(kind):
            for x in xpeers():
                for p in range(NP):
                    wf_copy(kind, x * 2 + 1 - core, x, p).wait_recv()

        def weights_sent():
            for kind in (0, 1):
                sib_copy(kind, me).wait_send()
                for x in xpeers():
                    for q in range(NX):
                        wx_copy(kind, me, q, x, xi).wait_send()
                    for q in range(NS):
                        wz_copy(kind, x, q, half).wait_send()
                    for p in range(NP):
                        wf_copy(kind, chip(x), x, p).wait_send()

        zeros_h = jnp.zeros((HD, L), BF16)

        def set_bias(i, a):
            own = r.pairs[sec, i, :, pl.ds(row0, L)].astype(F32)
            if a == 0:
                keys = r.pairs[sec, i].astype(F32)
            else:
                keys = r.pairs[0, i].astype(F32)
            kc = jnp.broadcast_to(keys, (128, SEQ)).T
            if L > 128:
                kc = jnp.concatenate([kc] * (L // 128), 1)
            same = kc == own
            if a == 0:
                qpos = row0 + lax.broadcasted_iota(jnp.int32, (1, L), 1)
                limit = jnp.where(dec, qpos, SEQ)
                same = same & (lax.broadcasted_iota(jnp.int32, (SEQ, L), 0) <= limit)
            r.bias[...] = jnp.where(same, 0.0, -1e30)

        def route_rows(i, a):
            ref = r.routes_s if a == 0 else r.routes_c
            return [ref[i, k : k + 1, pl.ds(row0, L)] for k in range(T)]

        def pick(rows, route, size):
            total = jnp.zeros((size, L), F32)
            for e in range(NE):
                total = jnp.where(route == e, rows[e * size : (e + 1) * size], total)
            return total

        def project_queries(i, a):
            n = r.n[i, a]
            ql = nt(r.wqr[a], n)
            routes = route_rows(i, a)
            chosen = []
            for k in range(T):
                r.qt[a, i, k] = (pick(ql[:NQ], routes[k], HD).astype(BF16).astype(F32) * scale).astype(BF16)
                chosen.append(pick(ql[NQ : NQ + NE], routes[k], 1))
            top = chosen[0]
            for k in range(1, T):
                top = jnp.maximum(top, chosen[k])
            ex = [jnp.exp(c - top) for c in chosen]
            total = ex[0]
            for k in range(1, T):
                total = total + ex[k]
            for k in range(T):
                r.gate[a, i, k] = jnp.broadcast_to(ex[k] / total, (8, L))

        def attend(i, a, kv_ref, base):
            kv = kv_ref[i]
            r.kvt[a, i] = kv.astype(F32).T.astype(BF16)

            def one(k, _):
                q = jnp.concatenate([r.qt[a, i, k], zeros_h], 0)
                s = nn(kv, q) + r.bias[...]
                m = jnp.max(s, 0, keepdims=True)
                ex = jnp.exp(s - m)
                inv = 1.0 / jnp.sum(ex, 0, keepdims=True)
                p = ex.astype(BF16)
                r.p[a, i, k] = p
                r.inv[a, i, k] = jnp.broadcast_to(inv, (8, L))
                r.heads[a, i, k] = nn(r.kvt[a, i, HD:], p) * inv
                return 0

            lax.fori_loop(0, T, one, 0, unroll=True)
            routes = route_rows(i, a)
            gated = [
                r.heads[a, i, k].astype(BF16).astype(F32) * r.gate[a, i, k, 0:1] for k in range(T)
            ]
            for e in range(NE):
                block = jnp.zeros((HD, L), F32)
                for k in range(T):
                    block = jnp.where(routes[k] == e, gated[k], block)
                r.ht[a, i, e * HD : (e + 1) * HD] = block.astype(BF16)
            return base + tn(r.ht[a, i], r.wo_all[a])

        def attend_back(i, a, kv_ref, dx, send_ref):
            dxb = dx.astype(BF16)
            routes = route_rows(i, a)
            r.g_o[a] += nn(r.ht[a, i], dxb)
            gt = nt(r.wo_all[a], dxb)
            dgates = []
            for k in range(T):
                g = pick(gt, routes[k], HD)
                dgates.append(
                    jnp.sum(r.heads[a, i, k].astype(BF16).astype(F32) * g, 0, keepdims=True)
                )
                r.dq[k] = (g * r.gate[a, i, k, 0:1]).astype(BF16)
            gates = [r.gate[a, i, k, 0:1] for k in range(T)]
            mid = gates[0] * dgates[0]
            for k in range(1, T):
                mid = mid + gates[k] * dgates[k]
            dchosen = [gates[k] * (dgates[k] - mid) for k in range(T)]
            kv = kv_ref[i]
            r.dkv_acc[...] = jnp.zeros_like(r.dkv_acc)

            def one(k, _):
                dheads = (r.dq[k].astype(F32) * r.inv[a, i, k, 0:1]).astype(BF16)
                p = r.p[a, i, k]
                dv = jnp.concatenate([zeros_h, dheads], 0)
                delta = jnp.sum(dheads.astype(F32) * r.heads[a, i, k], 0, keepdims=True)
                ds = (p.astype(F32) * (nn(kv, dv) - delta)).astype(BF16)
                qk = jnp.concatenate([r.qt[a, i, k], zeros_h], 0)
                r.dkv_acc[...] += nt(ds, qk) + nt(p, dv)
                r.dq[k] = (nn(r.kvt[a, i, :HD], ds) * scale).astype(BF16)
                return 0

            lax.fori_loop(0, T, one, 0, unroll=True)
            send_ref[i] = r.dkv_acc[...].astype(BF16)
            blocks = []
            for e in range(NE):
                block = jnp.zeros((HD, L), F32)
                for k in range(T):
                    block = jnp.where(routes[k] == e, r.dq[k].astype(F32), block)
                blocks.append(block)
            logit_rows = jnp.zeros((RT, L), F32)
            rows = lax.broadcasted_iota(jnp.int32, (RT, L), 0)
            for k in range(T):
                logit_rows = jnp.where(rows == routes[k], dchosen[k], logit_rows)
            dql = jnp.concatenate(blocks + [logit_rows], 0).astype(BF16)
            r.g_qr[a] += nn(dql, r.n[i, a])
            return tn(dql, r.wqr[a])

        def chunk_at(s):
            return lax.rem(xi + s // 2, X) * 2 + jnp.where(lax.rem(s, 2) == 0, core, 1 - core)

        def chunk_out(s):
            return lax.rem(xi + s // 2 + 1, X) * 2 + jnp.where(lax.rem(s, 2) == 0, 1 - core, core)

        def ffn_forward(i, low, high):
            n = r.n[i, 2]

            def one(s, _):
                c = chunk_at(s)
                act, slope = gelu_parts(nn(n, r.win_all[c]))
                act = act.astype(BF16)
                r.act[i, c] = act
                r.dh[i, c] = slope.astype(BF16)
                r.acc[...] += nn(act, r.wback_all[c])
                return 0

            lax.fori_loop(low, high, one, 0, unroll=True)

        def ffn_middle(i):
            n = r.n[i, 2]
            r.acc[...] = jnp.zeros_like(r.acc)

            def one(c, _):
                act, slope = gelu_parts(nn(n, r.win_all[c]))
                r.act[i, c] = act.astype(BF16)
                dh = (r.dh[i, c].astype(F32) * slope).astype(BF16)
                r.dh[i, c] = dh
                r.acc[...] += nt(dh, r.win_all[c])
                return 0

            lax.fori_loop(0, E, one, 0, unroll=True)
            return r.acc[...]

        def big_sib(kind):
            for o, x in enumerate(xpeers()):
                a_copy(kind, x).wait_recv()
                r.b_big[o, kind] = (
                    r.g_big[chip(x), kind] + r.a_big_r[kind, x].astype(F32)
                ).astype(BF16)

        def big_sib_own(kind):
            a_copy(kind, xi).wait_recv()
            r.g_big[me, kind] += r.a_big_r[kind, xi].astype(F32)

        def dp_at(s):
            return mates_at(s) if s < HP else mine_at((s - HP + 1) % HP)

        def big_send(kind, low, high):
            for s in range(low, high):
                for h in range(NH):
                    for o in range(X - 1):
                        b_copy(kind, o, dp_at(s), h).start()

        def big_over_x(kind, s):
            for h in range(NH):
                big_part_over_x(kind, s, h)

        def big_part_over_x(kind, s, h):
            d = dp_at(s)
            total = r.g_big[me, kind, part_rows(d, h)]
            for o in range(X - 1):
                b_copy(kind, o, d, h).wait_recv()
                total = total + r.b_big_r[o, kind, part_rows(d, h)].astype(F32)
            if s < HP:
                r.za_big[kind, s, sub_rows(h)] = total.astype(BF16)
                zab_copy(kind, s, h).start()
                return
            k = (s - HP + 1) % HP
            zab_copy(kind, k, h).wait_recv()
            total = total + r.za_big_r[kind, k, sub_rows(h)].astype(F32)
            if k > 0:
                r.zb_big[kind, k - 1, sub_rows(h)] = total.astype(BF16)
                zbb_copy(kind, k, h).start()
            else:
                r.g_big[me, kind, part_rows(d, h)] = total

        def big_end(kind, out):
            for h in range(NH):
                total = r.g_big[me, kind, part_rows(dpi, h)]
                for k in range(1, HP):
                    zbb_copy(kind, k, h).wait_recv()
                    total = total + r.zb_big_r[kind, k - 1, sub_rows(h)].astype(F32)
                out[sub_rows(h)] = total

        def hand_out(i, s, c, kind):
            @pl.when(jnp.logical_and(i == NI - 1, lax.rem(s, 2) == 0))
            def _():
                x = c // 2
                r.a_big[kind, x] = r.g_big[c, kind].astype(BF16)
                a_copy(kind, x).start()

        def ffn_back(i):
            dz = r.dz[i]
            dzt = dz.astype(F32).T.astype(BF16)

            def back(s, _):
                c = chunk_out(s)
                r.g_big[c, 1] += nn(dzt, r.act[i, c])
                hand_out(i, s, c, 1)
                return 0

            lax.fori_loop(0, E, back, 0, unroll=True)

            @pl.when(i == NI - 1)
            def _():
                big_sib(1)
                big_send(1, 0, HP)

            nt_ = r.n[i, 2].astype(F32).T.astype(BF16)
            r.acc[...] = jnp.zeros_like(r.acc)

            def inward(s, _):
                c = chunk_out(s)
                dh = (nt(dz, r.wback_all[c]) * r.dh[i, c].astype(F32)).astype(BF16)
                r.acc[...] += nt(dh, r.win_all[c])
                r.g_big[c, 0] += nn(nt_, dh)
                hand_out(i, s, c, 0)
                return 0

            lax.fori_loop(0, E, inward, 0, unroll=True)
            return r.acc[...]

        def ffn_weights(kind):
            for i in range(NI):
                r.turned[i] = (r.cot[i] if kind == 1 else r.n[i, 2]).astype(F32).T.astype(BF16)

            def one(s, _):
                c = chunk_out(s)
                total = jnp.zeros((D, HB), F32)
                for i in range(NI):
                    total += nn(r.turned[i], (r.act if kind == 1 else r.dh)[i, c])
                r.g_big[c, kind] = total
                hand_out(NI - 1, s, c, kind)
                return 0

            lax.fori_loop(0, E, one, 0)

        def ffn_output(i):
            r.acc[...] = r.x2[i]

            def one(c, _):
                r.acc[...] += nn(r.act[i, c], r.wback_all[c])
                return 0

            lax.fori_loop(0, E, one, 0, unroll=True)
            r.o_layer[i] = r.acc[...].astype(BF16)

        def add_small(which, dgain, dshift):
            r.small[2 * which : 2 * which + 1] += dgain
            r.small[2 * which + 1 : 2 * which + 2] += dshift

        def qo_rows(a, c):
            at = pl.ds(pl.multiple_of(c * QB, QB), QB)
            return jnp.concatenate([r.g_qr[a, at], r.g_o[a, at]], 0)

        def qo_send(a):
            for x in range(X):
                r.a_qo[a, x] = qo_rows(a, x * 2 + (1 - core)).astype(BF16)
            aq_copy(a).start()

        def rows_around(o):
            return block_rows(lax.rem(dpi + o + 1, DP))

        def qo_sib(a):
            aq_copy(a).wait_recv()
            for o, x in enumerate(xpeers()):
                r.b_qo[a, o] = (qo_rows(a, chip(x)) + r.a_qo_r[a, x].astype(F32)).astype(BF16)
                bq_copy(a, o).start()

        def qo_over_x(a):
            total = qo_rows(a, me) + r.a_qo_r[a, xi].astype(F32)
            for o in range(X - 1):
                bq_copy(a, o).wait_recv()
                total = total + r.b_qo_r[a, o].astype(F32)
            r.own_qo[...] = total.T
            for o in range(DP - 1):
                r.c_qo[a, o] = r.own_qo[rows_around(o)].astype(BF16)
                cq_copy(a, o).start()
            r.qo_own[a] = r.own_qo[block_rows(dpi)]

        def qo_end(a):
            total = r.qo_own[a]
            for o in range(DP - 1):
                cq_copy(a, o).wait_recv()
                total = total + r.c_qo_r[a, o].astype(F32)
            return total

        kv_busy = enc | (core == 0)
        kv_sib_busy = enc | (core == 1)

        def kv_send():
            @pl.when(kv_sib_busy)
            def _():
                ka_copy().start()

        def kv_sib():
            @pl.when(kv_busy)
            def _():
                ka_copy().wait_recv()
                r.kv_sum[...] = r.g_kv[core] + r.kv_ar[...]
                for o in range(DP - 1):
                    r.c_kv[o] = r.kv_sum[rows_around(o)].astype(BF16)
                    ck_copy(o).start()

        def kv_over_dp():
            @pl.when(kv_busy)
            def _():
                total = r.kv_sum[block_rows(dpi)]
                for o in range(DP - 1):
                    ck_copy(o).wait_recv()
                    total = total + r.c_kv_r[o].astype(F32)
                r.kv_fin[...] = total
                r.kv_b[...] = total.astype(BF16)
                for o in range(X - 1):
                    kb_copy(o).start()

        def kv_over_x():
            @pl.when(kv_busy)
            def _():
                total = r.kv_fin[...]
                for o in range(X - 1):
                    kb_copy(o).wait_recv()
                    total = total + r.kv_br[o].astype(F32)
                r.kv_fin[...] = total
                kf_copy().start()

            @pl.when(enc & (core == 1))
            def _():
                ks_copy(0).start()
                ks_copy(1).start()

        def kv_end():
            @pl.when(kv_sib_busy)
            def _():
                kf_copy().wait_recv()

            @pl.when(dec)
            def _():
                ks_copy(core).wait_recv()
                r.o_kv[0] = jnp.where(core == 0, r.kv_fin[...], r.kv_sib[...])
                r.o_kv[1] = r.kv_sec[...]

            @pl.when(enc)
            def _():
                r.o_kv[0] = jnp.where(core == 0, r.kv_fin[...], r.kv_sib[...])
                r.o_kv[1] = jnp.where(core == 0, r.kv_sib[...], r.kv_fin[...])

        def small_sib():
            sa_copy().wait_recv()
            r.sm_fin[...] = r.small[...] + r.sm_ar[...]
            r.sm_b[...] = r.sm_fin[...].astype(BF16)
            for o in range(X - 1):
                sb_copy(o).start()

        def small_over_x():
            total = r.sm_fin[...]
            for o in range(X - 1):
                sb_copy(o).wait_recv()
                total = total + r.sm_br[o].astype(F32)
            r.sm_fin[...] = total
            r.za_sm[...] = total.astype(BF16)
            for o in range(DP - 1):
                zs_copy(o).start()

        def small_over_dp():
            total = r.sm_fin[:, lanes(dpi)]
            for o in range(DP - 1):
                zs_copy(o).wait_recv()
                total = total + r.za_sm_r[o].astype(F32)
            r.sm_own[...] = total

        def self_forward(i):
            x1 = attend(i, 0, r.kv_s, r.x[i].astype(F32))
            r.x1[i] = x1

            @pl.when(enc)
            def _():
                g, b = gain_of(2)
                r.n[i, 2] = norm_rows(r.x1[i], g, b).astype(BF16)

            @pl.when(dec)
            def _():
                g, b = gain_of(1)
                r.n[i, 1] = norm_rows(r.x1[i], g, b).astype(BF16)

        def encoded(i):
            mem = r.acc[...].astype(BF16)
            r.o_layer[i] = mem
            r.ckv_own[i] = nn(mem, r.ckv[...]).astype(BF16)
            for x in xpeers():
                ckv_copy(i, chip(x)).start()
            ckv_copy(i, me).start()

        gather_relay(q_of(0, 0))
        gather_take(q_of(0, 0))
        project_queries(0, 0)
        set_bias(0, 0)
        gather_relay(kv_of(0))
        gather_relay(q_of(0, 1))
        gather_take(kv_of(0))
        gather_take(q_of(0, 1))
        self_forward(0)
        def later_rows(i, _):
            project_queries(i, 0)
            set_bias(i, 0)
            gather_relay(kv_of(i))
            gather_take(kv_of(i))
            self_forward(i)
            return 0

        @pl.when(dec)
        def _():
            lax.fori_loop(1, NI, later_rows, 0)

        for q in range(NS):
            weights_over_x(0, q)
        for kind in (0, 1):
            sib_copy(kind, sib).wait_recv()

        @pl.when(enc)
        def _():
            r.acc[...] = r.x1[0]
            ffn_forward(0, 0, 2)

        for q in range(NS):
            weights_over_x(1, q)
            weights_over_z(0, q)
        @pl.when(dec)
        def _():
            for i in range(NI):
                for s in range(2):
                    c = chunk_at(jnp.int32(s))
                    r.dh[i, c] = nt(r.cot[i], r.wback_all[c]).astype(BF16)

        for q in range(NS, NX):
            weights_over_x(0, q)
        for q in range(NS):
            weights_over_z(1, q)
        for q in range(NS, NX):
            weights_over_x(1, q)
        @pl.when(enc)
        def _():
            ffn_forward(0, 2, 3)

        for kind in (0, 1):
            weights_over_sib(kind)

        @pl.when(enc)
        def _():
            ffn_forward(0, 3, E)
            encoded(0)

        @pl.when(enc)
        def _():
            def later_outputs(i, _):
                later_rows(i, 0)
                r.acc[...] = r.x1[i]
                ffn_forward(i, 0, E)
                encoded(i)
                return 0

            lax.fori_loop(1, NI, later_outputs, 0)
            store("layer").start()

        r.small[...] = jnp.zeros_like(r.small)
        r.g_qr[...] = jnp.zeros_like(r.g_qr)
        r.g_o[...] = jnp.zeros_like(r.g_o)
        r.g_kv[...] = jnp.zeros_like(r.g_kv)

        def zero_big(c, _):
            r.g_big[c] = jnp.zeros((2, D, HB), F32)
            return 0

        lax.fori_loop(0, E, zero_big, 0)

        @pl.when(dec)
        def _():
            for kind in (0, 1):
                gather_relay(q_of(1, kind))
            for kind in (0, 1):
                gather_take(q_of(1, kind))

            def ahead(i, _):
                project_queries(i, 1)
                dz = r.cot[i]

                def one(s, _):
                    c = chunk_at(s)
                    r.dh[i, c] = nt(dz, r.wback_all[c]).astype(BF16)
                    return 0

                lax.fori_loop(2, E, one, 0)
                return 0

            lax.fori_loop(0, NI, ahead, 0)

            def middle(i, _):
                set_bias(i, 1)
                ckv_gather(i)
                x2 = attend(i, 1, r.kv_c, r.x1[i])
                r.x2[i] = x2
                g, b = gain_of(2)
                r.n[i, 2] = norm_rows(x2, g, b).astype(BF16)
                dn = ffn_middle(i)
                dx, dg, db = norm_back(r.x2[i], g, dn)
                add_small(2, dg, db)
                r.o_ig[i] = r.cot[i].astype(F32) + dx
                dn = attend_back(i, 1, r.kv_c, r.o_ig[i], r.dckv_send)
                dckv_out(i)
                g, b = gain_of(1)
                dx, dg, db = norm_back(r.x1[i], g, dn)
                add_small(1, dg, db)
                r.o_ig[i] += dx
                return 0

            lax.fori_loop(0, NI, middle, 0)

            qo_send(1)

        def backward(i, _):
            @pl.when(enc)
            def _():
                total = jnp.zeros((L, 2 * HD), F32)
                for x in range(X):
                    dckv_copy(i, x, x).wait_recv()
                    total = total + r.dckv_recv[i, x].astype(F32)
                dkv = total.astype(BF16)
                dmem = nt(dkv, r.ckv[...]).astype(BF16).astype(F32)
                dx = r.cot[i].astype(F32) + dmem
                r.o_ig[i] = dx
                r.dz[i] = dx.astype(BF16)
                dn = ffn_back(i)
                r.g_kv[1] += tn(r.o_layer[i], dkv)
                g, b = gain_of(2)
                dx, dg, db = norm_back(r.x1[i], g, dn)
                add_small(2, dg, db)
                r.o_ig[i] += dx

            first = i == 0
            last = i == NI - 1

            @pl.when(dec & first)
            def _():
                ffn_weights(1)

            r.dn[i] = attend_back(i, 0, r.kv_s, r.o_ig[i], r.dkv_send)

            @pl.when(dec & first)
            def _():
                big_sib(1)
                qo_sib(1)
                big_send(1, 0, HP)

            dkv_out(i)

            @pl.when(dec & first)
            def _():
                ffn_weights(0)

            @pl.when(last)
            def _():
                big_send(1, HP, DP - 1)
                big_sib(0)
                big_send(0, 0, HP)
                qo_send(0)

            return 0

        lax.fori_loop(0, NI, backward, 0)
        for kind in (1, 0):
            big_sib_own(kind)
        for s in range(HP):
            big_over_x(1, s)

        @pl.when(dec)
        def _():
            qo_over_x(1)

        def first_layer(i, _):
            dkv = dkv_in(i).astype(BF16)
            r.g_kv[0] += tn(r.n[i, 0], dkv)
            dn = r.dn[i] + nt(dkv, r.wkv[...])
            g, b = gain_of(0)
            dx, dg, db = norm_back(r.x[i].astype(F32), g, dn)
            add_small(0, dg, db)
            r.o_ig[i] += dx
            return 0

        lax.fori_loop(0, NI, first_layer, 0)
        store("ig").start()

        for a in range(2):
            r.small[6 + a * NE : 6 + (a + 1) * NE] = r.g_qr[a, NQ : NQ + NE]
        sa_copy().start()
        kv_send()

        qo_sib(0)
        small_sib()
        kv_sib()

        big_send(0, HP, DP - 1)
        for s in range(HP, DP - 1):
            big_over_x(1, s)
        for s in range(HP):
            big_over_x(0, s)

        @pl.when(dec)
        def _():
            def output(i, _):
                ffn_output(i)
                return 0

            lax.fori_loop(0, NI, output, 0)
            store("layer").start()

        small_over_x()

        qo_over_x(0)
        kv_over_dp()
        for kind in (1, 0):
            big_send(kind, DP - 1, DP)
        for s in range(HP, DP - 1):
            big_over_x(0, s)
        small_over_dp()

        @pl.when(dec)
        def _():
            sec_copy(1).start()
            r.qo_fin[...] = qo_end(1)
            sec_copy(0).start()
            r.o_qo[1] = r.qo_fin[...]
            r.o_small[...] = r.sm_own[...]

        for kind in (1, 0):
            big_over_x(kind, DP - 1)
        kv_over_x()
        r.o_qo[0] = qo_end(0)
        big_end(1, r.o_back)
        big_end(0, r.o_in)
        kv_end()

        @pl.when(enc)
        def _():
            sec_copy(1).wait_recv()
            sec_copy(0).wait_recv()
            r.o_qo[1] = r.qo_sec[...]
            rows = lax.broadcasted_iota(jnp.int32, (SR, 128), 0)
            theirs = ((rows >= 2) & (rows < 4)) | ((rows >= 6 + NE) & (rows < 6 + 2 * NE))
            r.o_small[...] = jnp.where(theirs, r.sm_sec[...], r.sm_own[...])

        store("layer").wait()
        store("ig").wait()
        for kind in (0, 1):
            gather_sent(q_of(0, kind))
            for x in range(X):
                a_copy(kind, x).wait_send()
            for h in range(NH):
                for o in range(X - 1):
                    for d in range(DP):
                        b_copy(kind, o, d, h).wait_send()
                for k in range(HP):
                    zab_copy(kind, k, h).wait_send()
                for k in range(1, HP):
                    zbb_copy(kind, k, h).wait_send()
        weights_sent()
        sa_copy().wait_send()
        for o in range(X - 1):
            sb_copy(o).wait_send()
        for o in range(DP - 1):
            zs_copy(o).wait_send()

        def qo_sent(a):
            aq_copy(a).wait_send()
            for o in range(X - 1):
                bq_copy(a, o).wait_send()
            for o in range(DP - 1):
                cq_copy(a, o).wait_send()

        qo_sent(0)

        @pl.when(dec)
        def _():
            for kind in (0, 1):
                gather_sent(q_of(1, kind))
                sec_copy(kind).wait_send()
            qo_sent(1)

        @pl.when(kv_sib_busy)
        def _():
            ka_copy().wait_send()

        @pl.when(kv_busy)
        def _():
            for o in range(X - 1):
                kb_copy(o).wait_send()
            for o in range(DP - 1):
                ck_copy(o).wait_send()
            kf_copy().wait_send()

        @pl.when(enc & (core == 1))
        def _():
            ks_copy(0).wait_send()
            ks_copy(1).wait_send()

        def sent(i, _):
            gather_sent(kv_of(i))
            for x in xpeers():
                dkv_copy(i, x, xi).wait_send()
            for x in range(X):
                dksum_copy(i, x).wait_send()

            @pl.when(enc)
            def _():
                for x in range(X):
                    ckv_copy(i, chip(x)).wait_send()

            @pl.when(dec)
            def _():
                for x in range(X):
                    ckv_relay(i, chip(x)).wait_send()
                    dsum_copy(i, x).wait_send()
                    dckv_copy(i, x, xi).wait_send()

            return 0

        lax.fori_loop(0, NI, sent, 0)

    return kernel


def make_finish(E, NE, EB, QB):
    def kernel(
        layer, grads, w_in, w_back, qo, kv, small, o_layer, o_grads, o_gain, o_bias, o_kv, o_router,
        o_query, o_out, o_w_in, o_w_back, o_cgain, o_cbias, o_ckv, o_crouter, o_cquery, o_cout,
    ):
        me = lax.axis_index("expert")
        o_layer[...] = layer[...]
        o_grads[...] = grads[...]
        o_w_in[...] = w_in[...]
        o_w_back[...] = w_back[...].T
        for a, (q, o) in enumerate(((o_query, o_out), (o_cquery, o_cout))):
            both = qo[a].T
            q[...] = both[:QB]
            o[...] = both[QB:]
        for a, out in enumerate((o_kv, o_ckv)):
            total = kv[a, :EB]
            for j in range(1, E):
                total = jnp.where(me == j, kv[a, j * EB : (j + 1) * EB], total)
            out[...] = total
        off = (lax.axis_index("dp") * E + me) * EB
        part = pltpu.roll(small[...], lax.rem(128 - lax.rem(off, 128), 128), 1)[:, :EB]
        o_gain[0] = jnp.concatenate([part[0:1], part[4:5]], 0)
        o_bias[0] = jnp.concatenate([part[1:2], part[5:6]], 0)
        o_cgain[...] = part[2:3]
        o_cbias[...] = part[3:4]
        o_router[...] = part[6 : 6 + NE]
        o_crouter[...] = part[6 + NE : 6 + 2 * NE]

    return kernel


def body(
    inputs, cotangents, pair_ids, self_routes, cross_routes, norm_gain, norm_bias, w_kv, w_router,
    w_query, w_out, w_in, w_back, cross_gain, cross_bias, cross_kv, cross_router, cross_query,
    cross_out,
):
    E = lax.axis_size("expert")
    DP = lax.axis_size("dp")
    _, MB, R, L, D = inputs.shape
    NI = MB * R
    SEQ = pair_ids.shape[-1]
    T = self_routes.shape[-1]
    NE = w_router.shape[-1]
    HD = w_query.shape[-1]
    HB = w_in.shape[-1]
    npd = NE // E
    QB = npd * HD
    dims = (NI, L, D, SEQ, T, NE, HD, HB, E, DP)
    ins, outs, bufs, sems = make_plan(dims)

    operands = [
        inputs.reshape(NI, L, D),
        cotangents.reshape(NI, L, D),
        pair_ids.reshape(2, NI, 1, SEQ),
        jnp.swapaxes(self_routes.reshape(NI, SEQ, T), 1, 2),
        jnp.swapaxes(cross_routes.reshape(NI, SEQ, T), 1, 2),
        norm_gain[0],
        norm_bias[0],
        w_kv[0],
        w_router[0].T,
        jnp.swapaxes(w_query[0], 1, 2),
        w_out[0],
        w_in[0],
        w_back[0],
        cross_gain[None],
        cross_bias[None],
        cross_kv,
        cross_router.T,
        jnp.swapaxes(cross_query, 1, 2),
        cross_out,
    ]
    vmem = pl.BlockSpec(memory_space=pltpu.VMEM)
    anywhere = pl.BlockSpec(memory_space=pl.ANY)
    res = pl.pallas_call(
        make_kernel(dims),
        out_shape=[jax.ShapeDtypeStruct(s, t) for s, t in outs.values()],
        in_specs=[vmem if n in STAY else anywhere for n in ins],
        out_specs=[anywhere if n[:4] == "out_" else vmem for n in outs],
        scratch_shapes=[pltpu.VMEM(s, t) for s, t in bufs.values()]
        + [pltpu.SemaphoreType.DMA(s) for s in sems.values()]
        + [pltpu.VMEM(o.shape, o.dtype) for n, o in zip(ins, operands) if n in fetched(ins)],
        compiler_params=pltpu.CompilerParams(
            collective_id=0, has_side_effects=True, vmem_limit_bytes=62 * 1024 * 1024
        ),
        name="layers",
    )(*operands)
    DB = D // DP
    EB = DB // E
    shapes = [
        ((NI, L, D), BF16),
        ((NI, L, D), F32),
        ((1, 2, EB), F32),
        ((1, 2, EB), F32),
        ((EB, 2 * HD), F32),
        ((NE, EB), F32),
        ((QB, DB), F32),
        ((QB, DB), F32),
        ((DB, HB), F32),
        ((HB, DB), F32),
        ((1, EB), F32),
        ((1, EB), F32),
        ((EB, 2 * HD), F32),
        ((NE, EB), F32),
        ((QB, DB), F32),
        ((QB, DB), F32),
    ]
    (
        layer, grads, gain, bias, kv, router, query, out, w_in_g, w_back_g, c_gain, c_bias, c_kv,
        c_router, c_query, c_out,
    ) = pl.pallas_call(
        make_finish(E, NE, EB, QB),
        out_shape=[jax.ShapeDtypeStruct(s, t) for s, t in shapes],
        in_specs=[vmem] * len(outs),
        out_specs=[vmem] * len(shapes),
        name="results",
    )(*res)

    def of_query(g):
        return jnp.swapaxes(g.reshape(npd, HD, DB), 1, 2)

    def of_out(g):
        return g.reshape(npd, HD, DB)

    return (
        layer.reshape(inputs.shape),
        grads.reshape(inputs.shape),
        gain,
        bias,
        kv[None],
        router.T[None],
        of_query(query)[None],
        of_out(out)[None],
        w_in_g[None],
        w_back_g[None],
        c_gain[0],
        c_bias[0],
        c_kv,
        c_router.T,
        of_query(c_query),
        of_out(c_out),
    )


def solution(mesh):
    placed = (
        P("section", None, "dp", "expert", None),
        P("section", None, "dp", "expert", None),
        P(None, None, "dp", None),
        P("section", None, "dp", None, None),
        P(None, "dp", None, None),
        P("section", None, None),
        P("section", None, None),
        P("section", None, None),
        P("section", None, None),
        P("section", "expert", None, None),
        P("section", "expert", None, None),
        P("section", None, "expert"),
        P("section", "expert", None),
        P(),
        P(),
        P(),
        P(),
        P("expert", None, None),
        P("expert", None, None),
    )
    return jax.shard_map(
        body,
        mesh=mesh,
        in_specs=placed,
        out_specs=(
            P("section", None, "dp", "expert", None),
            P("section", None, "dp", "expert", None),
            P("section", None, ("dp", "expert")),
            P("section", None, ("dp", "expert")),
            P("section", ("dp", "expert"), None),
            P("section", ("dp", "expert"), None),
            P("section", "expert", "dp", None),
            P("section", "expert", None, "dp"),
            P("section", "dp", "expert"),
            P("section", "expert", "dp"),
            P(("dp", "expert")),
            P(("dp", "expert")),
            P(("dp", "expert"), None),
            P(("dp", "expert"), None),
            P("expert", "dp", None),
            P("expert", None, "dp"),
        ),
        check_vma=False,
    )
```
